256 devices in a mesh: seg: 8 (over y, core), tm: 32 (over x, z).
Axes of the slice: x: 4, y: 4, z: 8, core: 2. Of those that a mesh axis runs over, the one named last changes fastest.
Arguments:
- transition: bfloat16 [512, 512, 512], P(('seg', 'tm')), may hold values from -1 to 1
- obs_gain: bfloat16 [512, 512, 512], P(('seg', 'tm')), may hold values from -0.0625 to 0.0625
- observed: bfloat16 [512, 4, 512], P(('seg', 'tm')), may hold values from -6 to 6
- init_mean: float32 [4, 512], replicated, may hold values from -6 to 6
- init_factor: float32 [512, 512], P('tm'), may hold values from -6 to 6
Outputs:
- means: float32 [512, 4, 512], P(('seg', 'tm'))
- factor_ends: float32 [8, 512, 512], P('seg', 'tm')
The draws below stay inside these ranges and needn't reach their ends.
All inputs are finite; a program needn't handle non-finite values.
Results may differ from the reference program's by a relative error of at most 0.0003.
Values sent between devices are 32-bit elements; how exact they have to be, the bound alone decides.
A program may use at most 128 MiB of HBM per device.

```python
import jax
import jax.numpy as jnp
from jax import lax

D = 512
OBS = 512
SER = 4
STEPS_DEV = 2
TOTAL_TIME_STEPS = 512
N_SEG = 8
N_TM = 32


def draw_transition(key, part):
    random_keys = jax.random.split(key, 7)
    vectors = jax.random.normal(random_keys[0], (TOTAL_TIME_STEPS, D), jnp.float32)
    lengths = jnp.sum(vectors * vectors, axis=1)
    reflect = jnp.eye(D, dtype=jnp.float32)[None] - 2.0 * vectors[:, :, None] * vectors[:, None, :] / lengths[:, None, None]
    share = 0.5
    picker = jax.random.uniform(random_keys[1], (D,), jnp.float32)
    slow_rate = -jax.random.uniform(random_keys[2], (D,), jnp.float32, 0.2, 1.9) / TOTAL_TIME_STEPS
    fast_rate = -1.0 / jax.random.uniform(random_keys[3], (D,), jnp.float32, 30.0, 50.0)
    baseline_level = jnp.where(picker < share, slow_rate, fast_rate)
    random_perturbation = jax.random.uniform(random_keys[4], (TOTAL_TIME_STEPS, D), jnp.float32, 0.5, 1.5)
    spike_selector = jax.random.uniform(random_keys[5], (TOTAL_TIME_STEPS,), jnp.float32)
    spike_magnitude = jax.random.uniform(random_keys[6], (TOTAL_TIME_STEPS,), jnp.float32, 0.5, 0.8)
    spike_amount = jnp.where(spike_selector < 6.0 / TOTAL_TIME_STEPS, spike_magnitude, 1.0)
    noise_scale = jnp.exp(baseline_level[None, :] * random_perturbation) * spike_amount[:, None]
    return (reflect * noise_scale[:, None, :]).astype(jnp.bfloat16)


def level_of(stream_key, shape, shards, low, high):
    loudness, own = 1.0, jax.random.fold_in(stream_key, 6)
    for dim, blocks in shards:
        heights = jnp.exp(jax.random.uniform(jax.random.fold_in(own, dim), (blocks,), jnp.float32, low / len(shards), high / len(shards)))
        loudness = loudness * jnp.repeat(heights, shape[dim] // blocks).reshape([-1 if axis == dim else 1 for axis in range(len(shape))])
    return loudness


def gaussian(key, dims, spread, bound, pieces=(), held_as=jnp.bfloat16):
    level = level_of(key, dims, pieces, -0.22, 0.18) if pieces else 1.0
    values = jax.random.normal(key, dims, jnp.float32) * spread * level
    return jnp.minimum(jnp.maximum(values, -bound), bound).astype(held_as)


def setup_inputs(seed: int = 0) -> dict:
    key_of = jax.random.split(jax.random.key(seed), 6)
    return {
        "transition": draw_transition(jax.random.fold_in(key_of[5], 71), 0),
        "obs_gain": gaussian(key_of[1], (TOTAL_TIME_STEPS, OBS, D), (OBS * 16) ** -0.5, 0.0625, ((0, 256),)),
        "observed": gaussian(key_of[2], (TOTAL_TIME_STEPS, SER, OBS), 1.0, 6.0, ((0, 256),)),
        "init_mean": gaussian(key_of[3], (SER, D), 1.0, 6.0, (), jnp.float32),
        "init_factor": gaussian(key_of[4], (D, D), 1.0, 6.0, ((0, 32),), jnp.float32),
    }


def exact_dot(left, right):
    return jnp.dot(left, right, precision=lax.Precision.HIGHEST, preferred_element_type=jnp.float32)


def reference(transition, obs_gain, observed, init_mean, init_factor):
    per_block = STEPS_DEV * N_TM
    trans_blocks = transition.reshape(N_SEG, per_block, D, D)
    gain_blocks = obs_gain.reshape(N_SEG, per_block, OBS, D)
    seen_blocks = observed.reshape(N_SEG, per_block, SER, OBS)

    def inner(carry, inputs):
        mean_now, factor_now = carry
        matrix, gain, seen = inputs
        matrix = matrix.astype(jnp.float32)
        mean_now = exact_dot(mean_now, matrix) + jnp.dot(seen, gain, preferred_element_type=jnp.float32)
        factor_now = exact_dot(factor_now, matrix)
        return (mean_now, factor_now), mean_now

    def outer(carry, inputs):
        carry, block_means = lax.scan(inner, carry, inputs)
        return carry, (block_means, carry[1])

    start = (init_mean.astype(jnp.float32), init_factor.astype(jnp.float32))
    _, (all_means, ends) = lax.scan(outer, start, (trans_blocks, gain_blocks, seen_blocks))
    return all_means.reshape(TOTAL_TIME_STEPS, SER, D), ends
```

```python
import functools

import jax
import jax.numpy as jnp
from jax import lax
from jax.experimental import pallas as pl
from jax.experimental.pallas import tpu as pltpu
from jax.sharding import PartitionSpec as P

MESH = pl.DeviceIdType.MESH
F32, BF16 = jnp.float32, jnp.bfloat16
D = 512
HALF = D // 2
ROWS = 32
NC = D // ROWS
NX = HALF // ROWS
LAG = 4
PAD = 8

NN = (((1,), (0,)), ((), ()))
NT = (((1,), (1,)), ((), ()))
TN = (((0,), (0,)), ((), ()))
TT = (((0,), (1,)), ((), ()))


def dot(a, b, dims=NN):
    return lax.dot_general(a, b, dims, preferred_element_type=F32)


def split(a):
    hi = a.astype(BF16)
    return hi, (a - hi.astype(F32)).astype(BF16)


def mm3(a, hi, lo, dims=NN):
    ah, al = split(a)
    n = a.shape[0]
    both = dot(jnp.concatenate([ah, al], axis=0), hi, dims)
    return both[:n] + both[n:] + dot(ah, lo, dims)


def mm2(a, exact):
    ah, al = split(a)
    n = a.shape[0]
    both = dot(jnp.concatenate([ah, al], axis=0), exact)
    return both[:n] + both[n:]


def kernel(
    t_ref, g_ref, o_ref, m0_ref, f0_ref, means_ref, ends_ref,
    zout, zin, whi, wlo, drv, cin, ch, csend,
    sphi, splo, px, wxhi, wxlo, xin, ab, abhi, ablo, pfhi, pflo,
    cs, cx, cseg, cown, m_in, m_out, f_in, f_out, f_box, inhi, inlo, e_in, e_out, e_half, e_x, e_next,
    zs, zr, cs_s, cs_r, ch_s, ch_r, xs, xr, abx_s, abx_r, abz_s, abz_r,
    cx_s, cx_r, m_s, m_r, f0_s, f0_r, f_s, f_r, fb_s, fb_r, e_s, e_r, ex_s, ex_r,
):
    seg = lax.axis_index("seg")
    tm = lax.axis_index("tm")
    c = seg % 2
    x, z = tm // 8, tm % 8
    zh, zi = z // 4, z % 4
    row = zh == c
    pos = jnp.where(row, zi, 3 - zi)
    nz = jnp.where(row, (z + 1) % 8, (z + 7) % 8)
    end = pos == 3
    inner = (x == 1) | (x == 2)
    root = end & inner
    outer = end & jnp.logical_not(inner)
    first, last = seg == 0, seg == 7
    xroot = jnp.where(x < 2, 1, 2)
    xouter = jnp.where(x < 2, 0, 3)

    def end_z(core, half):
        return jnp.where(core == 0, 3 + half, 7 * half)

    def did(s, xx, zz):
        return (s, xx * 8 + zz)

    myend = end_z(c, zh)

    def rcopy(src, dst, ssem, rsem, dev):
        return pltpu.make_async_remote_copy(
            src_ref=src, dst_ref=dst, send_sem=ssem, recv_sem=rsem, device_id=dev, device_id_type=MESH
        )

    def got(dst, rsem):
        rcopy(dst, dst, rsem, rsem, did(seg, x, nz)).wait_recv()

    barrier = pltpu.get_barrier_semaphore()

    def greet(dev):
        pl.semaphore_signal(barrier, inc=1, device_id=dev, device_id_type=MESH)

    for k in range(1, 8):
        greet(did(seg, x, (z + k) % 8))
    for k in range(1, 4):
        greet(did(seg, (x + k) % 4, z))

    @pl.when(jnp.logical_not(inner))
    def _():
        greet(did(seg, xroot, myend))

    @pl.when(root)
    def _():
        for k in range(4):
            greet(did(seg, xouter, zh * 4 + k))

        @pl.when(jnp.logical_not(last))
        def _():
            greet(did(seg + 1, x, end_z(1 - c, zh)))

        @pl.when(jnp.logical_not(first))
        def _():
            greet(did(seg - 1, x, end_z(1 - c, zh)))

    @pl.when(root & (x == 1) & jnp.logical_not(last))
    def _():
        greet(did(seg + 1, 0, end_z(1 - c, zh)))

    @pl.when(end & (x == 0) & jnp.logical_not(first))
    def _():
        greet(did(seg - 1, 1, end_z(1 - c, zh)))

    one = lambda p: jnp.where(p, 1, 0)
    greets = (
        10 + one(jnp.logical_not(inner))
        + one(root) * (4 + one(jnp.logical_not(last)) + one(jnp.logical_not(first)))
        + one(root & (x == 1) & jnp.logical_not(last)) + one(end & (x == 0) & jnp.logical_not(first))
    )

    def put_map(m):
        @pl.when(pos == 0)
        def _():
            zout[...] = m

        @pl.when(pos > 0)
        def _():
            hi, lo = split(m)
            whi[...] = hi
            wlo[...] = lo

    @pl.when(row)
    def _():
        put_map(dot(t_ref[0], t_ref[1]))

    @pl.when(jnp.logical_not(row))
    def _():
        put_map(dot(t_ref[1], t_ref[0], TT))

    pad = jnp.zeros((PAD - 4, D), F32)
    for s in range(2):
        drv[s] = jnp.concatenate([dot(o_ref[s], g_ref[s]), pad], axis=0)

    @pl.when(zi == 0)
    def _():
        cin[...] = jnp.zeros_like(cin)

    pl.semaphore_wait(barrier, greets)

    block = jnp.where(x == xroot, 0, 4) + zi

    def f0_copy():
        return rcopy(f0_ref, f_in.at[block], f0_s, f0_r.at[block], did(seg, xroot, myend))

    @pl.when(first & jnp.logical_not(root))
    def _():
        f0_copy().start()

    @pl.when(first & root)
    def _():
        f_in[block] = f0_ref[...]

    def two_steps(m):
        m1 = mm2(m, t_ref[0]) + drv[0]
        return m1, mm2(m1, t_ref[1]) + drv[1]

    def c_next():
        return rcopy(csend, cin, cs_s, cs_r, did(seg, x, (z + 1) % 8))

    def c_end(half):
        return rcopy(csend, ch.at[zh], ch_s.at[half], ch_r.at[zh], did(seg, x, end_z(c, half)))

    def c_step():
        @pl.when(zi > 0)
        def _():
            got(cin, cs_r)

        csend[...] = two_steps(cin[...])[1]

        @pl.when(zi < 3)
        def _():
            c_next().start()

        @pl.when(zi == 3)
        def _():
            for half in range(2):
                away = end_z(c, half) != z

                @pl.when(away)
                def _():
                    c_end(half).start()

                @pl.when(jnp.logical_not(away))
                def _():
                    ch[zh] = csend[...]

    turn = jnp.where(row, 0, jnp.where(pos == 1, NC // 2, jnp.where(pos == 0, NC, 0)))
    slot = jnp.where(end, 1, 0)

    def piece(k):
        return pl.ds(pl.multiple_of(k * ROWS, ROWS), ROWS)

    def z_copy(k):
        return rcopy(
            zout.at[piece(k)], zin.at[slot, piece(k)], zs.at[k], zr.at[slot, k], did(seg, x, nz)
        )

    def z_body(k, _):
        pl.when(k == turn)(c_step)

        @pl.when(k < NC)
        def _():
            @pl.when(pos > 0)
            def _():
                got(zin.at[0, piece(k)], zr.at[0, k])
                zout[piece(k), :] = mm3(zin[0, piece(k), :], whi[...], wlo[...])

            z_copy(k).start()

        return 0

    lax.fori_loop(0, NC + 1, z_body, 0)

    @pl.when(row & (pos > 0))
    def _():
        hi, lo = split(zin[0])
        inhi[...] = hi
        inlo[...] = lo

    iv = jnp.where(x < 2, 1, 0)
    w = jnp.where(x == 1, 0, 1)

    def half_rows(k, half):
        return pl.ds(pl.multiple_of(half * HALF + k * ROWS, ROWS), ROWS)

    def x_copy(k):
        return rcopy(px.at[half_rows(k, zh)], xin.at[piece(k)], xs.at[k], xr.at[k], did(seg, xroot, z))

    def abx_copy(k):
        return rcopy(
            ab.at[w, half_rows(k, zh)], ab.at[w, half_rows(k, zh)], abx_s.at[k], abx_r.at[k], did(seg, 3 - x, z)
        )

    def abz_copy(k, which):
        return rcopy(
            ab.at[which, half_rows(k, zh)], ab.at[which, half_rows(k, zh)],
            abz_s.at[which, k], abz_r.at[which, k], did(seg, x, nz),
        )

    def cx_copy(which, send, to):
        return rcopy(cown, cs.at[which], cx_s.at[send], cx_r.at[which], did(seg, to, z))

    @pl.when(end)
    def _():
        def x_wait(k, _):
            got(zin.at[1, piece(k)], zr.at[1, k])
            return 0

        lax.fori_loop(0, NC, x_wait, 0)
        ia = jnp.where((zh == 0) == (x < 2), 0, 1)
        hi, lo = split(zout[...])
        sphi[ia] = hi
        splo[ia] = lo
        hi, lo = split(zin[1])
        sphi[1 - ia] = hi
        splo[1 - ia] = lo
        for core, dims in ((0, NT), (1, TN)):
            @pl.when(c == core)
            def _():
                p = dot(sphi[0], sphi[1], dims)
                p += dot(splo[0], sphi[1], dims)
                p += dot(sphi[0], splo[1], dims)
                px[...] = p

        @pl.when(outer)
        def _():
            for k in range(NX):
                x_copy(k).start()

        hi, lo = split(px[...])
        wxhi[...] = hi
        wxlo[...] = lo

        @pl.when(zh != c)
        def _():
            got(ch.at[zh], ch_r.at[zh])

        got(ch.at[1 - zh], ch_r.at[1 - zh])
        for core, dims in ((0, NT), (1, NN)):
            @pl.when(c == core)
            def _():
                cx[...] = mm3(ch[0], sphi[iv], splo[iv], dims) + ch[1]

        @pl.when(x == 0)
        def _():
            cown[...] = cx[...]
            cx_copy(0, 0, 1).start()

        @pl.when(x == 1)
        def _():
            got(cs.at[0], cx_r.at[0])
            cown[...] = mm3(cs[0], wxhi[...], wxlo[...]) + cx[...]
            cs[1] = cown[...]
            cx_copy(1, 0, 2).start()

        @pl.when(x == 2)
        def _():
            cown[...] = cx[...]
            cx_copy(2, 0, 3).start()

        @pl.when(x == 3)
        def _():
            got(cs.at[2], cx_r.at[2])
            cown[...] = mm3(cs[2], wxhi[...], wxlo[...], NT) + cx[...]
            cx_copy(3, 0, 2).start()
            cx_copy(3, 1, 1).start()

    @pl.when(root)
    def _():
        def x_body(k, _):
            @pl.when(k < NX)
            def _():
                got(xin.at[piece(k)], xr.at[k])
                ab[w, half_rows(k, zh), :] = mm3(xin[piece(k), :], wxhi[...], wxlo[...])
                abx_copy(k).start()
                abz_copy(k, w).start()

            @pl.when(k >= LAG)
            def _():
                got(ab.at[1 - w, half_rows(k - LAG, zh)], abx_r.at[k - LAG])
                abz_copy(k - LAG, 1 - w).start()

            return 0

        lax.fori_loop(0, NX + LAG, x_body, 0)

        def ab_wait(k, _):
            for which in range(2):
                got(ab.at[which, half_rows(k, 1 - zh)], abz_r.at[which, k])
            return 0

        lax.fori_loop(0, NX, ab_wait, 0)
        for which in range(2):
            hi, lo = split(ab[which])
            abhi[which] = hi
            ablo[which] = lo
        p = dot(abhi[0], abhi[1], NT)
        p += dot(ablo[0], abhi[1], NT)
        p += dot(abhi[0], ablo[1], NT)
        hi, lo = split(p)
        pfhi[...] = hi
        pflo[...] = lo

        @pl.when(x == 2)
        def _():
            got(cs.at[1], cx_r.at[1])

        got(cs.at[3], cx_r.at[3])
        cseg[...] = mm3(cs[1], abhi[1], ablo[1], NT) + cs[3]

    m0 = jnp.concatenate([m0_ref[...], pad], axis=0)
    chained = root | (end & (x == 0))

    @pl.when(chained & first)
    def _():
        m_in[...] = m0

    @pl.when(chained & jnp.logical_not(first))
    def _():
        got(m_in, m_r)

    def m_copy(to, send):
        return rcopy(m_out, m_in, m_s.at[send], m_r, did(seg + 1, to, end_z(1 - c, zh)))

    def f_copy(q):
        part = pl.ds(2 * q, 2)
        return rcopy(f_out.at[part], f_in.at[part], f_s.at[q], f_r.at[q], did(seg + 1, x, end_z(1 - c, zh)))

    def owner(blk):
        return jnp.where(blk < 4, x, xouter), zh * 4 + blk % 4

    def fb_copy(blk):
        ox, oz = owner(blk)
        return rcopy(f_out.at[blk], f_box, fb_s.at[blk], fb_r, did(seg, ox, oz))

    def ex_copy(to):
        return rcopy(e_out, e_x, ex_s, ex_r, did(seg, to, z))

    @pl.when(root)
    def _():
        @pl.when(jnp.logical_not(last))
        def _():
            m_out[...] = mm3(m_in[...], pfhi[...], pflo[...]) + cseg[...]
            m_copy(x, 0).start()

            @pl.when(x == 1)
            def _():
                m_copy(0, 1).start()

        @pl.when(x == 2)
        def _():
            e_x[...] = mm3(m_in[...], abhi[0], ablo[0]) + cs[1]
            e_out[...] = mm3(e_x[...], wxhi[...], wxlo[...], NT) + cx[...]
            ex_copy(3).start()

        def f_body(q, _):
            for u in range(2):
                blk = 2 * q + u

                @pl.when(first & (blk != block))
                def _():
                    got(f_in.at[blk], f0_r.at[blk])

            @pl.when(jnp.logical_not(first))
            def _():
                got(f_in.at[pl.ds(2 * q, 2)], f_r.at[q])

            rows = jnp.concatenate([f_in[2 * q], f_in[2 * q + 1]], axis=0)
            rows = mm3(rows, pfhi[...], pflo[...])
            f_out[2 * q] = rows[:16]
            f_out[2 * q + 1] = rows[16:]

            @pl.when(jnp.logical_not(last))
            def _():
                f_copy(q).start()

            for u in range(2):
                blk = 2 * q + u

                @pl.when(blk != block)
                def _():
                    fb_copy(blk).start()

                @pl.when(blk == block)
                def _():
                    ends_ref[0] = f_out[blk]

            return 0

        lax.fori_loop(0, 4, f_body, 0)

    @pl.when(end & (x == 0))
    def _():
        e_out[...] = mm3(m_in[...], wxhi[...], wxlo[...]) + cx[...]
        ex_copy(1).start()
        e_x[...] = m_in[...]

    @pl.when(end & ((x == 1) | (x == 3)))
    def _():
        got(e_x, ex_r)

    @pl.when(end & (zh == 0))
    def _():
        e_half[...] = e_x[...]

    for core, dims in ((0, NN), (1, NT)):
        @pl.when(end & (zh == 1) & (c == core))
        def _():
            e_half[...] = mm3(e_x[...], sphi[1 - iv], splo[1 - iv], dims) + ch[0]

    def e_copy(src, to, send):
        return rcopy(src, e_in, e_s.at[send], e_r, did(seg, x, to))

    @pl.when(end & row)
    def _():
        for k in range(3):
            e_copy(e_half, zh * 4 + k, k).start()

    @pl.when(jnp.logical_not(end))
    def _():
        got(e_in, e_r)
        e_half[...] = e_in[...]

    @pl.when(row & (pos > 0))
    def _():
        e_half_entry = mm3(e_half[...], inhi[...], inlo[...]) + cin[...]
        m1, m2 = two_steps(e_half_entry)
        means_ref[0] = m1[:4]
        means_ref[1] = m2[:4]

    @pl.when(jnp.logical_not(row & (pos > 0)))
    def _():
        m1, m2 = two_steps(e_half[...])

        @pl.when(jnp.logical_not(row) & (zi < 3))
        def _():
            e_next[...] = m2
            e_copy(e_next, z + 1, 0).start()

        means_ref[0] = m1[:4]
        means_ref[1] = m2[:4]

    @pl.when(jnp.logical_not(root))
    def _():
        got(f_box, fb_r)
        ends_ref[0] = f_box[...]

    def z_done(k, _):
        z_copy(k).wait_send()
        return 0

    lax.fori_loop(0, NC, z_done, 0)

    @pl.when(zi < 3)
    def _():
        c_next().wait_send()

    @pl.when(zi == 3)
    def _():
        for half in range(2):
            @pl.when(end_z(c, half) != z)
            def _():
                c_end(half).wait_send()

    @pl.when(first & jnp.logical_not(root))
    def _():
        f0_copy().wait_send()

    @pl.when(outer)
    def _():
        for k in range(NX):
            x_copy(k).wait_send()

        @pl.when(x == 0)
        def _():
            cx_copy(0, 0, 1).wait_send()

        @pl.when(x == 3)
        def _():
            cx_copy(3, 0, 2).wait_send()
            cx_copy(3, 1, 1).wait_send()

    @pl.when(root)
    def _():
        def ab_done(k, _):
            abx_copy(k).wait_send()
            for which in range(2):
                abz_copy(k, which).wait_send()
            return 0

        lax.fori_loop(0, NX, ab_done, 0)
        cx_copy(1, 0, 3).wait_send()

        @pl.when(jnp.logical_not(last))
        def _():
            m_copy(x, 0).wait_send()

            @pl.when(x == 1)
            def _():
                m_copy(0, 1).wait_send()

            for q in range(4):
                f_copy(q).wait_send()

        for blk in range(8):
            @pl.when(blk != block)
            def _():
                fb_copy(blk).wait_send()

    @pl.when(end & ((x == 0) | (x == 2)))
    def _():
        ex_copy(1).wait_send()

    @pl.when(end & row)
    def _():
        for k in range(3):
            e_copy(e_half, zh * 4 + k, k).wait_send()

    @pl.when(jnp.logical_not(row) & (zi < 3))
    def _():
        e_copy(e_next, z + 1, 0).wait_send()


def per_device(transition, obs_gain, observed, init_mean, init_factor):
    vm = pl.BlockSpec(memory_space=pltpu.VMEM)
    f, b = (lambda *s: pltpu.VMEM(s, F32)), (lambda *s: pltpu.VMEM(s, BF16))
    dma = lambda *s: pltpu.SemaphoreType.DMA(s) if s else pltpu.SemaphoreType.DMA
    scratch = [
        f(D, D), f(2, D, D), b(D, D), b(D, D), f(2, PAD, D), f(PAD, D), f(2, PAD, D), f(PAD, D),
        b(2, D, D), b(2, D, D), f(D, D), b(D, D), b(D, D), f(HALF, D), f(2, D, D), b(2, D, D), b(2, D, D), b(D, D), b(D, D),
        f(4, PAD, D), f(PAD, D), f(PAD, D), f(PAD, D), f(PAD, D), f(PAD, D), f(8, 16, D), f(8, 16, D), f(16, D), b(D, D), b(D, D),
        f(PAD, D), f(PAD, D), f(PAD, D), f(PAD, D), f(PAD, D),
        dma(NC), dma(2, NC), dma(), dma(), dma(2), dma(2), dma(NX), dma(NX), dma(NX), dma(NX), dma(2, NX), dma(2, NX),
        dma(2), dma(4), dma(2), dma(), dma(), dma(8), dma(4), dma(4), dma(8), dma(), dma(3), dma(), dma(), dma(),
    ]
    return pl.pallas_call(
        kernel,
        out_shape=(jax.ShapeDtypeStruct((2, 4, D), F32), jax.ShapeDtypeStruct((1, 16, D), F32)),
        in_specs=[vm] * 5,
        out_specs=(vm, vm),
        scratch_shapes=scratch,
        compiler_params=pltpu.CompilerParams(
            collective_id=0, has_side_effects=True, vmem_limit_bytes=56 * 2**20
        ),
        name="filter_flow",
    )(transition, obs_gain, observed, init_mean, init_factor)


def solution(mesh):
    placed = P(("seg", "tm"), None, None)
    return jax.shard_map(
        per_device,
        mesh=mesh,
        in_specs=(placed, placed, placed, P(), P("tm", None)),
        out_specs=(placed, P("seg", "tm", None)),
        check_vma=False,
    )
```

```python
import functools

import jax
import jax.numpy as jnp
from jax import lax
from jax.experimental import pallas as pl
from jax.experimental.pallas import tpu as pltpu
from jax.sharding import PartitionSpec as P

MESH = pl.DeviceIdType.MESH
F32, BF16 = jnp.float32, jnp.bfloat16
D = 512
HALF = D // 2
ROWS = 32
NC = D // ROWS
NX = HALF // ROWS
LAG = 4
PAD = 8

NN = (((1,), (0,)), ((), ()))
NT = (((1,), (1,)), ((), ()))
TN = (((0,), (0,)), ((), ()))
TT = (((0,), (1,)), ((), ()))


def dot(a, b, dims=NN):
    return lax.dot_general(a, b, dims, preferred_element_type=F32)


def split(a):
    hi = a.astype(BF16)
    return hi, (a - hi.astype(F32)).astype(BF16)


def mm3(a, hi, lo, dims=NN):
    ah, al = split(a)
    n = a.shape[0]
    both = dot(jnp.concatenate([ah, al], axis=0), hi, dims)
    return both[:n] + both[n:] + dot(ah, lo, dims)


def mm2(a, exact):
    ah, al = split(a)
    n = a.shape[0]
    both = dot(jnp.concatenate([ah, al], axis=0), exact)
    return both[:n] + both[n:]


def kernel(
    t_ref, g_ref, o_ref, m0_ref, f0_ref, means_ref, ends_ref,
    zout, zin, whi, wlo, drv, cin, ch, csend,
    sphi, splo, px, wxhi, wxlo, xin, ab, abhi, ablo, pfhi, pflo,
    cs, cx, cseg, cown, m_in, m_out, f_in, f_out, inhi, inlo, e_in, e_out, e_half, e_x, e_next,
    zs, zr, cs_s, cs_r, ch_s, ch_r, xs, xr, abx_s, abx_r, abm_s, abm_r, abz_s, abz_r,
    cx_s, cx_r, m_s, m_r, f0_s, f0_r, f_s, f_r, fb_s, fb_r, e_s, e_r, ex_s, ex_r,
):
    seg = lax.axis_index("seg")
    tm = lax.axis_index("tm")

    def way(s):
        return (s + s // 2) % 2

    c = way(seg)
    x, z = tm // 8, tm % 8
    zh, zi = z // 4, z % 4
    row = zh == c
    pos = jnp.where(row, zi, 3 - zi)
    nz = jnp.where(row, (z + 1) % 8, (z + 7) % 8)
    end = pos == 3
    inner = (x == 1) | (x == 2)
    root = end & inner
    outer = end & jnp.logical_not(inner)
    first, last = seg == 0, seg == 7
    xroot = jnp.where(x < 2, 1, 2)
    xouter = jnp.where(x < 2, 0, 3)

    def end_z(core, half):
        return jnp.where(core == 0, 3 + half, 7 * half)

    def did(s, xx, zz):
        return (s, xx * 8 + zz)

    myend = end_z(c, zh)

    def rcopy(src, dst, ssem, rsem, dev):
        return pltpu.make_async_remote_copy(
            src_ref=src, dst_ref=dst, send_sem=ssem, recv_sem=rsem, device_id=dev, device_id_type=MESH
        )

    def got(dst, rsem):
        rcopy(dst, dst, rsem, rsem, did(seg, x, nz)).wait_recv()

    barrier = pltpu.get_barrier_semaphore()

    def greet(dev):
        pl.semaphore_signal(barrier, inc=1, device_id=dev, device_id_type=MESH)

    pz = jnp.where(row, z - 1, z + 1)

    @pl.when(pos < 3)
    def _():
        greet(did(seg, x, myend))

    @pl.when((pos < 2) | end)
    def _():
        greet(did(seg, x, nz))

    @pl.when((pos == 1) | (pos == 2))
    def _():
        greet(did(seg, x, pz))

    @pl.when((pos == 0) & jnp.logical_not(row))
    def _():
        greet(did(seg, x, end_z(c, 1 - zh)))

    @pl.when(end)
    def _():
        for k in range(1, 4):
            greet(did(seg, x, zh * 4 + (zi + k) % 4))

        @pl.when(row)
        def _():
            greet(did(seg, x, (1 - zh) * 4 + 3))

    for here, others in ((0, (1,)), (1, (0, 2, 3)), (2, (1, 3)), (3, (2, 1))):
        @pl.when(end & (x == here))
        def _():
            for k in others:
                greet(did(seg, k, z))

    @pl.when(jnp.logical_not(inner))
    def _():
        greet(did(seg, xroot, myend))

    @pl.when(root)
    def _():
        for k in range(4):
            greet(did(seg, xouter, zh * 4 + k))

        @pl.when(jnp.logical_not(last))
        def _():
            greet(did(seg + 1, x, end_z(way(seg + 1), zh)))

        @pl.when(jnp.logical_not(first))
        def _():
            greet(did(seg - 1, x, end_z(way(seg - 1), zh)))

    @pl.when(root & (x == 1) & jnp.logical_not(last))
    def _():
        greet(did(seg + 1, 0, end_z(way(seg + 1), zh)))

    @pl.when(end & (x == 0) & jnp.logical_not(first))
    def _():
        greet(did(seg - 1, 1, end_z(way(seg - 1), zh)))

    one = lambda p: jnp.where(p, 1, 0)
    greets = (
        one(pos < 3) + one((pos < 2) | end) + one((pos == 1) | (pos == 2)) + one((pos == 0) & jnp.logical_not(row))
        + one(end) * (3 + one(row) + jnp.where(x == 0, 1, jnp.where(x == 1, 3, 2))) + one(jnp.logical_not(inner))
        + one(root) * (4 + one(jnp.logical_not(last)) + one(jnp.logical_not(first)))
        + one(root & (x == 1) & jnp.logical_not(last)) + one(end & (x == 0) & jnp.logical_not(first))
    )

    def put_map(m):
        @pl.when(pos == 0)
        def _():
            zout[...] = m

        @pl.when(pos > 0)
        def _():
            hi, lo = split(m)
            whi[...] = hi
            wlo[...] = lo

    @pl.when(row)
    def _():
        put_map(dot(t_ref[0], t_ref[1]))

    @pl.when(jnp.logical_not(row))
    def _():
        put_map(dot(t_ref[1], t_ref[0], TT))

    pad = jnp.zeros((PAD - 4, D), F32)
    for s in range(2):
        drv[s] = jnp.concatenate([dot(o_ref[s], g_ref[s]), pad], axis=0)

    @pl.when(zi == 0)
    def _():
        cin[...] = jnp.zeros_like(cin)

    pl.semaphore_wait(barrier, greets)

    def two_steps(m):
        m1 = mm2(m, t_ref[0]) + drv[0]
        return m1, mm2(m1, t_ref[1]) + drv[1]

    def c_next():
        return rcopy(csend, cin, cs_s, cs_r, did(seg, x, (z + 1) % 8))

    def c_end(half):
        return rcopy(csend, ch.at[zh], ch_s.at[half], ch_r.at[zh], did(seg, x, end_z(c, half)))

    def c_step():
        @pl.when(zi > 0)
        def _():
            got(cin, cs_r)

        csend[...] = two_steps(cin[...])[1]

        @pl.when(zi < 3)
        def _():
            c_next().start()

        @pl.when(zi == 3)
        def _():
            for half in range(2):
                away = end_z(c, half) != z

                @pl.when(away)
                def _():
                    c_end(half).start()

                @pl.when(jnp.logical_not(away))
                def _():
                    ch[zh] = csend[...]

    turn = jnp.where(row, 0, jnp.where(pos == 1, NC // 2, jnp.where(pos == 0, NC, 0)))
    slot = jnp.where(end, 1, 0)

    def piece(k):
        return pl.ds(pl.multiple_of(k * ROWS, ROWS), ROWS)

    def z_copy(k):
        return rcopy(
            zout.at[piece(k)], zin.at[slot, piece(k)], zs.at[k], zr.at[slot, k], did(seg, x, nz)
        )

    ia = jnp.where((zh == 0) == (x < 2), 0, 1)

    def z_body(k, _):
        pl.when(k == turn)(c_step)

        @pl.when(k < NC)
        def _():
            @pl.when(pos > 0)
            def _():
                got(zin.at[0, piece(k)], zr.at[0, k])
                v = mm3(zin[0, piece(k), :], whi[...], wlo[...])
                zout[piece(k), :] = v

                @pl.when(end)
                def _():
                    sphi[ia, piece(k), :], splo[ia, piece(k), :] = split(v)


            z_copy(k).start()

        return 0

    lax.fori_loop(0, NC + 1, z_body, 0)

    def z_sent():
        def z_done(k, _):
            z_copy(k).wait_send()
            return 0

        lax.fori_loop(0, NC, z_done, 0)

        @pl.when(zi < 3)
        def _():
            c_next().wait_send()

        @pl.when(zi == 3)
        def _():
            for half in range(2):
                @pl.when(end_z(c, half) != z)
                def _():
                    c_end(half).wait_send()

    @pl.when(row & (pos > 0))
    def _():
        hi, lo = split(zin[0])
        inhi[...] = hi
        inlo[...] = lo

    iv = jnp.where(x < 2, 1, 0)
    w = jnp.where(x == 1, 0, 1)

    def half_rows(k, half):
        return pl.ds(pl.multiple_of(half * HALF + k * ROWS, ROWS), ROWS)

    def x_copy(k):
        return rcopy(px.at[half_rows(k, zh)], xin.at[piece(k)], xs.at[k], xr.at[k], did(seg, xroot, z))

    def abx_copy(k):
        return rcopy(
            ab.at[w, half_rows(k, zh)], ab.at[w, half_rows(k, zh)], abx_s.at[k], abx_r.at[k], did(seg, 3 - x, z)
        )

    def abz_copy(k, which):
        return rcopy(
            ab.at[which, half_rows(k, zh)], ab.at[which, half_rows(k, zh)],
            abz_s.at[which, k], abz_r.at[which, k], did(seg, x, nz),
        )

    def abx_more(k):
        return rcopy(
            ab.at[w, half_rows(k, 1 - zh)], ab.at[w, half_rows(k, 1 - zh)], abm_s.at[k], abm_r.at[k], did(seg, 3 - x, z)
        )

    def ab_split(which, rows):
        abhi[which, rows, :], ablo[which, rows, :] = split(ab[which, rows, :])

    def cx_copy(which, send, to):
        return rcopy(cown, cs.at[which], cx_s.at[send], cx_r.at[which], did(seg, to, z))

    @pl.when(end)
    def _():
        def x_wait(k, _):
            got(zin.at[1, piece(k)], zr.at[1, k])
            sphi[1 - ia, piece(k), :], splo[1 - ia, piece(k), :] = split(zin[1, piece(k), :])
            return 0

        lax.fori_loop(0, NC, x_wait, 0)
        for half in (zh, 1 - zh):
            part = pl.ds(pl.multiple_of(half * HALF, HALF), HALF)
            for core, dims in ((0, NT), (1, TN)):
                @pl.when(c == core)
                def _():
                    at = (part, slice(None)) if core == 0 else (slice(None), part)
                    p = dot(sphi[(0, *at)], sphi[1], dims)
                    p += dot(splo[(0, *at)], sphi[1], dims)
                    p += dot(sphi[(0, *at)], splo[1], dims)
                    px[part, :] = p

            if half is zh:
                @pl.when(outer)
                def _():
                    for k in range(NX):
                        x_copy(k).start()

        hi, lo = split(px[...])
        wxhi[...] = hi
        wxlo[...] = lo

        @pl.when(zh != c)
        def _():
            got(ch.at[zh], ch_r.at[zh])

        got(ch.at[1 - zh], ch_r.at[1 - zh])
        for core, dims in ((0, NT), (1, NN)):
            @pl.when(c == core)
            def _():
                cx[...] = mm3(ch[0], sphi[iv], splo[iv], dims) + ch[1]

        @pl.when(x == 0)
        def _():
            cown[...] = cx[...]
            cx_copy(0, 0, 1).start()

        @pl.when(x == 1)
        def _():
            got(cs.at[0], cx_r.at[0])
            cown[...] = mm3(cs[0], wxhi[...], wxlo[...]) + cx[...]
            cs[1] = cown[...]
            cx_copy(1, 0, 2).start()

        @pl.when(x == 2)
        def _():
            cown[...] = cx[...]
            cx_copy(2, 0, 3).start()

        @pl.when(x == 3)
        def _():
            got(cs.at[2], cx_r.at[2])
            cown[...] = mm3(cs[2], wxhi[...], wxlo[...], NT) + cx[...]
            cx_copy(3, 0, 2).start()
            cx_copy(3, 1, 1).start()

    @pl.when(root)
    def _():
        def x_body(k, _):
            @pl.when(k < NX)
            def _():
                got(xin.at[piece(k)], xr.at[k])
                v = mm3(xin[piece(k), :], wxhi[...], wxlo[...])
                mine = half_rows(k, zh)
                ab[w, mine, :] = v
                abx_copy(k).start()
                abz_copy(k, w).start()
                abhi[w, mine, :], ablo[w, mine, :] = split(v)

            @pl.when(k >= LAG)
            def _():
                j = k - LAG
                got(ab.at[1 - w, half_rows(j, zh)], abx_r.at[j])

                @pl.when(j % 2 == 0)
                def _():
                    abz_copy(j, 1 - w).start()

                ab_split(1 - w, half_rows(j, zh))
                got(ab.at[w, half_rows(j, 1 - zh)], abz_r.at[w, j])

                @pl.when(j % 2 == 1)
                def _():
                    abx_more(j).start()

                ab_split(w, half_rows(j, 1 - zh))

            return 0

        lax.fori_loop(0, NX + LAG, x_body, 0)

        def ab_wait(k, _):
            @pl.when(k % 2 == 0)
            def _():
                got(ab.at[1 - w, half_rows(k, 1 - zh)], abz_r.at[1 - w, k])

            @pl.when(k % 2 == 1)
            def _():
                got(ab.at[1 - w, half_rows(k, 1 - zh)], abm_r.at[k])

            ab_split(1 - w, half_rows(k, 1 - zh))
            return 0

        lax.fori_loop(0, NX, ab_wait, 0)
        p = dot(abhi[0], abhi[1], NT)
        p += dot(ablo[0], abhi[1], NT)
        p += dot(abhi[0], ablo[1], NT)
        hi, lo = split(p)
        pfhi[...] = hi
        pflo[...] = lo

        @pl.when(x == 2)
        def _():
            got(cs.at[1], cx_r.at[1])

        got(cs.at[3], cx_r.at[3])
        cseg[...] = mm3(cs[1], abhi[1], ablo[1], NT) + cs[3]

    def x_sent():
        @pl.when(outer)
        def _():
            for k in range(NX):
                x_copy(k).wait_send()

            @pl.when(x == 0)
            def _():
                cx_copy(0, 0, 1).wait_send()

            @pl.when(x == 3)
            def _():
                cx_copy(3, 0, 2).wait_send()
                cx_copy(3, 1, 1).wait_send()

        @pl.when(root)
        def _():
            def ab_done(k, _):
                abx_copy(k).wait_send()
                abz_copy(k, w).wait_send()

                @pl.when(k % 2 == 0)
                def _():
                    abz_copy(k, 1 - w).wait_send()

                @pl.when(k % 2 == 1)
                def _():
                    abx_more(k).wait_send()

                return 0

            lax.fori_loop(0, NX, ab_done, 0)
            cx_copy(1, 0, 3).wait_send()

    block = jnp.where(x == xroot, 0, 4) + zi

    def f0_copy():
        return rcopy(f0_ref, f_in.at[block], f0_s, f0_r.at[block], did(seg, xroot, myend))

    @pl.when(first & jnp.logical_not(root))
    def _():
        f0_copy().start()

    @pl.when(first & root)
    def _():
        f_in[block] = f0_ref[...]

    m0 = jnp.concatenate([m0_ref[...], pad], axis=0)
    chained = root | (end & (x == 0))

    @pl.when(chained & first)
    def _():
        m_in[...] = m0

    @pl.when(chained & jnp.logical_not(first))
    def _():
        got(m_in, m_r)

    def m_copy(to, send):
        return rcopy(m_out, m_in, m_s.at[send], m_r, did(seg + 1, to, end_z(way(seg + 1), zh)))

    def f_copy(blk):
        return rcopy(f_out.at[blk], f_in.at[blk], f_s.at[blk], f_r.at[blk], did(seg + 1, x, end_z(way(seg + 1), zh)))

    def owner(blk):
        return jnp.where(blk < 4, x, xouter), zh * 4 + blk % 4

    def fb_copy(blk):
        ox, oz = owner(blk)
        return rcopy(f_out.at[blk], ends_ref.at[0], fb_s.at[blk], fb_r, did(seg, ox, oz))

    def ex_copy(to):
        return rcopy(e_out, e_x, ex_s, ex_r, did(seg, to, z))

    @pl.when(root)
    def _():
        @pl.when(jnp.logical_not(last))
        def _():
            m_out[...] = mm3(m_in[...], pfhi[...], pflo[...]) + cseg[...]
            m_copy(x, 0).start()

            @pl.when(x == 1)
            def _():
                m_copy(0, 1).start()

        @pl.when(x == 2)
        def _():
            e_x[...] = mm3(m_in[...], abhi[0], ablo[0]) + cs[1]
            e_out[...] = mm3(e_x[...], wxhi[...], wxlo[...], NT) + cx[...]
            ex_copy(3).start()

        def f_body(blk, _):
            @pl.when(first & (blk != block))
            def _():
                got(f_in.at[blk], f0_r.at[blk])

            @pl.when(jnp.logical_not(first))
            def _():
                got(f_in.at[blk], f_r.at[blk])

            f_out[blk] = mm3(f_in[blk], pfhi[...], pflo[...])

            @pl.when(jnp.logical_not(last))
            def _():
                f_copy(blk).start()

            @pl.when(blk != block)
            def _():
                fb_copy(blk).start()

            @pl.when(blk == block)
            def _():
                ends_ref[0] = f_out[blk]

            return 0

        lax.fori_loop(0, 8, f_body, 0)

    @pl.when(end & (x == 0))
    def _():
        e_out[...] = mm3(m_in[...], wxhi[...], wxlo[...]) + cx[...]
        ex_copy(1).start()
        e_x[...] = m_in[...]

    @pl.when(end & ((x == 1) | (x == 3)))
    def _():
        got(e_x, ex_r)

    @pl.when(end & (zh == 0))
    def _():
        e_half[...] = e_x[...]

    for core, dims in ((0, NN), (1, NT)):
        @pl.when(end & (zh == 1) & (c == core))
        def _():
            e_half[...] = mm3(e_x[...], sphi[1 - iv], splo[1 - iv], dims) + ch[0]

    def e_copy(src, to, send):
        return rcopy(src, e_in, e_s.at[send], e_r, did(seg, x, to))

    @pl.when(end & row)
    def _():
        for k in range(3):
            e_copy(e_half, zh * 4 + k, k).start()

    @pl.when(jnp.logical_not(end))
    def _():
        got(e_in, e_r)
        e_half[...] = e_in[...]

    @pl.when(row & (pos > 0))
    def _():
        e_half_entry = mm3(e_half[...], inhi[...], inlo[...]) + cin[...]
        m1, m2 = two_steps(e_half_entry)
        means_ref[0] = m1[:4]
        means_ref[1] = m2[:4]

    @pl.when(jnp.logical_not(row & (pos > 0)))
    def _():
        m1, m2 = two_steps(e_half[...])

        @pl.when(jnp.logical_not(row) & (zi < 3))
        def _():
            e_next[...] = m2
            e_copy(e_next, z + 1, 0).start()

        means_ref[0] = m1[:4]
        means_ref[1] = m2[:4]

    @pl.when(jnp.logical_not(root))
    def _():
        got(ends_ref.at[0], fb_r)

    def rest_sent():
        @pl.when(first & jnp.logical_not(root))
        def _():
            f0_copy().wait_send()

        @pl.when(root)
        def _():
            @pl.when(jnp.logical_not(last))
            def _():
                m_copy(x, 0).wait_send()

                @pl.when(x == 1)
                def _():
                    m_copy(0, 1).wait_send()

                for blk in range(8):
                    f_copy(blk).wait_send()

            for blk in range(8):
                @pl.when(blk != block)
                def _():
                    fb_copy(blk).wait_send()

        @pl.when(end & ((x == 0) | (x == 2)))
        def _():
            ex_copy(1).wait_send()

        @pl.when(end & row)
        def _():
            for k in range(3):
                e_copy(e_half, zh * 4 + k, k).wait_send()

        @pl.when(jnp.logical_not(row) & (zi < 3))
        def _():
            e_copy(e_next, z + 1, 0).wait_send()

    z_sent()
    x_sent()
    rest_sent()


def per_device(transition, obs_gain, observed, init_mean, init_factor):
    vm = pl.BlockSpec(memory_space=pltpu.VMEM)
    f, b = (lambda *s: pltpu.VMEM(s, F32)), (lambda *s: pltpu.VMEM(s, BF16))
    dma = lambda *s: pltpu.SemaphoreType.DMA(s) if s else pltpu.SemaphoreType.DMA
    scratch = [
        f(D, D), f(2, D, D), b(D, D), b(D, D), f(2, PAD, D), f(PAD, D), f(2, PAD, D), f(PAD, D),
        b(2, D, D), b(2, D, D), f(D, D), b(D, D), b(D, D), f(HALF, D), f(2, D, D), b(2, D, D), b(2, D, D), b(D, D), b(D, D),
        f(4, PAD, D), f(PAD, D), f(PAD, D), f(PAD, D), f(PAD, D), f(PAD, D), f(8, 16, D), f(8, 16, D), b(D, D), b(D, D),
        f(PAD, D), f(PAD, D), f(PAD, D), f(PAD, D), f(PAD, D),
        dma(NC), dma(2, NC), dma(), dma(), dma(2), dma(2), dma(NX), dma(NX), dma(NX), dma(NX), dma(NX), dma(NX), dma(2, NX), dma(2, NX),
        dma(2), dma(4), dma(2), dma(), dma(), dma(8), dma(8), dma(8), dma(8), dma(), dma(3), dma(), dma(), dma(),
    ]
    return pl.pallas_call(
        kernel,
        out_shape=(jax.ShapeDtypeStruct((2, 4, D), F32), jax.ShapeDtypeStruct((1, 16, D), F32)),
        in_specs=[vm] * 5,
        out_specs=(vm, vm),
        scratch_shapes=scratch,
        compiler_params=pltpu.CompilerParams(
            collective_id=0, has_side_effects=True, vmem_limit_bytes=56 * 2**20
        ),
        name="filter_flow",
    )(transition, obs_gain, observed, init_mean, init_factor)


def solution(mesh):
    placed = P(("seg", "tm"), None, None)
    return jax.shard_map(
        per_device,
        mesh=mesh,
        in_specs=(placed, placed, placed, P(), P("tm", None)),
        out_specs=(placed, P("seg", "tm", None)),
        check_vma=False,
    )
```

```python
import functools

import jax
import jax.numpy as jnp
from jax import lax
from jax.experimental import pallas as pl
from jax.experimental.pallas import tpu as pltpu
from jax.sharding import PartitionSpec as P

MESH = pl.DeviceIdType.MESH
F32, BF16 = jnp.float32, jnp.bfloat16
D = 512
HALF = D // 2
ROWS = 32
NC = D // ROWS
NX = HALF // ROWS
LAG = 4
WIDE = 128
NP = D // WIDE
PAD = 8

NN = (((1,), (0,)), ((), ()))
NT = (((1,), (1,)), ((), ()))
TN = (((0,), (0,)), ((), ()))
TT = (((0,), (1,)), ((), ()))


def dot(a, b, dims=NN):
    return lax.dot_general(a, b, dims, preferred_element_type=F32)


def split(a):
    hi = a.astype(BF16)
    return hi, (a - hi.astype(F32)).astype(BF16)


def mm3(a, hi, lo, dims=NN):
    ah, al = split(a)
    n = a.shape[0]
    both = dot(jnp.concatenate([ah, al], axis=0), hi, dims)
    return both[:n] + both[n:] + dot(ah, lo, dims)


def mm2(a, exact):
    ah, al = split(a)
    n = a.shape[0]
    both = dot(jnp.concatenate([ah, al], axis=0), exact)
    return both[:n] + both[n:]


def kernel(
    t_ref, g_ref, o_ref, m0_ref, f0_ref, means_ref, ends_ref,
    zout, zin, whi, wlo, drv, cin, ch, csend,
    sphi, splo, px, wxhi, wxlo, xin, ab, abhi, ablo, pfhi, pflo,
    cs, cx, cseg, cown, m_in, m_out, f_in, f_out, inhi, inlo, e_in, e_out, e_half, e_x, pout,
    ps, zs, zr, cs_s, cs_r, ch_s, ch_r, xs, xr, abx_s, abx_r, abm_s, abm_r, abz_s, abz_r,
    cx_s, cx_r, m_s, m_r, f0_s, f0_r, f_s, f_r, fb_s, fb_r, e_s, e_r, ex_s, ex_r,
):
    seg = lax.axis_index("seg")
    tm = lax.axis_index("tm")

    def way(s):
        return (s + s // 2) % 2

    c = way(seg)
    x, z = tm // 8, tm % 8
    zh, zi = z // 4, z % 4
    row = zh == c
    pos = jnp.where(row, zi, 3 - zi)
    nz = jnp.where(row, (z + 1) % 8, (z + 7) % 8)
    end = pos == 3
    inner = (x == 1) | (x == 2)
    root = end & inner
    outer = end & jnp.logical_not(inner)
    first, last = seg == 0, seg == 7
    xroot = jnp.where(x < 2, 1, 2)
    xouter = jnp.where(x < 2, 0, 3)

    def end_z(core, half):
        return jnp.where(core == 0, 3 + half, 7 * half)

    def did(s, xx, zz):
        return (s, xx * 8 + zz)

    myend = end_z(c, zh)

    def rcopy(src, dst, ssem, rsem, dev):
        return pltpu.make_async_remote_copy(
            src_ref=src, dst_ref=dst, send_sem=ssem, recv_sem=rsem, device_id=dev, device_id_type=MESH
        )

    def got(dst, rsem):
        rcopy(dst, dst, rsem, rsem, did(seg, x, nz)).wait_recv()

    barrier = pltpu.get_barrier_semaphore()

    def greet(dev):
        pl.semaphore_signal(barrier, inc=1, device_id=dev, device_id_type=MESH)

    pz = jnp.where(row, z - 1, z + 1)

    @pl.when(pos < 3)
    def _():
        greet(did(seg, x, myend))

    @pl.when((pos < 2) | end)
    def _():
        greet(did(seg, x, nz))

    @pl.when((pos == 1) | (pos == 2))
    def _():
        greet(did(seg, x, pz))

    @pl.when((pos == 0) & jnp.logical_not(row))
    def _():
        greet(did(seg, x, end_z(c, 1 - zh)))

    @pl.when(end)
    def _():
        for k in range(1, 4):
            greet(did(seg, x, zh * 4 + (zi + k) % 4))

        @pl.when(row)
        def _():
            greet(did(seg, x, (1 - zh) * 4 + 3))

    for here, others in ((0, (1,)), (1, (0, 2, 3)), (2, (1, 3)), (3, (2, 1))):
        @pl.when(end & (x == here))
        def _():
            for k in others:
                greet(did(seg, k, z))

    @pl.when(jnp.logical_not(inner))
    def _():
        greet(did(seg, xroot, myend))

    @pl.when(root)
    def _():
        for k in range(4):
            greet(did(seg, xouter, zh * 4 + k))

        @pl.when(jnp.logical_not(last))
        def _():
            greet(did(seg + 1, x, end_z(way(seg + 1), zh)))

        @pl.when(jnp.logical_not(first))
        def _():
            greet(did(seg - 1, x, end_z(way(seg - 1), zh)))

    @pl.when(root & (x == 1) & jnp.logical_not(last))
    def _():
        greet(did(seg + 1, 0, end_z(way(seg + 1), zh)))

    @pl.when(end & (x == 0) & jnp.logical_not(first))
    def _():
        greet(did(seg - 1, 1, end_z(way(seg - 1), zh)))

    one = lambda p: jnp.where(p, 1, 0)
    greets = (
        one(pos < 3) + one((pos < 2) | end) + one((pos == 1) | (pos == 2)) + one((pos == 0) & jnp.logical_not(row))
        + one(end) * (3 + one(row) + jnp.where(x == 0, 1, jnp.where(x == 1, 3, 2))) + one(jnp.logical_not(inner))
        + one(root) * (4 + one(jnp.logical_not(last)) + one(jnp.logical_not(first)))
        + one(root & (x == 1) & jnp.logical_not(last)) + one(end & (x == 0) & jnp.logical_not(first))
    )

    def put_map(m):
        @pl.when(pos == 0)
        def _():
            zout[...] = m

        @pl.when(pos > 0)
        def _():
            hi, lo = split(m)
            whi[...] = hi
            wlo[...] = lo

    @pl.when(row)
    def _():
        put_map(dot(t_ref[0], t_ref[1]))

    @pl.when(jnp.logical_not(row))
    def _():
        put_map(dot(t_ref[1], t_ref[0], TT))

        @pl.when(end)
        def _():
            pout[...] = dot(t_ref[0], t_ref[1])

    pad = jnp.zeros((PAD - 4, D), F32)
    for s in range(2):
        drv[s] = jnp.concatenate([dot(o_ref[s], g_ref[s]), pad], axis=0)

    @pl.when(zi == 0)
    def _():
        cin[...] = jnp.zeros_like(cin)

    pl.semaphore_wait(barrier, greets)

    block = jnp.where(x == xroot, 0, 4) + zi

    def f0_copy():
        return rcopy(f0_ref, f_in.at[block], f0_s, f0_r.at[block], did(seg, xroot, myend))

    @pl.when(first & jnp.logical_not(root))
    def _():
        f0_copy().start()

    @pl.when(first & root)
    def _():
        f_in[block] = f0_ref[...]

    def two_steps(m):
        m1 = mm2(m, t_ref[0]) + drv[0]
        return m1, mm2(m1, t_ref[1]) + drv[1]

    def c_next():
        return rcopy(csend, cin, cs_s, cs_r, did(seg, x, (z + 1) % 8))

    def c_end(half):
        return rcopy(csend, ch.at[zh], ch_s.at[half], ch_r.at[zh], did(seg, x, end_z(c, half)))

    def c_step():
        @pl.when(zi > 0)
        def _():
            got(cin, cs_r)

        csend[...] = two_steps(cin[...])[1]

        @pl.when(zi < 3)
        def _():
            c_next().start()

        @pl.when(zi == 3)
        def _():
            for half in range(2):
                away = end_z(c, half) != z

                @pl.when(away)
                def _():
                    c_end(half).start()

                @pl.when(jnp.logical_not(away))
                def _():
                    ch[zh] = csend[...]

    turn = jnp.where(row, 0, jnp.where(pos == 1, NC // 2, jnp.where(pos == 0, NC, 0)))
    slot = jnp.where(end, 1, 0)

    def piece(k):
        return pl.ds(pl.multiple_of(k * ROWS, ROWS), ROWS)

    def z_copy(k):
        return rcopy(
            zout.at[piece(k)], zin.at[slot, piece(k)], zs.at[k], zr.at[slot, k], did(seg, x, nz)
        )

    ia = jnp.where((zh == 0) == (x < 2), 0, 1)

    def z_body(k, _):
        pl.when(k == turn)(c_step)

        @pl.when(k < NC)
        def _():
            @pl.when(pos > 0)
            def _():
                got(zin.at[0, piece(k)], zr.at[0, k])
                v = mm3(zin[0, piece(k), :], whi[...], wlo[...])
                zout[piece(k), :] = v

                @pl.when(end)
                def _():
                    sphi[ia, piece(k), :], splo[ia, piece(k), :] = split(v)


            z_copy(k).start()

        return 0

    lax.fori_loop(0, NC + 1, z_body, 0)

    def z_sent():
        def z_done(k, _):
            z_copy(k).wait_send()
            return 0

        lax.fori_loop(0, NC, z_done, 0)

        @pl.when(zi < 3)
        def _():
            c_next().wait_send()

        @pl.when(zi == 3)
        def _():
            for half in range(2):
                @pl.when(end_z(c, half) != z)
                def _():
                    c_end(half).wait_send()

    def wide(k):
        return pl.ds(pl.multiple_of(k * WIDE, WIDE), WIDE)

    def p_copy(k):
        return rcopy(pout.at[wide(k)], zin.at[1, wide(k)], ps.at[k], zr.at[1, k], did(seg, x, z + 1))

    def p_body(k, _):
        got(zin.at[1, wide(k)], zr.at[1, k])

        @pl.when(zi < 3)
        def _():
            pout[wide(k), :] = mm3(zin[1, wide(k), :], whi[...], wlo[...], NT)
            p_copy(k).start()

        return 0

    def p_start(k, _):
        p_copy(k).start()
        return 0

    def p_done(k, _):
        p_copy(k).wait_send()
        return 0

    @pl.when(jnp.logical_not(row | end))
    def _():
        lax.fori_loop(0, NP, p_body, 0)

    @pl.when(zi > 0)
    def _():
        hi, lo = split(zin[jnp.where(row, 0, 1)])
        inhi[...] = hi
        inlo[...] = lo

    iv = jnp.where(x < 2, 1, 0)
    w = jnp.where(x == 1, 0, 1)

    def half_rows(k, half):
        return pl.ds(pl.multiple_of(half * HALF + k * ROWS, ROWS), ROWS)

    def x_copy(k):
        return rcopy(px.at[half_rows(k, zh)], xin.at[piece(k)], xs.at[k], xr.at[k], did(seg, xroot, z))

    def abx_copy(k):
        return rcopy(
            ab.at[w, half_rows(k, zh)], ab.at[w, half_rows(k, zh)], abx_s.at[k], abx_r.at[k], did(seg, 3 - x, z)
        )

    def abz_copy(k, which):
        return rcopy(
            ab.at[which, half_rows(k, zh)], ab.at[which, half_rows(k, zh)],
            abz_s.at[which, k], abz_r.at[which, k], did(seg, x, nz),
        )

    def abx_more(k):
        return rcopy(
            ab.at[w, half_rows(k, 1 - zh)], ab.at[w, half_rows(k, 1 - zh)], abm_s.at[k], abm_r.at[k], did(seg, 3 - x, z)
        )

    def ab_split(which, rows):
        abhi[which, rows, :], ablo[which, rows, :] = split(ab[which, rows, :])

    def cx_copy(which, send, to):
        return rcopy(cown, cs.at[which], cx_s.at[send], cx_r.at[which], did(seg, to, z))

    @pl.when(end)
    def _():
        def x_wait(k, _):
            got(zin.at[1, piece(k)], zr.at[1, k])
            sphi[1 - ia, piece(k), :], splo[1 - ia, piece(k), :] = split(zin[1, piece(k), :])
            return 0

        lax.fori_loop(0, NC, x_wait, 0)
        for half in (zh, 1 - zh):
            part = pl.ds(pl.multiple_of(half * HALF, HALF), HALF)
            for core, dims in ((0, NT), (1, TN)):
                @pl.when(c == core)
                def _():
                    at = (part, slice(None)) if core == 0 else (slice(None), part)
                    p = dot(sphi[(0, *at)], sphi[1], dims)
                    p += dot(splo[(0, *at)], sphi[1], dims)
                    p += dot(sphi[(0, *at)], splo[1], dims)
                    px[part, :] = p

            if half is zh:
                @pl.when(outer)
                def _():
                    for k in range(NX):
                        x_copy(k).start()

        hi, lo = split(px[...])
        wxhi[...] = hi
        wxlo[...] = lo

        @pl.when(zh != c)
        def _():
            got(ch.at[zh], ch_r.at[zh])

        got(ch.at[1 - zh], ch_r.at[1 - zh])
        for core, dims in ((0, NT), (1, NN)):
            @pl.when(c == core)
            def _():
                cx[...] = mm3(ch[0], sphi[iv], splo[iv], dims) + ch[1]

        @pl.when(x == 0)
        def _():
            cown[...] = cx[...]
            cx_copy(0, 0, 1).start()

        @pl.when(x == 1)
        def _():
            got(cs.at[0], cx_r.at[0])
            cown[...] = mm3(cs[0], wxhi[...], wxlo[...]) + cx[...]
            cs[1] = cown[...]
            cx_copy(1, 0, 2).start()

        @pl.when(x == 2)
        def _():
            cown[...] = cx[...]
            cx_copy(2, 0, 3).start()

        @pl.when(x == 3)
        def _():
            got(cs.at[2], cx_r.at[2])
            cown[...] = mm3(cs[2], wxhi[...], wxlo[...], NT) + cx[...]
            cx_copy(3, 0, 2).start()
            cx_copy(3, 1, 1).start()

    @pl.when(end & jnp.logical_not(row))
    def _():
        lax.fori_loop(0, NP, p_start, 0)

    @pl.when(root)
    def _():
        def x_body(k, _):
            @pl.when(k < NX)
            def _():
                got(xin.at[piece(k)], xr.at[k])
                v = mm3(xin[piece(k), :], wxhi[...], wxlo[...])
                mine = half_rows(k, zh)
                ab[w, mine, :] = v
                abx_copy(k).start()
                abz_copy(k, w).start()
                abhi[w, mine, :], ablo[w, mine, :] = split(v)

            @pl.when(k >= LAG)
            def _():
                j = k - LAG
                got(ab.at[1 - w, half_rows(j, zh)], abx_r.at[j])

                @pl.when(j % 2 == 0)
                def _():
                    abz_copy(j, 1 - w).start()

                ab_split(1 - w, half_rows(j, zh))
                got(ab.at[w, half_rows(j, 1 - zh)], abz_r.at[w, j])

                @pl.when(j % 2 == 1)
                def _():
                    abx_more(j).start()

                ab_split(w, half_rows(j, 1 - zh))

            return 0

        lax.fori_loop(0, NX + LAG, x_body, 0)

        def ab_wait(k, _):
            @pl.when(k % 2 == 0)
            def _():
                got(ab.at[1 - w, half_rows(k, 1 - zh)], abz_r.at[1 - w, k])

            @pl.when(k % 2 == 1)
            def _():
                got(ab.at[1 - w, half_rows(k, 1 - zh)], abm_r.at[k])

            ab_split(1 - w, half_rows(k, 1 - zh))
            return 0

        lax.fori_loop(0, NX, ab_wait, 0)
        p = dot(abhi[0], abhi[1], NT)
        p += dot(ablo[0], abhi[1], NT)
        p += dot(abhi[0], ablo[1], NT)
        hi, lo = split(p)
        pfhi[...] = hi
        pflo[...] = lo

        @pl.when(x == 2)
        def _():
            got(cs.at[1], cx_r.at[1])

        got(cs.at[3], cx_r.at[3])
        cseg[...] = mm3(cs[1], abhi[1], ablo[1], NT) + cs[3]

    def x_sent():
        @pl.when(outer)
        def _():
            for k in range(NX):
                x_copy(k).wait_send()

            @pl.when(x == 0)
            def _():
                cx_copy(0, 0, 1).wait_send()

            @pl.when(x == 3)
            def _():
                cx_copy(3, 0, 2).wait_send()
                cx_copy(3, 1, 1).wait_send()

        @pl.when(root)
        def _():
            def ab_done(k, _):
                abx_copy(k).wait_send()
                abz_copy(k, w).wait_send()

                @pl.when(k % 2 == 0)
                def _():
                    abz_copy(k, 1 - w).wait_send()

                @pl.when(k % 2 == 1)
                def _():
                    abx_more(k).wait_send()

                return 0

            lax.fori_loop(0, NX, ab_done, 0)
            cx_copy(1, 0, 3).wait_send()

    m0 = jnp.concatenate([m0_ref[...], pad], axis=0)
    chained = root | (end & (x == 0))

    @pl.when(chained & first)
    def _():
        m_in[...] = m0

    @pl.when(chained & jnp.logical_not(first))
    def _():
        got(m_in, m_r)

    def m_copy(to, send):
        return rcopy(m_out, m_in, m_s.at[send], m_r, did(seg + 1, to, end_z(way(seg + 1), zh)))

    def f_copy(blk):
        return rcopy(f_out.at[blk], f_in.at[blk], f_s.at[blk], f_r.at[blk], did(seg + 1, x, end_z(way(seg + 1), zh)))

    def owner(blk):
        return jnp.where(blk < 4, x, xouter), zh * 4 + blk % 4

    def fb_copy(blk):
        ox, oz = owner(blk)
        return rcopy(f_out.at[blk], ends_ref.at[0], fb_s.at[blk], fb_r, did(seg, ox, oz))

    def ex_copy(to):
        return rcopy(e_out, e_x, ex_s, ex_r, did(seg, to, z))

    @pl.when(root)
    def _():
        @pl.when(jnp.logical_not(last))
        def _():
            m_out[...] = mm3(m_in[...], pfhi[...], pflo[...]) + cseg[...]
            m_copy(x, 0).start()

            @pl.when(x == 1)
            def _():
                m_copy(0, 1).start()

        @pl.when(x == 2)
        def _():
            e_x[...] = mm3(m_in[...], abhi[0], ablo[0]) + cs[1]
            e_out[...] = mm3(e_x[...], wxhi[...], wxlo[...], NT) + cx[...]
            ex_copy(3).start()


    def e_copy(k):
        return rcopy(e_half, e_in, e_s.at[k], e_r, did(seg, x, zh * 4 + (zi + k + 1) % 4))

    def go_down():
        @pl.when(end & (x == 0))
        def _():
            e_out[...] = mm3(m_in[...], wxhi[...], wxlo[...]) + cx[...]
            ex_copy(1).start()
            e_x[...] = m_in[...]

        @pl.when(end & ((x == 1) | (x == 3)))
        def _():
            got(e_x, ex_r)

        @pl.when(end & (zh == 0))
        def _():
            e_half[...] = e_x[...]

        for core, dims in ((0, NN), (1, NT)):
            @pl.when(end & (zh == 1) & (c == core))
            def _():
                e_half[...] = mm3(e_x[...], sphi[1 - iv], splo[1 - iv], dims) + ch[0]

        @pl.when(end)
        def _():
            for k in range(3):
                e_copy(k).start()

        @pl.when(jnp.logical_not(end))
        def _():
            got(e_in, e_r)
            e_half[...] = e_in[...]

        @pl.when(zi > 0)
        def _():
            e_in[...] = mm3(e_half[...], inhi[...], inlo[...]) + cin[...]

        @pl.when(zi == 0)
        def _():
            e_in[...] = e_half[...]

        m1, m2 = two_steps(e_in[...])
        means_ref[0] = m1[:4]
        means_ref[1] = m2[:4]

    def f_block(blk):
        @pl.when(first & (blk != block))
        def _():
            got(f_in.at[blk], f0_r.at[blk])

        @pl.when(jnp.logical_not(first))
        def _():
            got(f_in.at[blk], f_r.at[blk])

        f_out[blk] = mm3(f_in[blk], pfhi[...], pflo[...])

        @pl.when(jnp.logical_not(last))
        def _():
            f_copy(blk).start()

        @pl.when(blk != block)
        def _():
            fb_copy(blk).start()

        @pl.when(blk == block)
        def _():
            ends_ref[0] = f_out[blk]

    down_turn = jnp.where(root, jnp.where(last, jnp.where(x == 2, 0, 6), 8), 0)

    def chain_body(k, _):
        pl.when(k == down_turn)(go_down)

        @pl.when(root & (k < 8))
        def _():
            f_block(k)

        return 0

    lax.fori_loop(0, jnp.where(root, 9, 1), chain_body, 0)

    @pl.when(jnp.logical_not(root))
    def _():
        got(ends_ref.at[0], fb_r)

    def rest_sent():
        @pl.when(first & jnp.logical_not(root))
        def _():
            f0_copy().wait_send()

        @pl.when(root)
        def _():
            @pl.when(jnp.logical_not(last))
            def _():
                m_copy(x, 0).wait_send()

                @pl.when(x == 1)
                def _():
                    m_copy(0, 1).wait_send()

                for blk in range(8):
                    f_copy(blk).wait_send()

            for blk in range(8):
                @pl.when(blk != block)
                def _():
                    fb_copy(blk).wait_send()

        @pl.when(end & ((x == 0) | (x == 2)))
        def _():
            ex_copy(1).wait_send()

        @pl.when(end)
        def _():
            for k in range(3):
                e_copy(k).wait_send()

        @pl.when(jnp.logical_not(row) & (zi < 3))
        def _():
            lax.fori_loop(0, NP, p_done, 0)

    z_sent()
    x_sent()
    rest_sent()


def per_device(transition, obs_gain, observed, init_mean, init_factor):
    vm = pl.BlockSpec(memory_space=pltpu.VMEM)
    f, b = (lambda *s: pltpu.VMEM(s, F32)), (lambda *s: pltpu.VMEM(s, BF16))
    dma = lambda *s: pltpu.SemaphoreType.DMA(s) if s else pltpu.SemaphoreType.DMA
    scratch = [
        f(D, D), f(2, D, D), b(D, D), b(D, D), f(2, PAD, D), f(PAD, D), f(2, PAD, D), f(PAD, D),
        b(2, D, D), b(2, D, D), f(D, D), b(D, D), b(D, D), f(HALF, D), f(2, D, D), b(2, D, D), b(2, D, D), b(D, D), b(D, D),
        f(4, PAD, D), f(PAD, D), f(PAD, D), f(PAD, D), f(PAD, D), f(PAD, D), f(8, 16, D), f(8, 16, D), b(D, D), b(D, D),
        f(PAD, D), f(PAD, D), f(PAD, D), f(PAD, D), f(D, D),
        dma(NP), dma(NC), dma(2, NC), dma(), dma(), dma(2), dma(2), dma(NX), dma(NX), dma(NX), dma(NX), dma(NX), dma(NX), dma(2, NX), dma(2, NX),
        dma(2), dma(4), dma(2), dma(), dma(), dma(8), dma(8), dma(8), dma(8), dma(), dma(3), dma(), dma(), dma(),
    ]
    return pl.pallas_call(
        kernel,
        out_shape=(jax.ShapeDtypeStruct((2, 4, D), F32), jax.ShapeDtypeStruct((1, 16, D), F32)),
        in_specs=[vm] * 5,
        out_specs=(vm, vm),
        scratch_shapes=scratch,
        compiler_params=pltpu.CompilerParams(
            collective_id=0, has_side_effects=True, vmem_limit_bytes=56 * 2**20
        ),
        name="filter_flow",
    )(transition, obs_gain, observed, init_mean, init_factor)


def solution(mesh):
    placed = P(("seg", "tm"), None, None)
    return jax.shard_map(
        per_device,
        mesh=mesh,
        in_specs=(placed, placed, placed, P(), P("tm", None)),
        out_specs=(placed, P("seg", "tm", None)),
        check_vma=False,
    )
```

```python
import functools

import jax
import jax.numpy as jnp
from jax import lax
from jax.experimental import pallas as pl
from jax.experimental.pallas import tpu as pltpu
from jax.sharding import PartitionSpec as P

MESH = pl.DeviceIdType.MESH
F32, BF16 = jnp.float32, jnp.bfloat16
D = 512
HALF = D // 2
ROWS = 32
NC = D // ROWS
XROWS = 32
NX = HALF // XROWS
LAG = 6
WIDE = 128
NP = D // WIDE
PAD = 8

NN = (((1,), (0,)), ((), ()))
NT = (((1,), (1,)), ((), ()))
TN = (((0,), (0,)), ((), ()))
TT = (((0,), (1,)), ((), ()))


def dot(a, b, dims=NN):
    return lax.dot_general(a, b, dims, preferred_element_type=F32)


def split(a):
    hi = a.astype(BF16)
    return hi, (a - hi.astype(F32)).astype(BF16)


def mm3(a, hi, lo, dims=NN):
    ah, al = split(a)
    n = a.shape[0]
    both = dot(jnp.concatenate([ah, al], axis=0), hi, dims)
    return both[:n] + both[n:] + dot(ah, lo, dims)


def mm2(a, exact):
    ah, al = split(a)
    n = a.shape[0]
    both = dot(jnp.concatenate([ah, al], axis=0), exact)
    return both[:n] + both[n:]


def kernel(
    t_ref, g_ref, o_ref, m0_ref, f0_ref, means_ref, ends_ref,
    zout, zin, whi, wlo, drv, cin, ch, csend,
    sphi, splo, px, wxhi, wxlo, xin, ab, abhi, ablo, pfhi, pflo,
    cs, cx, cseg, cown, m_in, m_out, f_in, f_out, inhi, inlo, e_in, e_out, e_half, e_x, pout,
    ps, zs, zr, cs_s, cs_r, ch_s, ch_r, xs, xr, abx_s, abx_r, abm_s, abm_r, abz_s, abz_r,
    cx_s, cx_r, m_s, m_r, f0_s, f0_r, f_s, f_r, fb_s, fb_r, e_s, e_r, ex_s, ex_r,
):
    seg = lax.axis_index("seg")
    tm = lax.axis_index("tm")

    def way(s):
        return (s + s // 2) % 2

    c = way(seg)
    x, z = tm // 8, tm % 8
    zh, zi = z // 4, z % 4
    row = zh == c
    pos = jnp.where(row, zi, 3 - zi)
    nz = jnp.where(row, (z + 1) % 8, (z + 7) % 8)
    end = pos == 3
    inner = (x == 1) | (x == 2)
    root = end & inner
    outer = end & jnp.logical_not(inner)
    first, last = seg == 0, seg == 7
    xroot = jnp.where(x < 2, 1, 2)
    xouter = jnp.where(x < 2, 0, 3)

    def end_z(core, half):
        return jnp.where(core == 0, 3 + half, 7 * half)

    def did(s, xx, zz):
        return (s, xx * 8 + zz)

    myend = end_z(c, zh)

    def rcopy(src, dst, ssem, rsem, dev):
        return pltpu.make_async_remote_copy(
            src_ref=src, dst_ref=dst, send_sem=ssem, recv_sem=rsem, device_id=dev, device_id_type=MESH
        )

    def got(dst, rsem):
        rcopy(dst, dst, rsem, rsem, did(seg, x, nz)).wait_recv()

    barrier = pltpu.get_barrier_semaphore()

    def greet(dev):
        pl.semaphore_signal(barrier, inc=1, device_id=dev, device_id_type=MESH)

    pz = jnp.where(row, z - 1, z + 1)

    @pl.when(pos < 3)
    def _():
        greet(did(seg, x, myend))

    @pl.when((pos < 2) | end)
    def _():
        greet(did(seg, x, nz))

    @pl.when((pos == 1) | (pos == 2))
    def _():
        greet(did(seg, x, pz))

    @pl.when((pos == 0) & jnp.logical_not(row))
    def _():
        greet(did(seg, x, end_z(c, 1 - zh)))

    @pl.when(end)
    def _():
        for k in range(1, 4):
            greet(did(seg, x, zh * 4 + (zi + k) % 4))

        @pl.when(row)
        def _():
            greet(did(seg, x, (1 - zh) * 4 + 3))

    for here, others in ((0, (1,)), (1, (0, 2, 3)), (2, (1, 3)), (3, (2, 1))):
        @pl.when(end & (x == here))
        def _():
            for k in others:
                greet(did(seg, k, z))

    @pl.when(jnp.logical_not(inner))
    def _():
        greet(did(seg, xroot, myend))

    @pl.when(root)
    def _():
        for k in range(4):
            greet(did(seg, xouter, zh * 4 + k))

        @pl.when(jnp.logical_not(last))
        def _():
            greet(did(seg + 1, x, end_z(way(seg + 1), zh)))

        @pl.when(jnp.logical_not(first))
        def _():
            greet(did(seg - 1, x, end_z(way(seg - 1), zh)))

    @pl.when(root & (x == 1) & jnp.logical_not(last))
    def _():
        greet(did(seg + 1, 0, end_z(way(seg + 1), zh)))

    @pl.when(end & (x == 0) & jnp.logical_not(first))
    def _():
        greet(did(seg - 1, 1, end_z(way(seg - 1), zh)))

    one = lambda p: jnp.where(p, 1, 0)
    greets = (
        one(pos < 3) + one((pos < 2) | end) + one((pos == 1) | (pos == 2)) + one((pos == 0) & jnp.logical_not(row))
        + one(end) * (3 + one(row) + jnp.where(x == 0, 1, jnp.where(x == 1, 3, 2))) + one(jnp.logical_not(inner))
        + one(root) * (4 + one(jnp.logical_not(last)) + one(jnp.logical_not(first)))
        + one(root & (x == 1) & jnp.logical_not(last)) + one(end & (x == 0) & jnp.logical_not(first))
    )

    def put_map(m):
        @pl.when(pos == 0)
        def _():
            zout[...] = m

        @pl.when(pos > 0)
        def _():
            hi, lo = split(m)
            whi[...] = hi
            wlo[...] = lo

    @pl.when(row)
    def _():
        put_map(dot(t_ref[0], t_ref[1]))

    @pl.when(jnp.logical_not(row))
    def _():
        put_map(dot(t_ref[1], t_ref[0], TT))

        @pl.when(end)
        def _():
            pout[...] = dot(t_ref[0], t_ref[1])

    pad = jnp.zeros((PAD - 4, D), F32)
    for s in range(2):
        drv[s] = jnp.concatenate([dot(o_ref[s], g_ref[s]), pad], axis=0)

    @pl.when(zi == 0)
    def _():
        cin[...] = jnp.zeros_like(cin)

    pl.semaphore_wait(barrier, greets)

    block = jnp.where(x == xroot, 0, 4) + zi

    def f0_copy():
        return rcopy(f0_ref, f_in.at[block], f0_s, f0_r.at[block], did(seg, xroot, myend))

    @pl.when(first & jnp.logical_not(root))
    def _():
        f0_copy().start()

    @pl.when(first & root)
    def _():
        f_in[block] = f0_ref[...]

    def two_steps(m):
        m1 = mm2(m, t_ref[0]) + drv[0]
        return m1, mm2(m1, t_ref[1]) + drv[1]

    def c_next():
        return rcopy(csend, cin, cs_s, cs_r, did(seg, x, (z + 1) % 8))

    def c_end(half):
        return rcopy(csend, ch.at[zh], ch_s.at[half], ch_r.at[zh], did(seg, x, end_z(c, half)))

    def c_step():
        @pl.when(zi > 0)
        def _():
            got(cin, cs_r)

        csend[...] = two_steps(cin[...])[1]

        @pl.when(zi < 3)
        def _():
            c_next().start()

        @pl.when(zi == 3)
        def _():
            for half in range(2):
                away = end_z(c, half) != z

                @pl.when(away)
                def _():
                    c_end(half).start()

                @pl.when(jnp.logical_not(away))
                def _():
                    ch[zh] = csend[...]

    turn = jnp.where(row, 0, jnp.where(pos == 1, NC // 2, jnp.where(pos == 0, NC, 0)))
    slot = jnp.where(end, 1, 0)

    def piece(k):
        return pl.ds(pl.multiple_of(k * ROWS, ROWS), ROWS)

    def z_copy(k):
        return rcopy(
            zout.at[piece(k)], zin.at[slot, piece(k)], zs.at[k], zr.at[slot, k], did(seg, x, nz)
        )

    ia = jnp.where((zh == 0) == (x < 2), 0, 1)

    def z_body(k, _):
        pl.when(k == turn)(c_step)

        @pl.when(k < NC)
        def _():
            @pl.when(pos > 0)
            def _():
                got(zin.at[0, piece(k)], zr.at[0, k])
                v = mm3(zin[0, piece(k), :], whi[...], wlo[...])
                zout[piece(k), :] = v

                @pl.when(end)
                def _():
                    sphi[ia, piece(k), :], splo[ia, piece(k), :] = split(v)


            z_copy(k).start()

        return 0

    lax.fori_loop(0, NC + 1, z_body, 0)

    def z_sent():
        def z_done(k, _):
            z_copy(k).wait_send()
            return 0

        lax.fori_loop(0, NC, z_done, 0)

        @pl.when(zi < 3)
        def _():
            c_next().wait_send()

        @pl.when(zi == 3)
        def _():
            for half in range(2):
                @pl.when(end_z(c, half) != z)
                def _():
                    c_end(half).wait_send()

    def wide(k):
        return pl.ds(pl.multiple_of(k * WIDE, WIDE), WIDE)

    def p_copy(k):
        return rcopy(pout.at[wide(k)], zin.at[1, wide(k)], ps.at[k], zr.at[1, k], did(seg, x, z + 1))

    def p_body(k, _):
        got(zin.at[1, wide(k)], zr.at[1, k])

        @pl.when(zi < 3)
        def _():
            pout[wide(k), :] = mm3(zin[1, wide(k), :], whi[...], wlo[...], NT)
            p_copy(k).start()

        return 0

    def p_start(k, _):
        p_copy(k).start()
        return 0

    def p_done(k, _):
        p_copy(k).wait_send()
        return 0

    @pl.when(jnp.logical_not(row | end))
    def _():
        lax.fori_loop(0, NP, p_body, 0)

    @pl.when(zi > 0)
    def _():
        hi, lo = split(zin[jnp.where(row, 0, 1)])
        inhi[...] = hi
        inlo[...] = lo

    iv = jnp.where(x < 2, 1, 0)
    w = jnp.where(x == 1, 0, 1)

    def half_rows(k, half):
        return pl.ds(pl.multiple_of(half * HALF + k * XROWS, XROWS), XROWS)

    def x_copy(k):
        return rcopy(px.at[half_rows(k, zh)], xin.at[half_rows(k, 0)], xs.at[k], xr.at[k], did(seg, xroot, z))

    def abx_copy(k):
        return rcopy(
            ab.at[w, half_rows(k, zh)], ab.at[w, half_rows(k, zh)], abx_s.at[k], abx_r.at[k], did(seg, 3 - x, z)
        )

    def abz_copy(k, which):
        return rcopy(
            ab.at[which, half_rows(k, zh)], ab.at[which, half_rows(k, zh)],
            abz_s.at[which, k], abz_r.at[which, k], did(seg, x, nz),
        )

    def abx_more(k):
        return rcopy(
            ab.at[w, half_rows(k, 1 - zh)], ab.at[w, half_rows(k, 1 - zh)], abm_s.at[k], abm_r.at[k], did(seg, 3 - x, z)
        )

    def ab_split(which, rows):
        abhi[which, rows, :], ablo[which, rows, :] = split(ab[which, rows, :])

    def cx_copy(which, send, to):
        return rcopy(cown, cs.at[which], cx_s.at[send], cx_r.at[which], did(seg, to, z))

    @pl.when(end)
    def _():
        def x_wait(k, _):
            got(zin.at[1, piece(k)], zr.at[1, k])
            sphi[1 - ia, piece(k), :], splo[1 - ia, piece(k), :] = split(zin[1, piece(k), :])
            return 0

        lax.fori_loop(0, NC, x_wait, 0)
        for half in (zh, 1 - zh):
            part = pl.ds(pl.multiple_of(half * HALF, HALF), HALF)
            for core, dims in ((0, NT), (1, TN)):
                @pl.when(c == core)
                def _():
                    at = (part, slice(None)) if core == 0 else (slice(None), part)
                    p = dot(sphi[(0, *at)], sphi[1], dims)
                    p += dot(splo[(0, *at)], sphi[1], dims)
                    p += dot(sphi[(0, *at)], splo[1], dims)
                    px[part, :] = p

            if half is zh:
                @pl.when(outer)
                def _():
                    for k in range(NX):
                        x_copy(k).start()

        hi, lo = split(px[...])
        wxhi[...] = hi
        wxlo[...] = lo

        @pl.when(zh != c)
        def _():
            got(ch.at[zh], ch_r.at[zh])

        got(ch.at[1 - zh], ch_r.at[1 - zh])
        for core, dims in ((0, NT), (1, NN)):
            @pl.when(c == core)
            def _():
                cx[...] = mm3(ch[0], sphi[iv], splo[iv], dims) + ch[1]

        @pl.when(x == 0)
        def _():
            cown[...] = cx[...]
            cx_copy(0, 0, 1).start()

        @pl.when(x == 1)
        def _():
            got(cs.at[0], cx_r.at[0])
            cown[...] = mm3(cs[0], wxhi[...], wxlo[...]) + cx[...]
            cs[1] = cown[...]
            cx_copy(1, 0, 2).start()

        @pl.when(x == 2)
        def _():
            cown[...] = cx[...]
            cx_copy(2, 0, 3).start()

        @pl.when(x == 3)
        def _():
            got(cs.at[2], cx_r.at[2])
            cown[...] = mm3(cs[2], wxhi[...], wxlo[...], NT) + cx[...]
            cx_copy(3, 0, 2).start()
            cx_copy(3, 1, 1).start()

    @pl.when(end & jnp.logical_not(row))
    def _():
        lax.fori_loop(0, NP, p_start, 0)

    @pl.when(root)
    def _():
        def x_body(k, _):
            @pl.when(k < NX)
            def _():
                got(xin.at[half_rows(k, 0)], xr.at[k])
                v = mm3(xin[half_rows(k, 0), :], wxhi[...], wxlo[...])
                mine = half_rows(k, zh)
                ab[w, mine, :] = v
                abx_copy(k).start()
                abz_copy(k, w).start()
                abhi[w, mine, :], ablo[w, mine, :] = split(v)

            @pl.when(k >= LAG)
            def _():
                j = k - LAG
                got(ab.at[1 - w, half_rows(j, zh)], abx_r.at[j])

                @pl.when(j % 2 == 0)
                def _():
                    abz_copy(j, 1 - w).start()

                ab_split(1 - w, half_rows(j, zh))
                got(ab.at[w, half_rows(j, 1 - zh)], abz_r.at[w, j])

                @pl.when(j % 2 == 1)
                def _():
                    abx_more(j).start()

                ab_split(w, half_rows(j, 1 - zh))

            return 0

        lax.fori_loop(0, NX + LAG, x_body, 0)

        def ab_wait(k, _):
            @pl.when(k % 2 == 0)
            def _():
                got(ab.at[1 - w, half_rows(k, 1 - zh)], abz_r.at[1 - w, k])

            @pl.when(k % 2 == 1)
            def _():
                got(ab.at[1 - w, half_rows(k, 1 - zh)], abm_r.at[k])

            ab_split(1 - w, half_rows(k, 1 - zh))
            return 0

        lax.fori_loop(0, NX, ab_wait, 0)
        p = dot(abhi[0], abhi[1], NT)
        p += dot(ablo[0], abhi[1], NT)
        p += dot(abhi[0], ablo[1], NT)
        hi, lo = split(p)
        pfhi[...] = hi
        pflo[...] = lo

        @pl.when(x == 2)
        def _():
            got(cs.at[1], cx_r.at[1])

        got(cs.at[3], cx_r.at[3])
        cseg[...] = mm3(cs[1], abhi[1], ablo[1], NT) + cs[3]

    def x_sent():
        @pl.when(outer)
        def _():
            for k in range(NX):
                x_copy(k).wait_send()

            @pl.when(x == 0)
            def _():
                cx_copy(0, 0, 1).wait_send()

            @pl.when(x == 3)
            def _():
                cx_copy(3, 0, 2).wait_send()
                cx_copy(3, 1, 1).wait_send()

        @pl.when(root)
        def _():
            def ab_done(k, _):
                abx_copy(k).wait_send()
                abz_copy(k, w).wait_send()

                @pl.when(k % 2 == 0)
                def _():
                    abz_copy(k, 1 - w).wait_send()

                @pl.when(k % 2 == 1)
                def _():
                    abx_more(k).wait_send()

                return 0

            lax.fori_loop(0, NX, ab_done, 0)
            cx_copy(1, 0, 3).wait_send()

    m0 = jnp.concatenate([m0_ref[...], pad], axis=0)
    chained = root | (end & (x == 0))

    @pl.when(chained & first)
    def _():
        m_in[...] = m0

    @pl.when(chained & jnp.logical_not(first))
    def _():
        got(m_in, m_r)

    def m_copy(to, send):
        return rcopy(m_out, m_in, m_s.at[send], m_r, did(seg + 1, to, end_z(way(seg + 1), zh)))

    def f_copy(blk):
        return rcopy(f_out.at[blk], f_in.at[blk], f_s.at[blk], f_r.at[blk], did(seg + 1, x, end_z(way(seg + 1), zh)))

    def owner(blk):
        return jnp.where(blk < 4, x, xouter), zh * 4 + blk % 4

    def fb_copy(blk):
        ox, oz = owner(blk)
        return rcopy(f_out.at[blk], ends_ref.at[0], fb_s.at[blk], fb_r, did(seg, ox, oz))

    def ex_copy(to):
        return rcopy(e_out, e_x, ex_s, ex_r, did(seg, to, z))

    @pl.when(root)
    def _():
        @pl.when(jnp.logical_not(last))
        def _():
            m_out[...] = mm3(m_in[...], pfhi[...], pflo[...]) + cseg[...]
            m_copy(x, 0).start()

            @pl.when(x == 1)
            def _():
                m_copy(0, 1).start()


    def e_copy(k):
        return rcopy(e_half, e_in, e_s.at[k], e_r, did(seg, x, zh * 4 + (zi + k + 1) % 4))

    def go_down():
        @pl.when(root & (x == 2))
        def _():
            e_x[...] = mm3(m_in[...], abhi[0], ablo[0]) + cs[1]
            e_out[...] = mm3(e_x[...], wxhi[...], wxlo[...], NT) + cx[...]
            ex_copy(3).start()

        @pl.when(end & (x == 0))
        def _():
            e_out[...] = mm3(m_in[...], wxhi[...], wxlo[...]) + cx[...]
            ex_copy(1).start()
            e_x[...] = m_in[...]

        @pl.when(end & ((x == 1) | (x == 3)))
        def _():
            got(e_x, ex_r)

        @pl.when(end & (zh == 0))
        def _():
            e_half[...] = e_x[...]

        for core, dims in ((0, NN), (1, NT)):
            @pl.when(end & (zh == 1) & (c == core))
            def _():
                e_half[...] = mm3(e_x[...], sphi[1 - iv], splo[1 - iv], dims) + ch[0]

        @pl.when(end)
        def _():
            for k in range(3):
                e_copy(k).start()

        @pl.when(jnp.logical_not(end))
        def _():
            got(e_in, e_r)
            e_half[...] = e_in[...]

        @pl.when(zi > 0)
        def _():
            e_in[...] = mm3(e_half[...], inhi[...], inlo[...]) + cin[...]

        @pl.when(zi == 0)
        def _():
            e_in[...] = e_half[...]

        m1, m2 = two_steps(e_in[...])
        means_ref[0] = m1[:4]
        means_ref[1] = m2[:4]

    def f_home(blk):
        @pl.when(blk != block)
        def _():
            fb_copy(blk).start()

        @pl.when(blk == block)
        def _():
            ends_ref[0] = f_out[blk]

    def f_block(k):
        blk = jnp.where(k < 4, 4, 0) + jnp.where(zh == 0, k % 4, 3 - k % 4)

        @pl.when(first & (blk != block))
        def _():
            got(f_in.at[blk], f0_r.at[blk])

        @pl.when(jnp.logical_not(first))
        def _():
            got(f_in.at[blk], f_r.at[blk])

        f_out[blk] = mm3(f_in[blk], pfhi[...], pflo[...])

        @pl.when(jnp.logical_not(last))
        def _():
            f_copy(blk).start()

        @pl.when(last)
        def _():
            f_home(blk)

    down_turn = jnp.where(root, jnp.where(last, jnp.where(x == 2, 0, 6), 8), 0)

    def chain_body(k, _):
        pl.when(k == down_turn)(go_down)

        @pl.when(root & (k < 8))
        def _():
            f_block(k)

        return 0

    lax.fori_loop(0, jnp.where(root, 9, 1), chain_body, 0)

    @pl.when(root & jnp.logical_not(last))
    def _():
        for blk in range(8):
            f_home(blk)

    @pl.when(jnp.logical_not(root))
    def _():
        got(ends_ref.at[0], fb_r)

    def rest_sent():
        @pl.when(first & jnp.logical_not(root))
        def _():
            f0_copy().wait_send()

        @pl.when(root)
        def _():
            @pl.when(jnp.logical_not(last))
            def _():
                m_copy(x, 0).wait_send()

                @pl.when(x == 1)
                def _():
                    m_copy(0, 1).wait_send()

                for blk in range(8):
                    f_copy(blk).wait_send()

            for blk in range(8):
                @pl.when(blk != block)
                def _():
                    fb_copy(blk).wait_send()

        @pl.when(end & ((x == 0) | (x == 2)))
        def _():
            ex_copy(1).wait_send()

        @pl.when(end)
        def _():
            for k in range(3):
                e_copy(k).wait_send()

        @pl.when(jnp.logical_not(row) & (zi < 3))
        def _():
            lax.fori_loop(0, NP, p_done, 0)

    z_sent()
    x_sent()
    rest_sent()


def per_device(transition, obs_gain, observed, init_mean, init_factor):
    vm = pl.BlockSpec(memory_space=pltpu.VMEM)
    f, b = (lambda *s: pltpu.VMEM(s, F32)), (lambda *s: pltpu.VMEM(s, BF16))
    dma = lambda *s: pltpu.SemaphoreType.DMA(s) if s else pltpu.SemaphoreType.DMA
    scratch = [
        f(D, D), f(2, D, D), b(D, D), b(D, D), f(2, PAD, D), f(PAD, D), f(2, PAD, D), f(PAD, D),
        b(2, D, D), b(2, D, D), f(D, D), b(D, D), b(D, D), f(HALF, D), f(2, D, D), b(2, D, D), b(2, D, D), b(D, D), b(D, D),
        f(4, PAD, D), f(PAD, D), f(PAD, D), f(PAD, D), f(PAD, D), f(PAD, D), f(8, 16, D), f(8, 16, D), b(D, D), b(D, D),
        f(PAD, D), f(PAD, D), f(PAD, D), f(PAD, D), f(D, D),
        dma(NP), dma(NC), dma(2, NC), dma(), dma(), dma(2), dma(2), dma(NX), dma(NX), dma(NX), dma(NX), dma(NX), dma(NX), dma(2, NX), dma(2, NX),
        dma(2), dma(4), dma(2), dma(), dma(), dma(8), dma(8), dma(8), dma(8), dma(), dma(3), dma(), dma(), dma(),
    ]
    outs = pl.pallas_call(
        kernel,
        out_shape=(jax.ShapeDtypeStruct((2, 4, D), F32), jax.ShapeDtypeStruct((1, 16, D), F32)),
        in_specs=[vm] * 5,
        out_specs=(vm, vm),
        scratch_shapes=scratch,
        compiler_params=pltpu.CompilerParams(
            collective_id=0, has_side_effects=True, vmem_limit_bytes=56 * 2**20
        ),
        name="filter_flow",
    )(transition, obs_gain, observed, init_mean, init_factor)

    def hand_on(a_ref, b_ref, a_out, b_out):
        a_out[...] = a_ref[...]
        b_out[...] = b_ref[...]

    return pl.pallas_call(
        hand_on, out_shape=tuple(jax.ShapeDtypeStruct(o.shape, o.dtype) for o in outs), in_specs=[vm] * 2, out_specs=(vm, vm),
        name="hand_on",
    )(*outs)


def solution(mesh):
    placed = P(("seg", "tm"), None, None)
    return jax.shard_map(
        per_device,
        mesh=mesh,
        in_specs=(placed, placed, placed, P(), P("tm", None)),
        out_specs=(placed, P("seg", "tm", None)),
        check_vma=False,
    )
```

```python
import functools

import jax
import jax.numpy as jnp
from jax import lax
from jax.experimental import pallas as pl
from jax.experimental.pallas import tpu as pltpu
from jax.sharding import PartitionSpec as P

MESH = pl.DeviceIdType.MESH
F32, BF16 = jnp.float32, jnp.bfloat16
D = 512
HALF = D // 2
ROWS = 32
NC = D // ROWS
XROWS = 32
NX = HALF // XROWS
LAG = 6
WIDE = 128
NP = D // WIDE
PAD = 8

NN = (((1,), (0,)), ((), ()))
NT = (((1,), (1,)), ((), ()))
TN = (((0,), (0,)), ((), ()))
TT = (((0,), (1,)), ((), ()))


def dot(a, b, dims=NN):
    return lax.dot_general(a, b, dims, preferred_element_type=F32)


def split(a):
    hi = a.astype(BF16)
    return hi, (a - hi.astype(F32)).astype(BF16)


def mm3(a, hi, lo, dims=NN):
    ah, al = split(a)
    n = a.shape[0]
    both = dot(jnp.concatenate([ah, al], axis=0), hi, dims)
    return both[:n] + both[n:] + dot(ah, lo, dims)


def mm2(a, exact):
    ah, al = split(a)
    n = a.shape[0]
    both = dot(jnp.concatenate([ah, al], axis=0), exact)
    return both[:n] + both[n:]


def kernel(
    t_ref, g_ref, o_ref, m0_ref, f0_ref, means_ref, ends_ref,
    zout, zin, whi, wlo, drv, cin, ch, csend,
    sphi, splo, px, wxhi, wxlo, xin, ab, abhi, ablo, pfhi, pflo,
    cs, cx, cseg, cown, m_in, m_out, f_in, f_out, inhi, inlo, e_in, e_out, e_half, e_x, pout,
    map_s, map_r, const_s, const_r, ps, zs, zr, cs_s, cs_r, ch_s, ch_r, xs, xr, abx_s, abx_r, abm_s, abm_r, abz_s, abz_r,
    cx_s, cx_r, m_s, m_r, f0_s, f0_r, f_s, f_r, fb_s, fb_r, e_s, e_r, ex_s, ex_r,
):
    seg = lax.axis_index("seg")
    tm = lax.axis_index("tm")

    def way(s):
        return jnp.where(s < 6, s + s // 2, s) % 2

    c = way(seg)
    x, z = tm // 8, tm % 8
    zh, zi = z // 4, z % 4
    row = zh == c
    pos = jnp.where(row, zi, 3 - zi)
    nz = jnp.where(row, (z + 1) % 8, (z + 7) % 8)
    end = pos == 3
    inner = (x == 1) | (x == 2)
    root = end & inner
    outer = end & jnp.logical_not(inner)
    first, last = seg == 0, seg == 7
    xroot = jnp.where(x < 2, 1, 2)
    xouter = jnp.where(x < 2, 0, 3)

    def end_z(core, half):
        return jnp.where(core == 0, 3 + half, 7 * half)

    def did(s, xx, zz):
        return (s, xx * 8 + zz)

    myend = end_z(c, zh)

    def moved(s):
        return (s == 5) | (s == 7)

    def worker_z(s):
        return end_z(jnp.where(moved(s), 0, way(s)), zh)

    worker = inner & (z == worker_z(seg))
    guest = worker & moved(seg)
    host = root & moved(seg)

    def rcopy(src, dst, ssem, rsem, dev):
        return pltpu.make_async_remote_copy(
            src_ref=src, dst_ref=dst, send_sem=ssem, recv_sem=rsem, device_id=dev, device_id_type=MESH
        )

    def got(dst, rsem):
        rcopy(dst, dst, rsem, rsem, did(seg, x, nz)).wait_recv()

    barrier = pltpu.get_barrier_semaphore()

    def greet(dev):
        pl.semaphore_signal(barrier, inc=1, device_id=dev, device_id_type=MESH)

    pz = jnp.where(row, z - 1, z + 1)

    @pl.when(pos < 3)
    def _():
        greet(did(seg, x, myend))

    @pl.when((pos < 2) | end)
    def _():
        greet(did(seg, x, nz))

    @pl.when((pos == 1) | (pos == 2))
    def _():
        greet(did(seg, x, pz))

    @pl.when((pos == 0) & jnp.logical_not(row))
    def _():
        greet(did(seg, x, end_z(c, 1 - zh)))

    @pl.when(end)
    def _():
        for k in range(1, 4):
            greet(did(seg, x, zh * 4 + (zi + k) % 4))

        @pl.when(row)
        def _():
            greet(did(seg, x, (1 - zh) * 4 + 3))

    for here, others in ((0, (1,)), (1, (0, 2, 3)), (2, (1, 3)), (3, (2, 1))):
        @pl.when(end & (x == here))
        def _():
            for k in others:
                greet(did(seg, k, z))

    @pl.when(jnp.logical_not(inner))
    def _():
        greet(did(seg, xroot, myend))

        @pl.when(moved(seg))
        def _():
            greet(did(seg, xroot, worker_z(seg)))

    @pl.when(root | guest)
    def _():
        for k in range(4):
            greet(did(seg, xouter, zh * 4 + k))

    middle = inner & moved(seg) & ((pos == 1) | (pos == 2))

    @pl.when(middle)
    def _():
        greet(did(seg, x, worker_z(seg)))

    @pl.when(guest)
    def _():
        for k in (1, 2):
            greet(did(seg, x, jnp.where(row, z + k, z - k)))

    @pl.when(worker & jnp.logical_not(last))
    def _():
        greet(did(seg + 1, x, worker_z(seg + 1)))

        @pl.when(moved(seg + 1))
        def _():
            greet(did(seg + 1, x, end_z(way(seg + 1), zh)))

        @pl.when(x == 1)
        def _():
            greet(did(seg + 1, 0, end_z(way(seg + 1), zh)))

    @pl.when((worker | host) & jnp.logical_not(first))
    def _():
        greet(did(seg - 1, x, worker_z(seg - 1)))

    @pl.when(end & (x == 0) & jnp.logical_not(first))
    def _():
        greet(did(seg - 1, 1, worker_z(seg - 1)))

    one = lambda p: jnp.where(p, 1, 0)
    greets = (
        one(pos < 3) + one((pos < 2) | end) + one((pos == 1) | (pos == 2)) + one((pos == 0) & jnp.logical_not(row))
        + one(end) * (3 + one(row) + jnp.where(x == 0, 1, jnp.where(x == 1, 3, 2))) + one(jnp.logical_not(inner))
        + one(jnp.logical_not(inner) & moved(seg)) + 4 * one(root | guest) + one(middle) + 2 * one(guest)
        + one(worker & jnp.logical_not(last)) * (1 + one(moved(seg + 1)) + one(x == 1))
        + one((worker | host) & jnp.logical_not(first)) + one(end & (x == 0) & jnp.logical_not(first))
    )

    def put_map(m):
        @pl.when(pos == 0)
        def _():
            zout[...] = m

        @pl.when(pos > 0)
        def _():
            hi, lo = split(m)
            whi[...] = hi
            wlo[...] = lo

    @pl.when(row)
    def _():
        put_map(dot(t_ref[0], t_ref[1]))

    @pl.when(jnp.logical_not(row))
    def _():
        put_map(dot(t_ref[1], t_ref[0], TT))

        @pl.when(end)
        def _():
            pout[...] = dot(t_ref[0], t_ref[1])

    pad = jnp.zeros((PAD - 4, D), F32)
    for s in range(2):
        drv[s] = jnp.concatenate([dot(o_ref[s], g_ref[s]), pad], axis=0)

    @pl.when(zi == 0)
    def _():
        cin[...] = jnp.zeros_like(cin)

    pl.semaphore_wait(barrier, greets)

    block = jnp.where(x == xroot, 0, 4) + zi

    def f0_copy():
        return rcopy(f0_ref, f_in.at[block], f0_s, f0_r.at[block], did(seg, xroot, myend))

    @pl.when(first & jnp.logical_not(root))
    def _():
        f0_copy().start()

    @pl.when(first & root)
    def _():
        f_in[block] = f0_ref[...]

    def two_steps(m):
        m1 = mm2(m, t_ref[0]) + drv[0]
        return m1, mm2(m1, t_ref[1]) + drv[1]

    def c_next():
        return rcopy(csend, cin, cs_s, cs_r, did(seg, x, (z + 1) % 8))

    def c_end(half):
        return rcopy(csend, ch.at[zh], ch_s.at[half], ch_r.at[zh], did(seg, x, end_z(c, half)))

    def c_step():
        @pl.when(zi > 0)
        def _():
            got(cin, cs_r)

        csend[...] = two_steps(cin[...])[1]

        @pl.when(zi < 3)
        def _():
            c_next().start()

        @pl.when(zi == 3)
        def _():
            for half in range(2):
                away = end_z(c, half) != z

                @pl.when(away)
                def _():
                    c_end(half).start()

                @pl.when(jnp.logical_not(away))
                def _():
                    ch[zh] = csend[...]

    turn = jnp.where(row, 0, jnp.where(pos == 1, NC // 2, jnp.where(pos == 0, NC, 0)))
    slot = jnp.where(end, 1, 0)

    def piece(k):
        return pl.ds(pl.multiple_of(k * ROWS, ROWS), ROWS)

    def z_copy(k):
        return rcopy(
            zout.at[piece(k)], zin.at[slot, piece(k)], zs.at[k], zr.at[slot, k], did(seg, x, nz)
        )

    ia = jnp.where((zh == 0) == (x < 2), 0, 1)

    def z_body(k, _):
        pl.when(k == turn)(c_step)

        @pl.when(k < NC)
        def _():
            @pl.when(pos > 0)
            def _():
                got(zin.at[0, piece(k)], zr.at[0, k])
                v = mm3(zin[0, piece(k), :], whi[...], wlo[...])
                zout[piece(k), :] = v

                @pl.when(end)
                def _():
                    sphi[ia, piece(k), :], splo[ia, piece(k), :] = split(v)


            z_copy(k).start()

        return 0

    lax.fori_loop(0, NC + 1, z_body, 0)

    def z_sent():
        def z_done(k, _):
            z_copy(k).wait_send()
            return 0

        lax.fori_loop(0, NC, z_done, 0)

        @pl.when(zi < 3)
        def _():
            c_next().wait_send()

        @pl.when(zi == 3)
        def _():
            for half in range(2):
                @pl.when(end_z(c, half) != z)
                def _():
                    c_end(half).wait_send()

    def wide(k):
        return pl.ds(pl.multiple_of(k * WIDE, WIDE), WIDE)

    def p_copy(k):
        return rcopy(pout.at[wide(k)], zin.at[1, wide(k)], ps.at[k], zr.at[1, k], did(seg, x, z + 1))

    def p_body(k, _):
        got(zin.at[1, wide(k)], zr.at[1, k])

        @pl.when(zi < 3)
        def _():
            pout[wide(k), :] = mm3(zin[1, wide(k), :], whi[...], wlo[...], NT)
            p_copy(k).start()

        return 0

    def p_start(k, _):
        p_copy(k).start()
        return 0

    def p_done(k, _):
        p_copy(k).wait_send()
        return 0

    @pl.when(jnp.logical_not(row | end))
    def _():
        lax.fori_loop(0, NP, p_body, 0)

    @pl.when(zi > 0)
    def _():
        hi, lo = split(zin[jnp.where(row, 0, 1)])
        inhi[...] = hi
        inlo[...] = lo

    iv = jnp.where(x < 2, 1, 0)
    w = jnp.where(x == 1, 0, 1)

    def half_rows(k, half):
        return pl.ds(pl.multiple_of(half * HALF + k * XROWS, XROWS), XROWS)

    def x_copy(k):
        return rcopy(px.at[half_rows(k, zh)], xin.at[half_rows(k, 0)], xs.at[k], xr.at[k], did(seg, xroot, z))

    def abx_copy(k):
        return rcopy(
            ab.at[w, half_rows(k, zh)], ab.at[w, half_rows(k, zh)], abx_s.at[k], abx_r.at[k], did(seg, 3 - x, z)
        )

    def abz_copy(k, which):
        return rcopy(
            ab.at[which, half_rows(k, zh)], ab.at[which, half_rows(k, zh)],
            abz_s.at[which, k], abz_r.at[which, k], did(seg, x, nz),
        )

    def abx_more(k):
        return rcopy(
            ab.at[w, half_rows(k, 1 - zh)], ab.at[w, half_rows(k, 1 - zh)], abm_s.at[k], abm_r.at[k], did(seg, 3 - x, z)
        )

    def map_copy(k):
        return rcopy(px.at[wide(k)], zin.at[0, wide(k)], map_s.at[k], map_r.at[k], did(seg, x, worker_z(seg)))

    def const_copy():
        return rcopy(cseg, cseg, const_s, const_r, did(seg, x, worker_z(seg)))

    def ab_split(which, rows):
        abhi[which, rows, :], ablo[which, rows, :] = split(ab[which, rows, :])

    def cx_copy(which, send, to):
        return rcopy(cown, cs.at[which], cx_s.at[send], cx_r.at[which], did(seg, to, z))

    @pl.when(end)
    def _():
        def x_wait(k, _):
            got(zin.at[1, piece(k)], zr.at[1, k])
            sphi[1 - ia, piece(k), :], splo[1 - ia, piece(k), :] = split(zin[1, piece(k), :])
            return 0

        lax.fori_loop(0, NC, x_wait, 0)
        for half in (zh, 1 - zh):
            part = pl.ds(pl.multiple_of(half * HALF, HALF), HALF)
            for core, dims in ((0, NT), (1, TN)):
                @pl.when(c == core)
                def _():
                    at = (part, slice(None)) if core == 0 else (slice(None), part)
                    p = dot(sphi[(0, *at)], sphi[1], dims)
                    p += dot(splo[(0, *at)], sphi[1], dims)
                    p += dot(sphi[(0, *at)], splo[1], dims)
                    px[part, :] = p

            if half is zh:
                @pl.when(outer)
                def _():
                    for k in range(NX):
                        x_copy(k).start()

        hi, lo = split(px[...])
        wxhi[...] = hi
        wxlo[...] = lo

        @pl.when(zh != c)
        def _():
            got(ch.at[zh], ch_r.at[zh])

        got(ch.at[1 - zh], ch_r.at[1 - zh])
        for core, dims in ((0, NT), (1, NN)):
            @pl.when(c == core)
            def _():
                cx[...] = mm3(ch[0], sphi[iv], splo[iv], dims) + ch[1]

        @pl.when(x == 0)
        def _():
            cown[...] = cx[...]
            cx_copy(0, 0, 1).start()

        @pl.when(x == 1)
        def _():
            got(cs.at[0], cx_r.at[0])
            cown[...] = mm3(cs[0], wxhi[...], wxlo[...]) + cx[...]
            cs[1] = cown[...]
            cx_copy(1, 0, 2).start()

        @pl.when(x == 2)
        def _():
            cown[...] = cx[...]
            cx_copy(2, 0, 3).start()

        @pl.when(x == 3)
        def _():
            got(cs.at[2], cx_r.at[2])
            cown[...] = mm3(cs[2], wxhi[...], wxlo[...], NT) + cx[...]
            cx_copy(3, 0, 2).start()
            cx_copy(3, 1, 1).start()

    @pl.when(end & jnp.logical_not(row))
    def _():
        lax.fori_loop(0, NP, p_start, 0)

    @pl.when(root)
    def _():
        def x_body(k, _):
            @pl.when(k < NX)
            def _():
                got(xin.at[half_rows(k, 0)], xr.at[k])
                v = mm3(xin[half_rows(k, 0), :], wxhi[...], wxlo[...])
                mine = half_rows(k, zh)
                ab[w, mine, :] = v
                abx_copy(k).start()
                abz_copy(k, w).start()
                abhi[w, mine, :], ablo[w, mine, :] = split(v)

            @pl.when(k >= LAG)
            def _():
                j = k - LAG
                got(ab.at[1 - w, half_rows(j, zh)], abx_r.at[j])

                @pl.when(j % 2 == 0)
                def _():
                    abz_copy(j, 1 - w).start()

                ab_split(1 - w, half_rows(j, zh))
                got(ab.at[w, half_rows(j, 1 - zh)], abz_r.at[w, j])

                @pl.when(j % 2 == 1)
                def _():
                    abx_more(j).start()

                ab_split(w, half_rows(j, 1 - zh))

            return 0

        lax.fori_loop(0, NX + LAG, x_body, 0)

        def ab_wait(k, _):
            @pl.when(k % 2 == 0)
            def _():
                got(ab.at[1 - w, half_rows(k, 1 - zh)], abz_r.at[1 - w, k])

            @pl.when(k % 2 == 1)
            def _():
                got(ab.at[1 - w, half_rows(k, 1 - zh)], abm_r.at[k])

            ab_split(1 - w, half_rows(k, 1 - zh))
            return 0

        lax.fori_loop(0, NX, ab_wait, 0)
        p = dot(abhi[0], abhi[1], NT)
        p += dot(ablo[0], abhi[1], NT)
        p += dot(abhi[0], ablo[1], NT)

        @pl.when(host)
        def _():
            px[...] = p
            for k in range(NP):
                map_copy(k).start()

        hi, lo = split(p)
        pfhi[...] = hi
        pflo[...] = lo

        @pl.when(x == 2)
        def _():
            got(cs.at[1], cx_r.at[1])

        got(cs.at[3], cx_r.at[3])
        cseg[...] = mm3(cs[1], abhi[1], ablo[1], NT) + cs[3]

        @pl.when(host)
        def _():
            const_copy().start()

    @pl.when(guest)
    def _():
        def map_got(k, _):
            got(zin.at[0, wide(k)], map_r.at[k])
            pfhi[wide(k), :], pflo[wide(k), :] = split(zin[0, wide(k), :])
            return 0

        lax.fori_loop(0, NP, map_got, 0)
        got(cseg, const_r)

    def x_sent():
        @pl.when(outer)
        def _():
            for k in range(NX):
                x_copy(k).wait_send()

            @pl.when(x == 0)
            def _():
                cx_copy(0, 0, 1).wait_send()

            @pl.when(x == 3)
            def _():
                cx_copy(3, 0, 2).wait_send()
                cx_copy(3, 1, 1).wait_send()

        @pl.when(root)
        def _():
            def ab_done(k, _):
                abx_copy(k).wait_send()
                abz_copy(k, w).wait_send()

                @pl.when(k % 2 == 0)
                def _():
                    abz_copy(k, 1 - w).wait_send()

                @pl.when(k % 2 == 1)
                def _():
                    abx_more(k).wait_send()

                return 0

            lax.fori_loop(0, NX, ab_done, 0)
            cx_copy(1, 0, 3).wait_send()

    m0 = jnp.concatenate([m0_ref[...], pad], axis=0)
    chained = root | guest | (end & (x == 0))

    @pl.when(chained & first)
    def _():
        m_in[...] = m0

    @pl.when(chained & jnp.logical_not(first))
    def _():
        got(m_in, m_r)

    def m_copy(send):
        to = jnp.where(send == 1, 0, x)
        at = jnp.where(send == 0, worker_z(seg + 1), end_z(way(seg + 1), zh))
        return rcopy(m_out, m_in, m_s.at[send], m_r, did(seg + 1, to, at))

    def f_copy(blk):
        return rcopy(f_out.at[blk], f_in.at[blk], f_s.at[blk], f_r.at[blk], did(seg + 1, x, worker_z(seg + 1)))

    def owner(blk):
        return jnp.where(blk < 4, x, xouter), zh * 4 + blk % 4

    def fb_copy(blk):
        ox, oz = owner(blk)
        return rcopy(f_out.at[blk], ends_ref.at[0], fb_s.at[blk], fb_r, did(seg, ox, oz))

    def ex_copy(to):
        return rcopy(e_out, e_x, ex_s, ex_r, did(seg, to, z))

    @pl.when(worker & jnp.logical_not(last))
    def _():
        m_out[...] = mm3(m_in[...], pfhi[...], pflo[...]) + cseg[...]
        m_copy(0).start()

        @pl.when(x == 1)
        def _():
            m_copy(1).start()

        @pl.when(moved(seg + 1))
        def _():
            m_copy(2).start()


    def e_copy(k):
        return rcopy(e_half, e_in, e_s.at[k], e_r, did(seg, x, zh * 4 + (zi + k + 1) % 4))

    def go_down():
        @pl.when(root & (x == 2))
        def _():
            e_x[...] = mm3(m_in[...], abhi[0], ablo[0]) + cs[1]
            e_out[...] = mm3(e_x[...], wxhi[...], wxlo[...], NT) + cx[...]
            ex_copy(3).start()

        @pl.when(end & (x == 0))
        def _():
            e_out[...] = mm3(m_in[...], wxhi[...], wxlo[...]) + cx[...]
            ex_copy(1).start()
            e_x[...] = m_in[...]

        @pl.when(end & ((x == 1) | (x == 3)))
        def _():
            got(e_x, ex_r)

        @pl.when(end & (zh == 0))
        def _():
            e_half[...] = e_x[...]

        for core, dims in ((0, NN), (1, NT)):
            @pl.when(end & (zh == 1) & (c == core))
            def _():
                e_half[...] = mm3(e_x[...], sphi[1 - iv], splo[1 - iv], dims) + ch[0]

        @pl.when(end)
        def _():
            for k in range(3):
                e_copy(k).start()

        @pl.when(jnp.logical_not(end))
        def _():
            got(e_in, e_r)
            e_half[...] = e_in[...]

        @pl.when(zi > 0)
        def _():
            e_in[...] = mm3(e_half[...], inhi[...], inlo[...]) + cin[...]

        @pl.when(zi == 0)
        def _():
            e_in[...] = e_half[...]

        m1, m2 = two_steps(e_in[...])
        means_ref[0] = m1[:4]
        means_ref[1] = m2[:4]

    def f_home(blk):
        @pl.when(blk != block)
        def _():
            fb_copy(blk).start()

        @pl.when(blk == block)
        def _():
            ends_ref[0] = f_out[blk]

    def f_block(k):
        blk = jnp.where(k < 4, 4, 0) + jnp.where(zh == 0, k % 4, 3 - k % 4)

        @pl.when(first & (blk != block))
        def _():
            got(f_in.at[blk], f0_r.at[blk])

        @pl.when(jnp.logical_not(first))
        def _():
            got(f_in.at[blk], f_r.at[blk])

        f_out[blk] = mm3(f_in[blk], pfhi[...], pflo[...])

        @pl.when(jnp.logical_not(last))
        def _():
            f_copy(blk).start()

        @pl.when(last)
        def _():
            f_home(blk)

    down_turn = jnp.where(worker, 8, 0)

    def chain_body(k, _):
        pl.when(k == down_turn)(go_down)

        @pl.when(worker & (k < 8))
        def _():
            f_block(k)

        return 0

    lax.fori_loop(0, jnp.where(worker, 9, 1), chain_body, 0)

    @pl.when(worker & jnp.logical_not(last))
    def _():
        for blk in range(8):
            f_home(blk)

    @pl.when(jnp.logical_not(worker))
    def _():
        got(ends_ref.at[0], fb_r)

    def rest_sent():
        @pl.when(first & jnp.logical_not(root))
        def _():
            f0_copy().wait_send()

        @pl.when(worker)
        def _():
            @pl.when(jnp.logical_not(last))
            def _():
                m_copy(0).wait_send()

                @pl.when(x == 1)
                def _():
                    m_copy(1).wait_send()

                @pl.when(moved(seg + 1))
                def _():
                    m_copy(2).wait_send()

                for blk in range(8):
                    f_copy(blk).wait_send()

            for blk in range(8):
                @pl.when(blk != block)
                def _():
                    fb_copy(blk).wait_send()

        @pl.when(end & ((x == 0) | (x == 2)))
        def _():
            ex_copy(1).wait_send()

        @pl.when(end)
        def _():
            for k in range(3):
                e_copy(k).wait_send()

        @pl.when(jnp.logical_not(row) & (zi < 3))
        def _():
            lax.fori_loop(0, NP, p_done, 0)

        @pl.when(host)
        def _():
            const_copy().wait_send()
            for k in range(NP):
                map_copy(k).wait_send()

    z_sent()
    x_sent()
    rest_sent()


def per_device(transition, obs_gain, observed, init_mean, init_factor):
    vm = pl.BlockSpec(memory_space=pltpu.VMEM)
    f, b = (lambda *s: pltpu.VMEM(s, F32)), (lambda *s: pltpu.VMEM(s, BF16))
    dma = lambda *s: pltpu.SemaphoreType.DMA(s) if s else pltpu.SemaphoreType.DMA
    scratch = [
        f(D, D), f(2, D, D), b(D, D), b(D, D), f(2, PAD, D), f(PAD, D), f(2, PAD, D), f(PAD, D),
        b(2, D, D), b(2, D, D), f(D, D), b(D, D), b(D, D), f(HALF, D), f(2, D, D), b(2, D, D), b(2, D, D), b(D, D), b(D, D),
        f(4, PAD, D), f(PAD, D), f(PAD, D), f(PAD, D), f(PAD, D), f(PAD, D), f(8, 16, D), f(8, 16, D), b(D, D), b(D, D),
        f(PAD, D), f(PAD, D), f(PAD, D), f(PAD, D), f(D, D),
        dma(NP), dma(NP), dma(), dma(), dma(NP), dma(NC), dma(2, NC), dma(), dma(), dma(2), dma(2), dma(NX), dma(NX), dma(NX), dma(NX), dma(NX), dma(NX), dma(2, NX), dma(2, NX),
        dma(2), dma(4), dma(3), dma(), dma(), dma(8), dma(8), dma(8), dma(8), dma(), dma(3), dma(), dma(), dma(),
    ]
    outs = pl.pallas_call(
        kernel,
        out_shape=(jax.ShapeDtypeStruct((2, 4, D), F32), jax.ShapeDtypeStruct((1, 16, D), F32)),
        in_specs=[vm] * 5,
        out_specs=(vm, vm),
        scratch_shapes=scratch,
        compiler_params=pltpu.CompilerParams(
            collective_id=0, has_side_effects=True, vmem_limit_bytes=56 * 2**20
        ),
        name="filter_flow",
    )(transition, obs_gain, observed, init_mean, init_factor)

    def hand_on(a_ref, b_ref, a_out, b_out):
        a_out[...] = a_ref[...]
        b_out[...] = b_ref[...]

    return pl.pallas_call(
        hand_on, out_shape=tuple(jax.ShapeDtypeStruct(o.shape, o.dtype) for o in outs), in_specs=[vm] * 2, out_specs=(vm, vm),
        name="hand_on",
    )(*outs)


def solution(mesh):
    placed = P(("seg", "tm"), None, None)
    return jax.shard_map(
        per_device,
        mesh=mesh,
        in_specs=(placed, placed, placed, P(), P("tm", None)),
        out_specs=(placed, P("seg", "tm", None)),
        check_vma=False,
    )
```

```python
import functools

import jax
import jax.numpy as jnp
from jax import lax
from jax.experimental import pallas as pl
from jax.experimental.pallas import tpu as pltpu
from jax.sharding import PartitionSpec as P

MESH = pl.DeviceIdType.MESH
F32, BF16 = jnp.float32, jnp.bfloat16
D = 512
HALF = D // 2
ROWS = 32
NC = D // ROWS
XROWS = 32
NX = HALF // XROWS
LAG = 6
WIDE = 128
NP = D // WIDE
PAD = 8

NN = (((1,), (0,)), ((), ()))
NT = (((1,), (1,)), ((), ()))
TN = (((0,), (0,)), ((), ()))
TT = (((0,), (1,)), ((), ()))


def dot(a, b, dims=NN):
    return lax.dot_general(a, b, dims, preferred_element_type=F32)


def split(a):
    hi = a.astype(BF16)
    return hi, (a - hi.astype(F32)).astype(BF16)


def mm3(a, hi, lo, dims=NN):
    ah, al = split(a)
    n = a.shape[0]
    both = dot(jnp.concatenate([ah, al], axis=0), hi, dims)
    return both[:n] + both[n:] + dot(ah, lo, dims)


def mm2(a, exact):
    ah, al = split(a)
    n = a.shape[0]
    both = dot(jnp.concatenate([ah, al], axis=0), exact)
    return both[:n] + both[n:]


def kernel(
    t_ref, g_ref, o_ref, m0_ref, f0_ref, means_ref, ends_ref,
    zout, zin, whi, wlo, drv, cin, ch, csend,
    sphi, splo, px, wxhi, wxlo, xin, ab, abhi, ablo, pfhi, pflo,
    cs, cx, cseg, cown, m_in, m_out, f_in, f_out, inhi, inlo, e_in, e_out, e_half, e_x, pout,
    map_s, map_r, const_s, const_r, ps, zs, zr, cs_s, cs_r, ch_s, ch_r, xs, xr, abx_s, abx_r, abm_s, abm_r, abz_s, abz_r,
    cx_s, cx_r, m_s, m_r, f0_s, f0_r, f_s, f_r, fb_s, fb_r, e_s, e_r, ex_s, ex_r,
):
    seg = lax.axis_index("seg")
    tm = lax.axis_index("tm")

    def way(s):
        return jnp.where(s < 6, s + s // 2, s) % 2

    c = way(seg)
    x, z = tm // 8, tm % 8
    zh, zi = z // 4, z % 4
    row = zh == c
    pos = jnp.where(row, zi, 3 - zi)
    nz = jnp.where(row, (z + 1) % 8, (z + 7) % 8)
    end = pos == 3
    inner = (x == 1) | (x == 2)
    root = end & inner
    outer = end & jnp.logical_not(inner)
    first, last = seg == 0, seg == 7
    xroot = jnp.where(x < 2, 1, 2)
    xouter = jnp.where(x < 2, 0, 3)

    def end_z(core, half):
        return jnp.where(core == 0, 3 + half, 7 * half)

    def did(s, xx, zz):
        return (s, xx * 8 + zz)

    myend = end_z(c, zh)

    def moved(s):
        return (s == 5) | (s == 7)

    def worker_z(s):
        return end_z(jnp.where(moved(s), 0, way(s)), zh)

    worker = inner & (z == worker_z(seg))
    guest = worker & moved(seg)
    host = root & moved(seg)

    def rcopy(src, dst, ssem, rsem, dev):
        return pltpu.make_async_remote_copy(
            src_ref=src, dst_ref=dst, send_sem=ssem, recv_sem=rsem, device_id=dev, device_id_type=MESH
        )

    def got(dst, rsem):
        rcopy(dst, dst, rsem, rsem, did(seg, x, nz)).wait_recv()

    barrier = pltpu.get_barrier_semaphore()

    def greet(dev):
        pl.semaphore_signal(barrier, inc=1, device_id=dev, device_id_type=MESH)

    pz = jnp.where(row, z - 1, z + 1)

    @pl.when(pos < 3)
    def _():
        greet(did(seg, x, myend))

    @pl.when((pos < 2) | end)
    def _():
        greet(did(seg, x, nz))

    @pl.when((pos == 1) | (pos == 2))
    def _():
        greet(did(seg, x, pz))

    @pl.when((pos == 0) & jnp.logical_not(row))
    def _():
        greet(did(seg, x, end_z(c, 1 - zh)))

    @pl.when(end)
    def _():
        for k in range(1, 4):
            greet(did(seg, x, zh * 4 + (zi + k) % 4))

        @pl.when(row)
        def _():
            greet(did(seg, x, (1 - zh) * 4 + 3))

    for here, others in ((0, (1,)), (1, (0, 2, 3)), (2, (1, 3)), (3, (2, 1))):
        @pl.when(end & (x == here))
        def _():
            for k in others:
                greet(did(seg, k, z))

    @pl.when(jnp.logical_not(inner))
    def _():
        greet(did(seg, xroot, myend))

        @pl.when(moved(seg))
        def _():
            greet(did(seg, xroot, worker_z(seg)))

    @pl.when(root | guest)
    def _():
        for k in range(4):
            greet(did(seg, xouter, zh * 4 + k))

    middle = inner & moved(seg) & ((pos == 1) | (pos == 2))

    @pl.when(middle)
    def _():
        greet(did(seg, x, worker_z(seg)))

    @pl.when(guest)
    def _():
        for k in (1, 2):
            greet(did(seg, x, jnp.where(row, z + k, z - k)))

    @pl.when(worker & jnp.logical_not(last))
    def _():
        greet(did(seg + 1, x, worker_z(seg + 1)))

        @pl.when(moved(seg + 1))
        def _():
            greet(did(seg + 1, x, end_z(way(seg + 1), zh)))

        @pl.when(x == 1)
        def _():
            greet(did(seg + 1, 0, end_z(way(seg + 1), zh)))

    @pl.when((worker | host) & jnp.logical_not(first))
    def _():
        greet(did(seg - 1, x, worker_z(seg - 1)))

    @pl.when(end & (x == 0) & jnp.logical_not(first))
    def _():
        greet(did(seg - 1, 1, worker_z(seg - 1)))

    one = lambda p: jnp.where(p, 1, 0)
    greets = (
        one(pos < 3) + one((pos < 2) | end) + one((pos == 1) | (pos == 2)) + one((pos == 0) & jnp.logical_not(row))
        + one(end) * (3 + one(row) + jnp.where(x == 0, 1, jnp.where(x == 1, 3, 2))) + one(jnp.logical_not(inner))
        + one(jnp.logical_not(inner) & moved(seg)) + 4 * one(root | guest) + one(middle) + 2 * one(guest)
        + one(worker & jnp.logical_not(last)) * (1 + one(moved(seg + 1)) + one(x == 1))
        + one((worker | host) & jnp.logical_not(first)) + one(end & (x == 0) & jnp.logical_not(first))
    )

    def put_map(m):
        @pl.when(pos == 0)
        def _():
            zout[...] = m

        @pl.when(pos > 0)
        def _():
            hi, lo = split(m)
            whi[...] = hi
            wlo[...] = lo

    @pl.when(row)
    def _():
        put_map(dot(t_ref[0], t_ref[1]))

    @pl.when(jnp.logical_not(row))
    def _():
        put_map(dot(t_ref[1], t_ref[0], TT))

        @pl.when(end)
        def _():
            pout[...] = dot(t_ref[0], t_ref[1])

    pad = jnp.zeros((PAD - 4, D), F32)
    for s in range(2):
        drv[s] = jnp.concatenate([dot(o_ref[s], g_ref[s]), pad], axis=0)

    @pl.when(zi == 0)
    def _():
        cin[...] = jnp.zeros_like(cin)

    pl.semaphore_wait(barrier, greets)

    block = jnp.where(x == xroot, 0, 4) + zi

    def f0_copy():
        return rcopy(f0_ref, f_in.at[block], f0_s, f0_r.at[block], did(seg, xroot, myend))

    @pl.when(first & jnp.logical_not(root))
    def _():
        f0_copy().start()

    @pl.when(first & root)
    def _():
        f_in[block] = f0_ref[...]

    def two_steps(m):
        m1 = mm2(m, t_ref[0]) + drv[0]
        return m1, mm2(m1, t_ref[1]) + drv[1]

    def c_next():
        return rcopy(csend, cin, cs_s, cs_r, did(seg, x, (z + 1) % 8))

    def c_end(half):
        return rcopy(csend, ch.at[zh], ch_s.at[half], ch_r.at[zh], did(seg, x, end_z(c, half)))

    def c_step():
        @pl.when(zi > 0)
        def _():
            got(cin, cs_r)

        csend[...] = two_steps(cin[...])[1]

        @pl.when(zi < 3)
        def _():
            c_next().start()

        @pl.when(zi == 3)
        def _():
            for half in range(2):
                away = end_z(c, half) != z

                @pl.when(away)
                def _():
                    c_end(half).start()

                @pl.when(jnp.logical_not(away))
                def _():
                    ch[zh] = csend[...]

    turn = jnp.where(row, 0, jnp.where(pos == 1, NC // 2, jnp.where(pos == 0, NC, 0)))
    slot = jnp.where(end, 1, 0)

    def piece(k):
        return pl.ds(pl.multiple_of(k * ROWS, ROWS), ROWS)

    def z_copy(k):
        return rcopy(
            zout.at[piece(k)], zin.at[slot, piece(k)], zs.at[k], zr.at[slot, k], did(seg, x, nz)
        )

    ia = jnp.where((zh == 0) == (x < 2), 0, 1)

    def z_body(k, _):
        pl.when(k == turn)(c_step)

        @pl.when(k < NC)
        def _():
            @pl.when(pos > 0)
            def _():
                got(zin.at[0, piece(k)], zr.at[0, k])
                v = mm3(zin[0, piece(k), :], whi[...], wlo[...])
                zout[piece(k), :] = v

                @pl.when(end)
                def _():
                    sphi[ia, piece(k), :], splo[ia, piece(k), :] = split(v)


            z_copy(k).start()

        return 0

    lax.fori_loop(0, NC + 1, z_body, 0)

    def z_sent():
        def z_done(k, _):
            z_copy(k).wait_send()
            return 0

        lax.fori_loop(0, NC, z_done, 0)

        @pl.when(zi < 3)
        def _():
            c_next().wait_send()

        @pl.when(zi == 3)
        def _():
            for half in range(2):
                @pl.when(end_z(c, half) != z)
                def _():
                    c_end(half).wait_send()

    def wide(k):
        return pl.ds(pl.multiple_of(k * WIDE, WIDE), WIDE)

    def p_copy(k):
        return rcopy(pout.at[wide(k)], zin.at[1, wide(k)], ps.at[k], zr.at[1, k], did(seg, x, z + 1))

    def p_body(k, _):
        got(zin.at[1, wide(k)], zr.at[1, k])

        @pl.when(zi < 3)
        def _():
            pout[wide(k), :] = mm3(zin[1, wide(k), :], whi[...], wlo[...], NT)
            p_copy(k).start()

        return 0

    def p_start(k, _):
        p_copy(k).start()
        return 0

    def p_done(k, _):
        p_copy(k).wait_send()
        return 0

    def prefix():
        @pl.when(jnp.logical_not(row | end))
        def _():
            lax.fori_loop(0, NP, p_body, 0)

        @pl.when(zi > 0)
        def _():
            hi, lo = split(zin[jnp.where(row, 0, 1)])
            inhi[...] = hi
            inlo[...] = lo

    pl.when(jnp.logical_not(guest))(prefix)

    iv = jnp.where(x < 2, 1, 0)
    w = jnp.where(x == 1, 0, 1)

    def half_rows(k, half):
        return pl.ds(pl.multiple_of(half * HALF + k * XROWS, XROWS), XROWS)

    def x_copy(k):
        return rcopy(px.at[half_rows(k, zh)], xin.at[half_rows(k, 0)], xs.at[k], xr.at[k], did(seg, xroot, z))

    def abx_copy(k):
        return rcopy(
            ab.at[w, half_rows(k, zh)], ab.at[w, half_rows(k, zh)], abx_s.at[k], abx_r.at[k], did(seg, 3 - x, z)
        )

    def abz_copy(k, which):
        return rcopy(
            ab.at[which, half_rows(k, zh)], ab.at[which, half_rows(k, zh)],
            abz_s.at[which, k], abz_r.at[which, k], did(seg, x, nz),
        )

    def abx_more(k):
        return rcopy(
            ab.at[w, half_rows(k, 1 - zh)], ab.at[w, half_rows(k, 1 - zh)], abm_s.at[k], abm_r.at[k], did(seg, 3 - x, z)
        )

    def map_copy(k):
        return rcopy(px.at[wide(k)], zin.at[0, wide(k)], map_s.at[k], map_r.at[k], did(seg, x, worker_z(seg)))

    def const_copy():
        return rcopy(cseg, cseg, const_s, const_r, did(seg, x, worker_z(seg)))

    def ab_split(which, rows):
        abhi[which, rows, :], ablo[which, rows, :] = split(ab[which, rows, :])

    def cx_copy(which, send, to):
        return rcopy(cown, cs.at[which], cx_s.at[send], cx_r.at[which], did(seg, to, z))

    @pl.when(end)
    def _():
        def x_wait(k, _):
            got(zin.at[1, piece(k)], zr.at[1, k])
            sphi[1 - ia, piece(k), :], splo[1 - ia, piece(k), :] = split(zin[1, piece(k), :])
            return 0

        lax.fori_loop(0, NC, x_wait, 0)
        for half in (zh, 1 - zh):
            part = pl.ds(pl.multiple_of(half * HALF, HALF), HALF)
            for core, dims in ((0, NT), (1, TN)):
                @pl.when(c == core)
                def _():
                    at = (part, slice(None)) if core == 0 else (slice(None), part)
                    p = dot(sphi[(0, *at)], sphi[1], dims)
                    p += dot(splo[(0, *at)], sphi[1], dims)
                    p += dot(sphi[(0, *at)], splo[1], dims)
                    px[part, :] = p

            if half is zh:
                @pl.when(outer)
                def _():
                    for k in range(NX):
                        x_copy(k).start()

        hi, lo = split(px[...])
        wxhi[...] = hi
        wxlo[...] = lo

        @pl.when(zh != c)
        def _():
            got(ch.at[zh], ch_r.at[zh])

        got(ch.at[1 - zh], ch_r.at[1 - zh])
        for core, dims in ((0, NT), (1, NN)):
            @pl.when(c == core)
            def _():
                cx[...] = mm3(ch[0], sphi[iv], splo[iv], dims) + ch[1]

        @pl.when(x == 0)
        def _():
            cown[...] = cx[...]
            cx_copy(0, 0, 1).start()

        @pl.when(x == 1)
        def _():
            got(cs.at[0], cx_r.at[0])
            cown[...] = mm3(cs[0], wxhi[...], wxlo[...]) + cx[...]
            cs[1] = cown[...]
            cx_copy(1, 0, 2).start()

        @pl.when(x == 2)
        def _():
            cown[...] = cx[...]
            cx_copy(2, 0, 3).start()

        @pl.when(x == 3)
        def _():
            got(cs.at[2], cx_r.at[2])
            cown[...] = mm3(cs[2], wxhi[...], wxlo[...], NT) + cx[...]
            cx_copy(3, 0, 2).start()
            cx_copy(3, 1, 1).start()

    @pl.when(end & jnp.logical_not(row))
    def _():
        lax.fori_loop(0, NP, p_start, 0)

    @pl.when(root)
    def _():
        def x_body(k, _):
            @pl.when(k < NX)
            def _():
                got(xin.at[half_rows(k, 0)], xr.at[k])
                v = mm3(xin[half_rows(k, 0), :], wxhi[...], wxlo[...])
                mine = half_rows(k, zh)
                ab[w, mine, :] = v
                abx_copy(k).start()
                abz_copy(k, w).start()
                abhi[w, mine, :], ablo[w, mine, :] = split(v)

            @pl.when(k >= LAG)
            def _():
                j = k - LAG
                got(ab.at[1 - w, half_rows(j, zh)], abx_r.at[j])

                @pl.when(j % 2 == 0)
                def _():
                    abz_copy(j, 1 - w).start()

                ab_split(1 - w, half_rows(j, zh))
                got(ab.at[w, half_rows(j, 1 - zh)], abz_r.at[w, j])

                @pl.when(j % 2 == 1)
                def _():
                    abx_more(j).start()

                ab_split(w, half_rows(j, 1 - zh))

            return 0

        lax.fori_loop(0, NX + LAG, x_body, 0)

        def ab_wait(k, _):
            @pl.when(k % 2 == 0)
            def _():
                got(ab.at[1 - w, half_rows(k, 1 - zh)], abz_r.at[1 - w, k])

            @pl.when(k % 2 == 1)
            def _():
                got(ab.at[1 - w, half_rows(k, 1 - zh)], abm_r.at[k])

            ab_split(1 - w, half_rows(k, 1 - zh))
            return 0

        lax.fori_loop(0, NX, ab_wait, 0)
        p = dot(abhi[0], abhi[1], NT)
        p += dot(ablo[0], abhi[1], NT)
        p += dot(abhi[0], ablo[1], NT)

        @pl.when(host)
        def _():
            px[...] = p
            for k in range(NP):
                map_copy(k).start()

        hi, lo = split(p)
        pfhi[...] = hi
        pflo[...] = lo

        @pl.when(x == 2)
        def _():
            got(cs.at[1], cx_r.at[1])

        got(cs.at[3], cx_r.at[3])
        cseg[...] = mm3(cs[1], abhi[1], ablo[1], NT) + cs[3]

        @pl.when(host)
        def _():
            const_copy().start()

    @pl.when(guest)
    def _():
        def map_got(k, _):
            got(zin.at[0, wide(k)], map_r.at[k])
            pfhi[wide(k), :], pflo[wide(k), :] = split(zin[0, wide(k), :])
            return 0

        lax.fori_loop(0, NP, map_got, 0)
        got(cseg, const_r)

    def x_sent():
        @pl.when(outer)
        def _():
            for k in range(NX):
                x_copy(k).wait_send()

            @pl.when(x == 0)
            def _():
                cx_copy(0, 0, 1).wait_send()

            @pl.when(x == 3)
            def _():
                cx_copy(3, 0, 2).wait_send()
                cx_copy(3, 1, 1).wait_send()

        @pl.when(root)
        def _():
            def ab_done(k, _):
                abx_copy(k).wait_send()
                abz_copy(k, w).wait_send()

                @pl.when(k % 2 == 0)
                def _():
                    abz_copy(k, 1 - w).wait_send()

                @pl.when(k % 2 == 1)
                def _():
                    abx_more(k).wait_send()

                return 0

            lax.fori_loop(0, NX, ab_done, 0)
            cx_copy(1, 0, 3).wait_send()

    m0 = jnp.concatenate([m0_ref[...], pad], axis=0)
    chained = root | guest | (end & (x == 0))

    @pl.when(chained & first)
    def _():
        m_in[...] = m0

    @pl.when(chained & jnp.logical_not(first))
    def _():
        got(m_in, m_r)

    def m_copy(send):
        to = jnp.where(send == 1, 0, x)
        at = jnp.where(send == 0, worker_z(seg + 1), end_z(way(seg + 1), zh))
        return rcopy(m_out, m_in, m_s.at[send], m_r, did(seg + 1, to, at))

    def f_copy(blk):
        return rcopy(f_out.at[blk], f_in.at[blk], f_s.at[blk], f_r.at[blk], did(seg + 1, x, worker_z(seg + 1)))

    def owner(blk):
        return jnp.where(blk < 4, x, xouter), zh * 4 + blk % 4

    def fb_copy(blk):
        ox, oz = owner(blk)
        return rcopy(f_out.at[blk], ends_ref.at[0], fb_s.at[blk], fb_r, did(seg, ox, oz))

    def ex_copy(to):
        return rcopy(e_out, e_x, ex_s, ex_r, did(seg, to, z))

    @pl.when(worker & jnp.logical_not(last))
    def _():
        m_out[...] = mm3(m_in[...], pfhi[...], pflo[...]) + cseg[...]
        m_copy(0).start()

        @pl.when(x == 1)
        def _():
            m_copy(1).start()

        @pl.when(moved(seg + 1))
        def _():
            m_copy(2).start()


    def e_copy(k):
        return rcopy(e_half, e_in, e_s.at[k], e_r, did(seg, x, zh * 4 + (zi + k + 1) % 4))

    def go_down():
        pl.when(guest)(prefix)

        @pl.when(root & (x == 2))
        def _():
            e_x[...] = mm3(m_in[...], abhi[0], ablo[0]) + cs[1]
            e_out[...] = mm3(e_x[...], wxhi[...], wxlo[...], NT) + cx[...]
            ex_copy(3).start()

        @pl.when(end & (x == 0))
        def _():
            e_out[...] = mm3(m_in[...], wxhi[...], wxlo[...]) + cx[...]
            ex_copy(1).start()
            e_x[...] = m_in[...]

        @pl.when(end & ((x == 1) | (x == 3)))
        def _():
            got(e_x, ex_r)

        @pl.when(end & (zh == 0))
        def _():
            e_half[...] = e_x[...]

        for core, dims in ((0, NN), (1, NT)):
            @pl.when(end & (zh == 1) & (c == core))
            def _():
                e_half[...] = mm3(e_x[...], sphi[1 - iv], splo[1 - iv], dims) + ch[0]

        @pl.when(end)
        def _():
            for k in range(3):
                e_copy(k).start()

        @pl.when(jnp.logical_not(end))
        def _():
            got(e_in, e_r)
            e_half[...] = e_in[...]

        @pl.when(zi > 0)
        def _():
            e_in[...] = mm3(e_half[...], inhi[...], inlo[...]) + cin[...]

        @pl.when(zi == 0)
        def _():
            e_in[...] = e_half[...]

        m1, m2 = two_steps(e_in[...])
        means_ref[0] = m1[:4]
        means_ref[1] = m2[:4]

    def f_home(blk):
        @pl.when(blk != block)
        def _():
            fb_copy(blk).start()

        @pl.when(blk == block)
        def _():
            ends_ref[0] = f_out[blk]

    def f_block(k):
        blk = jnp.where(k < 4, 4, 0) + jnp.where(zh == 0, k % 4, 3 - k % 4)

        @pl.when(first & (blk != block))
        def _():
            got(f_in.at[blk], f0_r.at[blk])

        @pl.when(jnp.logical_not(first))
        def _():
            got(f_in.at[blk], f_r.at[blk])

        f_out[blk] = mm3(f_in[blk], pfhi[...], pflo[...])

        @pl.when(jnp.logical_not(last))
        def _():
            f_copy(blk).start()

        @pl.when(last)
        def _():
            f_home(blk)

    down_turn = jnp.where(worker, 8, 0)

    def chain_body(k, _):
        pl.when(k == down_turn)(go_down)

        @pl.when(worker & (k < 8))
        def _():
            f_block(k)

        return 0

    lax.fori_loop(0, jnp.where(worker, 9, 1), chain_body, 0)

    @pl.when(worker & jnp.logical_not(last))
    def _():
        for blk in range(8):
            f_home(blk)

    @pl.when(jnp.logical_not(worker))
    def _():
        got(ends_ref.at[0], fb_r)

    def rest_sent():
        @pl.when(first & jnp.logical_not(root))
        def _():
            f0_copy().wait_send()

        @pl.when(worker)
        def _():
            @pl.when(jnp.logical_not(last))
            def _():
                m_copy(0).wait_send()

                @pl.when(x == 1)
                def _():
                    m_copy(1).wait_send()

                @pl.when(moved(seg + 1))
                def _():
                    m_copy(2).wait_send()

                for blk in range(8):
                    f_copy(blk).wait_send()

            for blk in range(8):
                @pl.when(blk != block)
                def _():
                    fb_copy(blk).wait_send()

        @pl.when(end & ((x == 0) | (x == 2)))
        def _():
            ex_copy(1).wait_send()

        @pl.when(end)
        def _():
            for k in range(3):
                e_copy(k).wait_send()

        @pl.when(jnp.logical_not(row) & (zi < 3))
        def _():
            lax.fori_loop(0, NP, p_done, 0)

        @pl.when(host)
        def _():
            const_copy().wait_send()
            for k in range(NP):
                map_copy(k).wait_send()

    z_sent()
    x_sent()
    rest_sent()


def per_device(transition, obs_gain, observed, init_mean, init_factor):
    vm = pl.BlockSpec(memory_space=pltpu.VMEM)
    f, b = (lambda *s: pltpu.VMEM(s, F32)), (lambda *s: pltpu.VMEM(s, BF16))
    dma = lambda *s: pltpu.SemaphoreType.DMA(s) if s else pltpu.SemaphoreType.DMA
    scratch = [
        f(D, D), f(2, D, D), b(D, D), b(D, D), f(2, PAD, D), f(PAD, D), f(2, PAD, D), f(PAD, D),
        b(2, D, D), b(2, D, D), f(D, D), b(D, D), b(D, D), f(HALF, D), f(2, D, D), b(2, D, D), b(2, D, D), b(D, D), b(D, D),
        f(4, PAD, D), f(PAD, D), f(PAD, D), f(PAD, D), f(PAD, D), f(PAD, D), f(8, 16, D), f(8, 16, D), b(D, D), b(D, D),
        f(PAD, D), f(PAD, D), f(PAD, D), f(PAD, D), f(D, D),
        dma(NP), dma(NP), dma(), dma(), dma(NP), dma(NC), dma(2, NC), dma(), dma(), dma(2), dma(2), dma(NX), dma(NX), dma(NX), dma(NX), dma(NX), dma(NX), dma(2, NX), dma(2, NX),
        dma(2), dma(4), dma(3), dma(), dma(), dma(8), dma(8), dma(8), dma(8), dma(), dma(3), dma(), dma(), dma(),
    ]
    outs = pl.pallas_call(
        kernel,
        out_shape=(jax.ShapeDtypeStruct((2, 4, D), F32), jax.ShapeDtypeStruct((1, 16, D), F32)),
        in_specs=[vm] * 5,
        out_specs=(vm, vm),
        scratch_shapes=scratch,
        compiler_params=pltpu.CompilerParams(
            collective_id=0, has_side_effects=True, vmem_limit_bytes=56 * 2**20
        ),
        name="filter_flow",
    )(transition, obs_gain, observed, init_mean, init_factor)

    def hand_on(a_ref, b_ref, a_out, b_out):
        a_out[...] = a_ref[...]
        b_out[...] = b_ref[...]

    return pl.pallas_call(
        hand_on, out_shape=tuple(jax.ShapeDtypeStruct(o.shape, o.dtype) for o in outs), in_specs=[vm] * 2, out_specs=(vm, vm),
        name="hand_on",
    )(*outs)


def solution(mesh):
    placed = P(("seg", "tm"), None, None)
    return jax.shard_map(
        per_device,
        mesh=mesh,
        in_specs=(placed, placed, placed, P(), P("tm", None)),
        out_specs=(placed, P("seg", "tm", None)),
        check_vma=False,
    )
```

```python
import functools

import jax
import jax.numpy as jnp
from jax import lax
from jax.experimental import pallas as pl
from jax.experimental.pallas import tpu as pltpu
from jax.sharding import PartitionSpec as P

MESH = pl.DeviceIdType.MESH
F32, BF16 = jnp.float32, jnp.bfloat16
D = 512
HALF = D // 2
ROWS = 32
NC = D // ROWS
XROWS = 32
NX = HALF // XROWS
LAG = 6
WIDE = 128
NP = D // WIDE
PAD = 8

NN = (((1,), (0,)), ((), ()))
NT = (((1,), (1,)), ((), ()))
TN = (((0,), (0,)), ((), ()))
TT = (((0,), (1,)), ((), ()))


def dot(a, b, dims=NN):
    return lax.dot_general(a, b, dims, preferred_element_type=F32)


def split(a):
    hi = a.astype(BF16)
    return hi, (a - hi.astype(F32)).astype(BF16)


def mm3(a, hi, lo, dims=NN):
    ah, al = split(a)
    n = a.shape[0]
    both = dot(jnp.concatenate([ah, al], axis=0), hi, dims)
    return both[:n] + both[n:] + dot(ah, lo, dims)


def mm2(a, exact):
    ah, al = split(a)
    n = a.shape[0]
    both = dot(jnp.concatenate([ah, al], axis=0), exact)
    return both[:n] + both[n:]


def kernel(
    t_ref, g_ref, o_ref, m0_ref, f0_ref, means_ref, ends_ref,
    zout, zin, whi, wlo, drv, cin, ch, csend,
    sphi, splo, px, wxhi, wxlo, xin, ab, abhi, ablo, pfhi, pflo,
    cs, cx, cseg, cown, m_in, m_out, f_in, f_out, inhi, inlo, e_in, e_out, e_half, e_x, pout,
    map_s, map_r, const_s, const_r, ps, zs, zr, cs_s, cs_r, ch_s, ch_r, xs, xr, abx_s, abx_r, abm_s, abm_r, abz_s, abz_r,
    cx_s, cx_r, m_s, m_r, f0_s, f0_r, f_s, f_r, fb_s, fb_r, e_s, e_r, ex_s, ex_r,
):
    seg = lax.axis_index("seg")
    tm = lax.axis_index("tm")

    def way(s):
        return jnp.where(s < 6, s + s // 2, s) % 2

    c = way(seg)
    x, z = tm // 8, tm % 8
    zh, zi = z // 4, z % 4
    row = zh == c
    pos = jnp.where(row, zi, 3 - zi)
    nz = jnp.where(row, (z + 1) % 8, (z + 7) % 8)
    end = pos == 3
    inner = (x == 1) | (x == 2)
    root = end & inner
    outer = end & jnp.logical_not(inner)
    first, last = seg == 0, seg == 7
    xroot = jnp.where(x < 2, 1, 2)
    xouter = jnp.where(x < 2, 0, 3)

    def end_z(core, half):
        return jnp.where(core == 0, 3 + half, 7 * half)

    def did(s, xx, zz):
        return (s, xx * 8 + zz)

    myend = end_z(c, zh)

    def moved(s):
        return (s == 5) | (s == 7)

    def worker_z(s):
        return end_z(jnp.where(moved(s), 0, way(s)), zh)

    worker = inner & (z == worker_z(seg))
    guest = worker & moved(seg)
    host = root & moved(seg)

    def rcopy(src, dst, ssem, rsem, dev):
        return pltpu.make_async_remote_copy(
            src_ref=src, dst_ref=dst, send_sem=ssem, recv_sem=rsem, device_id=dev, device_id_type=MESH
        )

    def got(dst, rsem):
        rcopy(dst, dst, rsem, rsem, did(seg, x, nz)).wait_recv()

    barrier = pltpu.get_barrier_semaphore()

    def greet(dev):
        pl.semaphore_signal(barrier, inc=1, device_id=dev, device_id_type=MESH)

    pz = jnp.where(row, z - 1, z + 1)

    @pl.when(pos < 3)
    def _():
        greet(did(seg, x, myend))

    @pl.when((pos < 2) | end)
    def _():
        greet(did(seg, x, nz))

    @pl.when((pos == 1) | (pos == 2))
    def _():
        greet(did(seg, x, pz))

    @pl.when((pos == 0) & jnp.logical_not(row))
    def _():
        greet(did(seg, x, end_z(c, 1 - zh)))

    @pl.when(end)
    def _():
        for k in range(1, 4):
            greet(did(seg, x, zh * 4 + (zi + k) % 4))

        @pl.when(row)
        def _():
            greet(did(seg, x, (1 - zh) * 4 + 3))

    for here, others in ((0, (1,)), (1, (0, 2, 3)), (2, (1, 3)), (3, (2, 1))):
        @pl.when(end & (x == here))
        def _():
            for k in others:
                greet(did(seg, k, z))

    @pl.when(jnp.logical_not(inner))
    def _():
        greet(did(seg, xroot, myend))

        @pl.when(moved(seg))
        def _():
            greet(did(seg, xroot, worker_z(seg)))

    @pl.when(root | guest)
    def _():
        for k in range(4):
            greet(did(seg, xouter, zh * 4 + k))

    middle = inner & moved(seg) & ((pos == 1) | (pos == 2))

    @pl.when(middle)
    def _():
        greet(did(seg, x, worker_z(seg)))

    @pl.when(guest)
    def _():
        for k in (1, 2):
            greet(did(seg, x, jnp.where(row, z + k, z - k)))

    @pl.when(worker & jnp.logical_not(last))
    def _():
        greet(did(seg + 1, x, worker_z(seg + 1)))

        @pl.when(moved(seg + 1))
        def _():
            greet(did(seg + 1, x, end_z(way(seg + 1), zh)))

        @pl.when(x == 1)
        def _():
            greet(did(seg + 1, 0, end_z(way(seg + 1), zh)))

    @pl.when((worker | host) & jnp.logical_not(first))
    def _():
        greet(did(seg - 1, x, worker_z(seg - 1)))

    @pl.when(end & (x == 0) & jnp.logical_not(first))
    def _():
        greet(did(seg - 1, 1, worker_z(seg - 1)))

    one = lambda p: jnp.where(p, 1, 0)
    greets = (
        one(pos < 3) + one((pos < 2) | end) + one((pos == 1) | (pos == 2)) + one((pos == 0) & jnp.logical_not(row))
        + one(end) * (3 + one(row) + jnp.where(x == 0, 1, jnp.where(x == 1, 3, 2))) + one(jnp.logical_not(inner))
        + one(jnp.logical_not(inner) & moved(seg)) + 4 * one(root | guest) + one(middle) + 2 * one(guest)
        + one(worker & jnp.logical_not(last)) * (1 + one(moved(seg + 1)) + one(x == 1))
        + one((worker | host) & jnp.logical_not(first)) + one(end & (x == 0) & jnp.logical_not(first))
    )

    def put_map(m):
        @pl.when(pos == 0)
        def _():
            zout[...] = m

        @pl.when(pos > 0)
        def _():
            hi, lo = split(m)
            whi[...] = hi
            wlo[...] = lo

    @pl.when(row)
    def _():
        put_map(dot(t_ref[0], t_ref[1]))

    @pl.when(jnp.logical_not(row))
    def _():
        put_map(dot(t_ref[1], t_ref[0], TT))

        @pl.when(end)
        def _():
            pout[...] = dot(t_ref[0], t_ref[1])

    pad = jnp.zeros((PAD - 4, D), F32)
    for s in range(2):
        drv[s] = jnp.concatenate([dot(o_ref[s], g_ref[s]), pad], axis=0)

    @pl.when(zi == 0)
    def _():
        cin[...] = jnp.zeros_like(cin)

    pl.semaphore_wait(barrier, greets)

    block = jnp.where(x == xroot, 0, 4) + zi

    def f0_copy():
        return rcopy(f0_ref, f_in.at[block], f0_s, f0_r.at[block], did(seg, xroot, myend))

    @pl.when(first & jnp.logical_not(root))
    def _():
        f0_copy().start()

    @pl.when(first & root)
    def _():
        f_in[block] = f0_ref[...]

    def two_steps(m):
        m1 = mm2(m, t_ref[0]) + drv[0]
        return m1, mm2(m1, t_ref[1]) + drv[1]

    def c_next():
        return rcopy(csend, cin, cs_s, cs_r, did(seg, x, (z + 1) % 8))

    def c_end(half):
        return rcopy(csend, ch.at[zh], ch_s.at[half], ch_r.at[zh], did(seg, x, end_z(c, half)))

    def c_step():
        @pl.when(zi > 0)
        def _():
            got(cin, cs_r)

        csend[...] = two_steps(cin[...])[1]

        @pl.when(zi < 3)
        def _():
            c_next().start()

        @pl.when(zi == 3)
        def _():
            for half in range(2):
                away = end_z(c, half) != z

                @pl.when(away)
                def _():
                    c_end(half).start()

                @pl.when(jnp.logical_not(away))
                def _():
                    ch[zh] = csend[...]

    turn = jnp.where(row, 0, jnp.where(pos == 1, NC // 2, jnp.where(pos == 0, NC, 0)))
    slot = jnp.where(end, 1, 0)

    def piece(k):
        return pl.ds(pl.multiple_of(k * ROWS, ROWS), ROWS)

    def z_copy(k):
        return rcopy(
            zout.at[piece(k)], zin.at[slot, piece(k)], zs.at[k], zr.at[slot, k], did(seg, x, nz)
        )

    ia = jnp.where((zh == 0) == (x < 2), 0, 1)

    def z_body(k, _):
        pl.when(k == turn)(c_step)

        @pl.when(k < NC)
        def _():
            @pl.when(pos > 0)
            def _():
                got(zin.at[0, piece(k)], zr.at[0, k])
                v = mm3(zin[0, piece(k), :], whi[...], wlo[...])
                zout[piece(k), :] = v

                @pl.when(end)
                def _():
                    sphi[ia, piece(k), :], splo[ia, piece(k), :] = split(v)


            z_copy(k).start()

        return 0

    lax.fori_loop(0, NC + 1, z_body, 0)

    def z_sent():
        def z_done(k, _):
            z_copy(k).wait_send()
            return 0

        lax.fori_loop(0, NC, z_done, 0)

        @pl.when(zi < 3)
        def _():
            c_next().wait_send()

        @pl.when(zi == 3)
        def _():
            for half in range(2):
                @pl.when(end_z(c, half) != z)
                def _():
                    c_end(half).wait_send()

    def wide(k):
        return pl.ds(pl.multiple_of(k * WIDE, WIDE), WIDE)

    def p_copy(k):
        return rcopy(pout.at[wide(k)], zin.at[1, wide(k)], ps.at[k], zr.at[1, k], did(seg, x, z + 1))

    def p_body(k, _):
        got(zin.at[1, wide(k)], zr.at[1, k])

        @pl.when(zi < 3)
        def _():
            pout[wide(k), :] = mm3(zin[1, wide(k), :], whi[...], wlo[...], NT)
            p_copy(k).start()

        return 0

    def p_start(k, _):
        p_copy(k).start()
        return 0

    def p_done(k, _):
        p_copy(k).wait_send()
        return 0

    def prefix():
        @pl.when(jnp.logical_not(row | end))
        def _():
            lax.fori_loop(0, NP, p_body, 0)

        @pl.when(zi > 0)
        def _():
            hi, lo = split(zin[jnp.where(row, 0, 1)])
            inhi[...] = hi
            inlo[...] = lo

    pl.when(jnp.logical_not(guest))(prefix)

    iv = jnp.where(x < 2, 1, 0)
    w = jnp.where(x == 1, 0, 1)

    def half_rows(k, half):
        return pl.ds(pl.multiple_of(half * HALF + k * XROWS, XROWS), XROWS)

    def x_copy(k):
        return rcopy(px.at[half_rows(k, zh)], xin.at[half_rows(k, 0)], xs.at[k], xr.at[k], did(seg, xroot, z))

    def abx_copy(k):
        return rcopy(
            ab.at[w, half_rows(k, zh)], ab.at[w, half_rows(k, zh)], abx_s.at[k], abx_r.at[k], did(seg, 3 - x, z)
        )

    def abz_copy(k, which):
        return rcopy(
            ab.at[which, half_rows(k, zh)], ab.at[which, half_rows(k, zh)],
            abz_s.at[which, k], abz_r.at[which, k], did(seg, x, nz),
        )

    def abx_more(k):
        return rcopy(
            ab.at[w, half_rows(k, 1 - zh)], ab.at[w, half_rows(k, 1 - zh)], abm_s.at[k], abm_r.at[k], did(seg, 3 - x, z)
        )

    def map_copy(k):
        return rcopy(px.at[wide(k)], zin.at[0, wide(k)], map_s.at[k], map_r.at[k], did(seg, x, worker_z(seg)))

    def const_copy():
        return rcopy(cseg, cseg, const_s, const_r, did(seg, x, worker_z(seg)))

    def ab_split(which, rows):
        abhi[which, rows, :], ablo[which, rows, :] = split(ab[which, rows, :])

    def cx_copy(which, send, to):
        return rcopy(cown, cs.at[which], cx_s.at[send], cx_r.at[which], did(seg, to, z))

    @pl.when(end)
    def _():
        def x_wait(k, _):
            got(zin.at[1, piece(k)], zr.at[1, k])
            sphi[1 - ia, piece(k), :], splo[1 - ia, piece(k), :] = split(zin[1, piece(k), :])
            return 0

        lax.fori_loop(0, NC, x_wait, 0)
        for half in (zh, 1 - zh):
            part = pl.ds(pl.multiple_of(half * HALF, HALF), HALF)
            for core, dims in ((0, NT), (1, TN)):
                @pl.when(c == core)
                def _():
                    at = (part, slice(None)) if core == 0 else (slice(None), part)
                    p = dot(sphi[(0, *at)], sphi[1], dims)
                    p += dot(splo[(0, *at)], sphi[1], dims)
                    p += dot(sphi[(0, *at)], splo[1], dims)
                    px[part, :] = p

            if half is zh:
                @pl.when(outer)
                def _():
                    for k in range(NX):
                        x_copy(k).start()

        hi, lo = split(px[...])
        wxhi[...] = hi
        wxlo[...] = lo

        @pl.when(zh != c)
        def _():
            got(ch.at[zh], ch_r.at[zh])

        got(ch.at[1 - zh], ch_r.at[1 - zh])
        for core, dims in ((0, NT), (1, NN)):
            @pl.when(c == core)
            def _():
                cx[...] = mm3(ch[0], sphi[iv], splo[iv], dims) + ch[1]

        @pl.when(x == 0)
        def _():
            cown[...] = cx[...]
            cx_copy(0, 0, 1).start()

        @pl.when(x == 1)
        def _():
            got(cs.at[0], cx_r.at[0])
            cown[...] = mm3(cs[0], wxhi[...], wxlo[...]) + cx[...]
            cs[1] = cown[...]
            cx_copy(1, 0, 2).start()

        @pl.when(x == 2)
        def _():
            cown[...] = cx[...]
            cx_copy(2, 0, 3).start()

        @pl.when(x == 3)
        def _():
            got(cs.at[2], cx_r.at[2])
            cown[...] = mm3(cs[2], wxhi[...], wxlo[...], NT) + cx[...]
            cx_copy(3, 0, 2).start()
            cx_copy(3, 1, 1).start()

    @pl.when(end & jnp.logical_not(row))
    def _():
        lax.fori_loop(0, NP, p_start, 0)

    @pl.when(root)
    def _():
        def x_body(k, _):
            @pl.when(k < NX)
            def _():
                got(xin.at[half_rows(k, 0)], xr.at[k])
                v = mm3(xin[half_rows(k, 0), :], wxhi[...], wxlo[...])
                mine = half_rows(k, zh)
                ab[w, mine, :] = v
                abx_copy(k).start()
                abz_copy(k, w).start()
                abhi[w, mine, :], ablo[w, mine, :] = split(v)

            @pl.when(k >= LAG)
            def _():
                j = k - LAG
                got(ab.at[1 - w, half_rows(j, zh)], abx_r.at[j])

                @pl.when(j % 2 == 0)
                def _():
                    abz_copy(j, 1 - w).start()

                ab_split(1 - w, half_rows(j, zh))
                got(ab.at[w, half_rows(j, 1 - zh)], abz_r.at[w, j])

                @pl.when(j % 2 == 1)
                def _():
                    abx_more(j).start()

                ab_split(w, half_rows(j, 1 - zh))

            return 0

        lax.fori_loop(0, NX + LAG, x_body, 0)

        def ab_wait(k, _):
            @pl.when(k % 2 == 0)
            def _():
                got(ab.at[1 - w, half_rows(k, 1 - zh)], abz_r.at[1 - w, k])

            @pl.when(k % 2 == 1)
            def _():
                got(ab.at[1 - w, half_rows(k, 1 - zh)], abm_r.at[k])

            ab_split(1 - w, half_rows(k, 1 - zh))
            return 0

        lax.fori_loop(0, NX, ab_wait, 0)
        p = dot(abhi[0], abhi[1], NT)
        p += dot(ablo[0], abhi[1], NT)
        p += dot(abhi[0], ablo[1], NT)

        @pl.when(host)
        def _():
            px[...] = p
            for k in range(NP):
                map_copy(k).start()

        hi, lo = split(p)
        pfhi[...] = hi
        pflo[...] = lo

        @pl.when(x == 2)
        def _():
            got(cs.at[1], cx_r.at[1])

        got(cs.at[3], cx_r.at[3])
        cseg[...] = mm3(cs[1], abhi[1], ablo[1], NT) + cs[3]

        @pl.when(host)
        def _():
            const_copy().start()

    @pl.when(guest)
    def _():
        def map_got(k, _):
            got(zin.at[0, wide(k)], map_r.at[k])
            pfhi[wide(k), :], pflo[wide(k), :] = split(zin[0, wide(k), :])
            return 0

        lax.fori_loop(0, NP, map_got, 0)
        got(cseg, const_r)

    def x_sent():
        @pl.when(outer)
        def _():
            for k in range(NX):
                x_copy(k).wait_send()

            @pl.when(x == 0)
            def _():
                cx_copy(0, 0, 1).wait_send()

            @pl.when(x == 3)
            def _():
                cx_copy(3, 0, 2).wait_send()
                cx_copy(3, 1, 1).wait_send()

        @pl.when(root)
        def _():
            def ab_done(k, _):
                abx_copy(k).wait_send()
                abz_copy(k, w).wait_send()

                @pl.when(k % 2 == 0)
                def _():
                    abz_copy(k, 1 - w).wait_send()

                @pl.when(k % 2 == 1)
                def _():
                    abx_more(k).wait_send()

                return 0

            lax.fori_loop(0, NX, ab_done, 0)
            cx_copy(1, 0, 3).wait_send()

    m0 = jnp.concatenate([m0_ref[...], pad], axis=0)
    chained = root | guest | (end & (x == 0))

    @pl.when(chained & first)
    def _():
        m_in[...] = m0

    @pl.when(chained & jnp.logical_not(first))
    def _():
        got(m_in, m_r)

    def m_copy(send):
        to = jnp.where(send == 1, 0, x)
        at = jnp.where(send == 0, worker_z(seg + 1), end_z(way(seg + 1), zh))
        return rcopy(m_out, m_in, m_s.at[send], m_r, did(seg + 1, to, at))

    def f_copy(blk):
        return rcopy(f_out.at[blk], f_in.at[blk], f_s.at[blk], f_r.at[blk], did(seg + 1, x, worker_z(seg + 1)))

    def owner(blk):
        return jnp.where(blk < 4, x, xouter), zh * 4 + blk % 4

    def fb_copy(blk):
        ox, oz = owner(blk)
        return rcopy(f_out.at[blk], ends_ref.at[0], fb_s.at[blk], fb_r, did(seg, ox, oz))

    def ex_copy(to):
        return rcopy(e_out, e_x, ex_s, ex_r, did(seg, to, z))

    @pl.when(worker & jnp.logical_not(last))
    def _():
        m_out[...] = mm3(m_in[...], pfhi[...], pflo[...]) + cseg[...]
        m_copy(0).start()

        @pl.when(x == 1)
        def _():
            m_copy(1).start()

        @pl.when(moved(seg + 1))
        def _():
            m_copy(2).start()


    def e_copy(k):
        return rcopy(e_half, e_in, e_s.at[k], e_r, did(seg, x, zh * 4 + (zi + k + 1) % 4))

    def go_down():
        pl.when(guest)(prefix)

        @pl.when(root & (x == 2))
        def _():
            e_x[...] = mm3(m_in[...], abhi[0], ablo[0]) + cs[1]
            e_out[...] = mm3(e_x[...], wxhi[...], wxlo[...], NT) + cx[...]
            ex_copy(3).start()

        @pl.when(end & (x == 0))
        def _():
            e_out[...] = mm3(m_in[...], wxhi[...], wxlo[...]) + cx[...]
            ex_copy(1).start()
            e_x[...] = m_in[...]

        @pl.when(end & ((x == 1) | (x == 3)))
        def _():
            got(e_x, ex_r)

        @pl.when(end & (zh == 0))
        def _():
            e_half[...] = e_x[...]

        for core, dims in ((0, NN), (1, NT)):
            @pl.when(end & (zh == 1) & (c == core))
            def _():
                e_half[...] = mm3(e_x[...], sphi[1 - iv], splo[1 - iv], dims) + ch[0]

        @pl.when(end)
        def _():
            for k in range(3):
                e_copy(k).start()

        @pl.when(jnp.logical_not(end))
        def _():
            got(e_in, e_r)
            e_half[...] = e_in[...]

        @pl.when(zi > 0)
        def _():
            e_in[...] = mm3(e_half[...], inhi[...], inlo[...]) + cin[...]

        @pl.when(zi == 0)
        def _():
            e_in[...] = e_half[...]

        m1, m2 = two_steps(e_in[...])
        means_ref[0] = m1[:4]
        means_ref[1] = m2[:4]

    def f_home(blk):
        @pl.when(blk != block)
        def _():
            fb_copy(blk).start()

        @pl.when(blk == block)
        def _():
            ends_ref[0] = f_out[blk]

    def f_block(k):
        blk = jnp.where(k < 4, 4, 0) + jnp.where(zh == 0, k % 4, 3 - k % 4)

        @pl.when(first & (blk != block))
        def _():
            got(f_in.at[blk], f0_r.at[blk])

        @pl.when(jnp.logical_not(first))
        def _():
            got(f_in.at[blk], f_r.at[blk])

        f_out[blk] = mm3(f_in[blk], pfhi[...], pflo[...])

        @pl.when(jnp.logical_not(last))
        def _():
            f_copy(blk).start()

        @pl.when(last)
        def _():
            f_home(blk)

    down_turn = jnp.where(worker, 8, 0)

    def all_home():
        for blk in range(8):
            f_home(blk)

    def chain_body(k, _):
        pl.when((k == 8) & worker & jnp.logical_not(last))(all_home)
        pl.when(k == down_turn)(go_down)

        @pl.when(worker & (k < 8))
        def _():
            f_block(k)

        return 0

    lax.fori_loop(0, jnp.where(worker, 9, 1), chain_body, 0)


    @pl.when(jnp.logical_not(worker))
    def _():
        got(ends_ref.at[0], fb_r)

    def rest_sent():
        @pl.when(first & jnp.logical_not(root))
        def _():
            f0_copy().wait_send()

        @pl.when(worker)
        def _():
            @pl.when(jnp.logical_not(last))
            def _():
                m_copy(0).wait_send()

                @pl.when(x == 1)
                def _():
                    m_copy(1).wait_send()

                @pl.when(moved(seg + 1))
                def _():
                    m_copy(2).wait_send()

                for blk in range(8):
                    f_copy(blk).wait_send()

            for blk in range(8):
                @pl.when(blk != block)
                def _():
                    fb_copy(blk).wait_send()

        @pl.when(end & ((x == 0) | (x == 2)))
        def _():
            ex_copy(1).wait_send()

        @pl.when(end)
        def _():
            for k in range(3):
                e_copy(k).wait_send()

        @pl.when(jnp.logical_not(row) & (zi < 3))
        def _():
            lax.fori_loop(0, NP, p_done, 0)

        @pl.when(host)
        def _():
            const_copy().wait_send()
            for k in range(NP):
                map_copy(k).wait_send()

    z_sent()
    x_sent()
    rest_sent()


def per_device(transition, obs_gain, observed, init_mean, init_factor):
    vm = pl.BlockSpec(memory_space=pltpu.VMEM)
    f, b = (lambda *s: pltpu.VMEM(s, F32)), (lambda *s: pltpu.VMEM(s, BF16))
    dma = lambda *s: pltpu.SemaphoreType.DMA(s) if s else pltpu.SemaphoreType.DMA
    scratch = [
        f(D, D), f(2, D, D), b(D, D), b(D, D), f(2, PAD, D), f(PAD, D), f(2, PAD, D), f(PAD, D),
        b(2, D, D), b(2, D, D), f(D, D), b(D, D), b(D, D), f(HALF, D), f(2, D, D), b(2, D, D), b(2, D, D), b(D, D), b(D, D),
        f(4, PAD, D), f(PAD, D), f(PAD, D), f(PAD, D), f(PAD, D), f(PAD, D), f(8, 16, D), f(8, 16, D), b(D, D), b(D, D),
        f(PAD, D), f(PAD, D), f(PAD, D), f(PAD, D), f(D, D),
        dma(NP), dma(NP), dma(), dma(), dma(NP), dma(NC), dma(2, NC), dma(), dma(), dma(2), dma(2), dma(NX), dma(NX), dma(NX), dma(NX), dma(NX), dma(NX), dma(2, NX), dma(2, NX),
        dma(2), dma(4), dma(3), dma(), dma(), dma(8), dma(8), dma(8), dma(8), dma(), dma(3), dma(), dma(), dma(),
    ]
    outs = pl.pallas_call(
        kernel,
        out_shape=(jax.ShapeDtypeStruct((2, 4, D), F32), jax.ShapeDtypeStruct((1, 16, D), F32)),
        in_specs=[vm] * 5,
        out_specs=(vm, vm),
        scratch_shapes=scratch,
        compiler_params=pltpu.CompilerParams(
            collective_id=0, has_side_effects=True, vmem_limit_bytes=56 * 2**20
        ),
        name="filter_flow",
    )(transition, obs_gain, observed, init_mean, init_factor)

    def hand_on(a_ref, b_ref, a_out, b_out):
        a_out[...] = a_ref[...]
        b_out[...] = b_ref[...]

    return pl.pallas_call(
        hand_on, out_shape=tuple(jax.ShapeDtypeStruct(o.shape, o.dtype) for o in outs), in_specs=[vm] * 2, out_specs=(vm, vm),
        name="hand_on",
    )(*outs)


def solution(mesh):
    placed = P(("seg", "tm"), None, None)
    return jax.shard_map(
        per_device,
        mesh=mesh,
        in_specs=(placed, placed, placed, P(), P("tm", None)),
        out_specs=(placed, P("seg", "tm", None)),
        check_vma=False,
    )
```

```python
import functools

import jax
import jax.numpy as jnp
from jax import lax
from jax.experimental import pallas as pl
from jax.experimental.pallas import tpu as pltpu
from jax.sharding import PartitionSpec as P

MESH = pl.DeviceIdType.MESH
F32, BF16 = jnp.float32, jnp.bfloat16
D = 512
HALF = D // 2
ROWS = 32
NC = D // ROWS
XROWS = 32
NX = HALF // XROWS
LAG = 8
WIDE = 128
NP = D // WIDE
PAD = 8

NN = (((1,), (0,)), ((), ()))
NT = (((1,), (1,)), ((), ()))
TN = (((0,), (0,)), ((), ()))
TT = (((0,), (1,)), ((), ()))


def dot(a, b, dims=NN):
    return lax.dot_general(a, b, dims, preferred_element_type=F32)


def split(a):
    hi = a.astype(BF16)
    return hi, (a - hi.astype(F32)).astype(BF16)


def mm3(a, hi, lo, dims=NN):
    ah, al = split(a)
    n = a.shape[0]
    both = dot(jnp.concatenate([ah, al], axis=0), hi, dims)
    return both[:n] + both[n:] + dot(ah, lo, dims)


def mm2(a, exact):
    ah, al = split(a)
    n = a.shape[0]
    both = dot(jnp.concatenate([ah, al], axis=0), exact)
    return both[:n] + both[n:]


def kernel(
    t_ref, g_ref, o_ref, m0_ref, f0_ref, means_ref, ends_ref,
    zout, zin, whi, wlo, drv, cin, ch, csend,
    sphi, splo, px, wxhi, wxlo, xin, ab, abhi, ablo, pfhi, pflo,
    cs, cx, cseg, cown, m_in, m_out, f_in, f_out, inhi, inlo, e_in, e_out, e_half, e_x, pout,
    map_s, map_r, const_s, const_r, ps, zs, zr, cs_s, cs_r, ch_s, ch_r, xs, xr, abx_s, abx_r, abm_s, abm_r, abz_s, abz_r,
    cx_s, cx_r, m_s, m_r, f0_s, f0_r, f_s, f_r, fb_s, fb_r, e_s, e_r, ex_s, ex_r,
):
    seg = lax.axis_index("seg")
    tm = lax.axis_index("tm")

    def way(s):
        return jnp.where(s < 6, s + s // 2, s) % 2

    c = way(seg)
    x, z = tm // 8, tm % 8
    zh, zi = z // 4, z % 4
    row = zh == c
    pos = jnp.where(row, zi, 3 - zi)
    nz = jnp.where(row, (z + 1) % 8, (z + 7) % 8)
    end = pos == 3
    inner = (x == 1) | (x == 2)
    root = end & inner
    outer = end & jnp.logical_not(inner)
    first, last = seg == 0, seg == 7
    xroot = jnp.where(x < 2, 1, 2)
    xouter = jnp.where(x < 2, 0, 3)

    def end_z(core, half):
        return jnp.where(core == 0, 3 + half, 7 * half)

    def did(s, xx, zz):
        return (s, xx * 8 + zz)

    myend = end_z(c, zh)

    def moved(s):
        return (s == 5) | (s == 7)

    def worker_z(s):
        return end_z(jnp.where(moved(s), 0, way(s)), zh)

    worker = inner & (z == worker_z(seg))
    guest = worker & moved(seg)
    host = root & moved(seg)

    def rcopy(src, dst, ssem, rsem, dev):
        return pltpu.make_async_remote_copy(
            src_ref=src, dst_ref=dst, send_sem=ssem, recv_sem=rsem, device_id=dev, device_id_type=MESH
        )

    def got(dst, rsem):
        rcopy(dst, dst, rsem, rsem, did(seg, x, nz)).wait_recv()

    barrier = pltpu.get_barrier_semaphore()

    def greet(dev):
        pl.semaphore_signal(barrier, inc=1, device_id=dev, device_id_type=MESH)

    pz = jnp.where(row, z - 1, z + 1)

    @pl.when(pos < 3)
    def _():
        greet(did(seg, x, myend))

    @pl.when((pos < 2) | end)
    def _():
        greet(did(seg, x, nz))

    @pl.when((pos == 1) | (pos == 2))
    def _():
        greet(did(seg, x, pz))

    @pl.when((pos == 0) & jnp.logical_not(row))
    def _():
        greet(did(seg, x, end_z(c, 1 - zh)))

    @pl.when(end)
    def _():
        for k in range(1, 4):
            greet(did(seg, x, zh * 4 + (zi + k) % 4))

        @pl.when(row)
        def _():
            greet(did(seg, x, (1 - zh) * 4 + 3))

    for here, others in ((0, (1,)), (1, (0, 2, 3)), (2, (1, 3)), (3, (2, 1))):
        @pl.when(end & (x == here))
        def _():
            for k in others:
                greet(did(seg, k, z))

    @pl.when(jnp.logical_not(inner))
    def _():
        greet(did(seg, xroot, myend))

        @pl.when(moved(seg))
        def _():
            greet(did(seg, xroot, worker_z(seg)))

    @pl.when(root | guest)
    def _():
        for k in range(4):
            greet(did(seg, xouter, zh * 4 + k))

    middle = inner & moved(seg) & ((pos == 1) | (pos == 2))

    @pl.when(middle)
    def _():
        greet(did(seg, x, worker_z(seg)))

    @pl.when(guest)
    def _():
        for k in (1, 2):
            greet(did(seg, x, jnp.where(row, z + k, z - k)))

    @pl.when(worker & jnp.logical_not(last))
    def _():
        greet(did(seg + 1, x, worker_z(seg + 1)))

        @pl.when(moved(seg + 1))
        def _():
            greet(did(seg + 1, x, end_z(way(seg + 1), zh)))

        @pl.when(x == 1)
        def _():
            greet(did(seg + 1, 0, end_z(way(seg + 1), zh)))

    @pl.when((worker | host) & jnp.logical_not(first))
    def _():
        greet(did(seg - 1, x, worker_z(seg - 1)))

    @pl.when(end & (x == 0) & jnp.logical_not(first))
    def _():
        greet(did(seg - 1, 1, worker_z(seg - 1)))

    one = lambda p: jnp.where(p, 1, 0)
    greets = (
        one(pos < 3) + one((pos < 2) | end) + one((pos == 1) | (pos == 2)) + one((pos == 0) & jnp.logical_not(row))
        + one(end) * (3 + one(row) + jnp.where(x == 0, 1, jnp.where(x == 1, 3, 2))) + one(jnp.logical_not(inner))
        + one(jnp.logical_not(inner) & moved(seg)) + 4 * one(root | guest) + one(middle) + 2 * one(guest)
        + one(worker & jnp.logical_not(last)) * (1 + one(moved(seg + 1)) + one(x == 1))
        + one((worker | host) & jnp.logical_not(first)) + one(end & (x == 0) & jnp.logical_not(first))
    )

    def put_map(m):
        @pl.when(pos == 0)
        def _():
            zout[...] = m

        @pl.when(pos > 0)
        def _():
            hi, lo = split(m)
            whi[...] = hi
            wlo[...] = lo

    @pl.when(row)
    def _():
        put_map(dot(t_ref[0], t_ref[1]))

    @pl.when(jnp.logical_not(row))
    def _():
        put_map(dot(t_ref[1], t_ref[0], TT))

        @pl.when(end)
        def _():
            pout[...] = dot(t_ref[0], t_ref[1])

    pad = jnp.zeros((PAD - 4, D), F32)
    for s in range(2):
        drv[s] = jnp.concatenate([dot(o_ref[s], g_ref[s]), pad], axis=0)

    @pl.when(zi == 0)
    def _():
        cin[...] = jnp.zeros_like(cin)

    pl.semaphore_wait(barrier, greets)

    block = jnp.where(x == xroot, 0, 4) + zi

    def f0_copy():
        return rcopy(f0_ref, f_in.at[block], f0_s, f0_r.at[block], did(seg, xroot, myend))

    @pl.when(first & jnp.logical_not(root))
    def _():
        f0_copy().start()

    @pl.when(first & root)
    def _():
        f_in[block] = f0_ref[...]

    def two_steps(m):
        m1 = mm2(m, t_ref[0]) + drv[0]
        return m1, mm2(m1, t_ref[1]) + drv[1]

    def c_next():
        return rcopy(csend, cin, cs_s, cs_r, did(seg, x, (z + 1) % 8))

    def c_end(half):
        return rcopy(csend, ch.at[zh], ch_s.at[half], ch_r.at[zh], did(seg, x, end_z(c, half)))

    def c_step():
        @pl.when(zi > 0)
        def _():
            got(cin, cs_r)

        csend[...] = two_steps(cin[...])[1]

        @pl.when(zi < 3)
        def _():
            c_next().start()

        @pl.when(zi == 3)
        def _():
            for half in range(2):
                away = end_z(c, half) != z

                @pl.when(away)
                def _():
                    c_end(half).start()

                @pl.when(jnp.logical_not(away))
                def _():
                    ch[zh] = csend[...]

    turn = jnp.where(row, 0, jnp.where(pos == 1, NC // 2, jnp.where(pos == 0, NC, 0)))
    slot = jnp.where(end, 1, 0)

    def piece(k):
        return pl.ds(pl.multiple_of(k * ROWS, ROWS), ROWS)

    def z_copy(k):
        return rcopy(
            zout.at[piece(k)], zin.at[slot, piece(k)], zs.at[k], zr.at[slot, k], did(seg, x, nz)
        )

    ia = jnp.where((zh == 0) == (x < 2), 0, 1)

    def z_body(k, _):
        pl.when(k == turn)(c_step)

        @pl.when(k < NC)
        def _():
            @pl.when(pos > 0)
            def _():
                got(zin.at[0, piece(k)], zr.at[0, k])
                v = mm3(zin[0, piece(k), :], whi[...], wlo[...])
                zout[piece(k), :] = v

                @pl.when(end)
                def _():
                    sphi[ia, piece(k), :], splo[ia, piece(k), :] = split(v)


            z_copy(k).start()

        return 0

    lax.fori_loop(0, NC + 1, z_body, 0)

    def z_sent():
        def z_done(k, _):
            z_copy(k).wait_send()
            return 0

        lax.fori_loop(0, NC, z_done, 0)

        @pl.when(zi < 3)
        def _():
            c_next().wait_send()

        @pl.when(zi == 3)
        def _():
            for half in range(2):
                @pl.when(end_z(c, half) != z)
                def _():
                    c_end(half).wait_send()

    def wide(k):
        return pl.ds(pl.multiple_of(k * WIDE, WIDE), WIDE)

    def p_copy(k):
        return rcopy(pout.at[wide(k)], zin.at[1, wide(k)], ps.at[k], zr.at[1, k], did(seg, x, z + 1))

    def p_body(k, _):
        got(zin.at[1, wide(k)], zr.at[1, k])

        @pl.when(zi < 3)
        def _():
            pout[wide(k), :] = mm3(zin[1, wide(k), :], whi[...], wlo[...], NT)
            p_copy(k).start()

        return 0

    def p_start(k, _):
        p_copy(k).start()
        return 0

    def p_done(k, _):
        p_copy(k).wait_send()
        return 0

    def prefix():
        @pl.when(jnp.logical_not(row | end))
        def _():
            lax.fori_loop(0, NP, p_body, 0)

        @pl.when(zi > 0)
        def _():
            hi, lo = split(zin[jnp.where(row, 0, 1)])
            inhi[...] = hi
            inlo[...] = lo

    pl.when(jnp.logical_not(guest))(prefix)

    iv = jnp.where(x < 2, 1, 0)
    w = jnp.where(x == 1, 0, 1)

    def half_rows(k, half):
        return pl.ds(pl.multiple_of(half * HALF + k * XROWS, XROWS), XROWS)

    def x_copy(k):
        return rcopy(px.at[half_rows(k, zh)], xin.at[half_rows(k, 0)], xs.at[k], xr.at[k], did(seg, xroot, z))

    def abx_copy(k):
        return rcopy(
            ab.at[w, half_rows(k, zh)], ab.at[w, half_rows(k, zh)], abx_s.at[k], abx_r.at[k], did(seg, 3 - x, z)
        )

    def abz_copy(k, which):
        return rcopy(
            ab.at[which, half_rows(k, zh)], ab.at[which, half_rows(k, zh)],
            abz_s.at[which, k], abz_r.at[which, k], did(seg, x, nz),
        )

    def abx_more(k):
        return rcopy(
            ab.at[w, half_rows(k, 1 - zh)], ab.at[w, half_rows(k, 1 - zh)], abm_s.at[k], abm_r.at[k], did(seg, 3 - x, z)
        )

    def map_copy(k):
        return rcopy(px.at[wide(k)], zin.at[0, wide(k)], map_s.at[k], map_r.at[k], did(seg, x, worker_z(seg)))

    def const_copy():
        return rcopy(cseg, cseg, const_s, const_r, did(seg, x, worker_z(seg)))

    def ab_split(which, rows):
        abhi[which, rows, :], ablo[which, rows, :] = split(ab[which, rows, :])

    def cx_copy(which, send, to):
        return rcopy(cown, cs.at[which], cx_s.at[send], cx_r.at[which], did(seg, to, z))

    @pl.when(end)
    def _():
        def x_wait(k, _):
            got(zin.at[1, piece(k)], zr.at[1, k])
            sphi[1 - ia, piece(k), :], splo[1 - ia, piece(k), :] = split(zin[1, piece(k), :])
            return 0

        lax.fori_loop(0, NC, x_wait, 0)
        for half in (zh, 1 - zh):
            part = pl.ds(pl.multiple_of(half * HALF, HALF), HALF)
            for core, dims in ((0, NT), (1, TN)):
                @pl.when(c == core)
                def _():
                    at = (part, slice(None)) if core == 0 else (slice(None), part)
                    p = dot(sphi[(0, *at)], sphi[1], dims)
                    p += dot(splo[(0, *at)], sphi[1], dims)
                    p += dot(sphi[(0, *at)], splo[1], dims)
                    px[part, :] = p

            if half is zh:
                @pl.when(outer)
                def _():
                    for k in range(NX):
                        x_copy(k).start()

        hi, lo = split(px[...])
        wxhi[...] = hi
        wxlo[...] = lo

        @pl.when(zh != c)
        def _():
            got(ch.at[zh], ch_r.at[zh])

        got(ch.at[1 - zh], ch_r.at[1 - zh])
        for core, dims in ((0, NT), (1, NN)):
            @pl.when(c == core)
            def _():
                cx[...] = mm3(ch[0], sphi[iv], splo[iv], dims) + ch[1]

        @pl.when(x == 0)
        def _():
            cown[...] = cx[...]
            cx_copy(0, 0, 1).start()

        @pl.when(x == 1)
        def _():
            got(cs.at[0], cx_r.at[0])
            cown[...] = mm3(cs[0], wxhi[...], wxlo[...]) + cx[...]
            cs[1] = cown[...]
            cx_copy(1, 0, 2).start()

        @pl.when(x == 2)
        def _():
            cown[...] = cx[...]
            cx_copy(2, 0, 3).start()

        @pl.when(x == 3)
        def _():
            got(cs.at[2], cx_r.at[2])
            cown[...] = mm3(cs[2], wxhi[...], wxlo[...], NT) + cx[...]
            cx_copy(3, 0, 2).start()
            cx_copy(3, 1, 1).start()

    @pl.when(end & jnp.logical_not(row))
    def _():
        lax.fori_loop(0, NP, p_start, 0)

    @pl.when(root)
    def _():
        def x_body(k, _):
            @pl.when(k < NX)
            def _():
                got(xin.at[half_rows(k, 0)], xr.at[k])
                v = mm3(xin[half_rows(k, 0), :], wxhi[...], wxlo[...])
                mine = half_rows(k, zh)
                ab[w, mine, :] = v
                abx_copy(k).start()
                abz_copy(k, w).start()
                abhi[w, mine, :], ablo[w, mine, :] = split(v)

            @pl.when(k >= LAG)
            def _():
                j = k - LAG
                got(ab.at[1 - w, half_rows(j, zh)], abx_r.at[j])

                @pl.when(j % 2 == 0)
                def _():
                    abz_copy(j, 1 - w).start()

                ab_split(1 - w, half_rows(j, zh))
                got(ab.at[w, half_rows(j, 1 - zh)], abz_r.at[w, j])

                @pl.when(j % 2 == 1)
                def _():
                    abx_more(j).start()

                ab_split(w, half_rows(j, 1 - zh))

            return 0

        lax.fori_loop(0, NX + LAG, x_body, 0)

        def ab_wait(k, _):
            @pl.when(k % 2 == 0)
            def _():
                got(ab.at[1 - w, half_rows(k, 1 - zh)], abz_r.at[1 - w, k])

            @pl.when(k % 2 == 1)
            def _():
                got(ab.at[1 - w, half_rows(k, 1 - zh)], abm_r.at[k])

            ab_split(1 - w, half_rows(k, 1 - zh))
            return 0

        lax.fori_loop(0, NX, ab_wait, 0)
        p = dot(abhi[0], abhi[1], NT)
        p += dot(ablo[0], abhi[1], NT)
        p += dot(abhi[0], ablo[1], NT)

        @pl.when(host)
        def _():
            px[...] = p
            for k in range(NP):
                map_copy(k).start()

        hi, lo = split(p)
        pfhi[...] = hi
        pflo[...] = lo

        @pl.when(x == 2)
        def _():
            got(cs.at[1], cx_r.at[1])

        got(cs.at[3], cx_r.at[3])
        cseg[...] = mm3(cs[1], abhi[1], ablo[1], NT) + cs[3]

        @pl.when(host)
        def _():
            const_copy().start()

    @pl.when(guest)
    def _():
        def map_got(k, _):
            got(zin.at[0, wide(k)], map_r.at[k])
            pfhi[wide(k), :], pflo[wide(k), :] = split(zin[0, wide(k), :])
            return 0

        lax.fori_loop(0, NP, map_got, 0)
        got(cseg, const_r)

    def x_sent():
        @pl.when(outer)
        def _():
            for k in range(NX):
                x_copy(k).wait_send()

            @pl.when(x == 0)
            def _():
                cx_copy(0, 0, 1).wait_send()

            @pl.when(x == 3)
            def _():
                cx_copy(3, 0, 2).wait_send()
                cx_copy(3, 1, 1).wait_send()

        @pl.when(root)
        def _():
            def ab_done(k, _):
                abx_copy(k).wait_send()
                abz_copy(k, w).wait_send()

                @pl.when(k % 2 == 0)
                def _():
                    abz_copy(k, 1 - w).wait_send()

                @pl.when(k % 2 == 1)
                def _():
                    abx_more(k).wait_send()

                return 0

            lax.fori_loop(0, NX, ab_done, 0)
            cx_copy(1, 0, 3).wait_send()

    m0 = jnp.concatenate([m0_ref[...], pad], axis=0)
    chained = root | guest | (end & (x == 0))

    @pl.when(chained & first)
    def _():
        m_in[...] = m0

    @pl.when(chained & jnp.logical_not(first))
    def _():
        got(m_in, m_r)

    def m_copy(send):
        to = jnp.where(send == 1, 0, x)
        at = jnp.where(send == 0, worker_z(seg + 1), end_z(way(seg + 1), zh))
        return rcopy(m_out, m_in, m_s.at[send], m_r, did(seg + 1, to, at))

    def f_copy(blk):
        return rcopy(f_out.at[blk], f_in.at[blk], f_s.at[blk], f_r.at[blk], did(seg + 1, x, worker_z(seg + 1)))

    def owner(blk):
        return jnp.where(blk < 4, x, xouter), zh * 4 + blk % 4

    def fb_copy(blk):
        ox, oz = owner(blk)
        return rcopy(f_out.at[blk], ends_ref.at[0], fb_s.at[blk], fb_r, did(seg, ox, oz))

    def ex_copy(to):
        return rcopy(e_out, e_x, ex_s, ex_r, did(seg, to, z))

    @pl.when(worker & jnp.logical_not(last))
    def _():
        m_out[...] = mm3(m_in[...], pfhi[...], pflo[...]) + cseg[...]
        m_copy(0).start()

        @pl.when(x == 1)
        def _():
            m_copy(1).start()

        @pl.when(moved(seg + 1))
        def _():
            m_copy(2).start()


    def e_copy(k):
        return rcopy(e_half, e_in, e_s.at[k], e_r, did(seg, x, zh * 4 + (zi + k + 1) % 4))

    def go_down():
        pl.when(guest)(prefix)

        @pl.when(root & (x == 2))
        def _():
            e_x[...] = mm3(m_in[...], abhi[0], ablo[0]) + cs[1]
            e_out[...] = mm3(e_x[...], wxhi[...], wxlo[...], NT) + cx[...]
            ex_copy(3).start()

        @pl.when(end & (x == 0))
        def _():
            e_out[...] = mm3(m_in[...], wxhi[...], wxlo[...]) + cx[...]
            ex_copy(1).start()
            e_x[...] = m_in[...]

        @pl.when(end & ((x == 1) | (x == 3)))
        def _():
            got(e_x, ex_r)

        @pl.when(end & (zh == 0))
        def _():
            e_half[...] = e_x[...]

        for core, dims in ((0, NN), (1, NT)):
            @pl.when(end & (zh == 1) & (c == core))
            def _():
                e_half[...] = mm3(e_x[...], sphi[1 - iv], splo[1 - iv], dims) + ch[0]

        @pl.when(end)
        def _():
            for k in range(3):
                e_copy(k).start()

        @pl.when(jnp.logical_not(end))
        def _():
            got(e_in, e_r)
            e_half[...] = e_in[...]

        @pl.when(zi > 0)
        def _():
            e_in[...] = mm3(e_half[...], inhi[...], inlo[...]) + cin[...]

        @pl.when(zi == 0)
        def _():
            e_in[...] = e_half[...]

        m1, m2 = two_steps(e_in[...])
        means_ref[0] = m1[:4]
        means_ref[1] = m2[:4]

    def f_home(blk):
        @pl.when(blk != block)
        def _():
            fb_copy(blk).start()

        @pl.when(blk == block)
        def _():
            ends_ref[0] = f_out[blk]

    def f_block(k):
        blk = jnp.where(k < 4, 4, 0) + jnp.where(zh == 0, k % 4, 3 - k % 4)

        @pl.when(first & (blk != block))
        def _():
            got(f_in.at[blk], f0_r.at[blk])

        @pl.when(jnp.logical_not(first))
        def _():
            got(f_in.at[blk], f_r.at[blk])

        f_out[blk] = mm3(f_in[blk], pfhi[...], pflo[...])

        @pl.when(jnp.logical_not(last))
        def _():
            f_copy(blk).start()

        @pl.when(last)
        def _():
            f_home(blk)

    down_turn = jnp.where(worker, 8, 0)

    def all_home():
        for blk in range(8):
            f_home(blk)

    def chain_body(k, _):
        pl.when((k == 8) & worker & jnp.logical_not(last))(all_home)
        pl.when(k == down_turn)(go_down)

        @pl.when(worker & (k < 8))
        def _():
            f_block(k)

        return 0

    lax.fori_loop(0, jnp.where(worker, 9, 1), chain_body, 0)


    @pl.when(jnp.logical_not(worker))
    def _():
        got(ends_ref.at[0], fb_r)

    def rest_sent():
        @pl.when(first & jnp.logical_not(root))
        def _():
            f0_copy().wait_send()

        @pl.when(worker)
        def _():
            @pl.when(jnp.logical_not(last))
            def _():
                m_copy(0).wait_send()

                @pl.when(x == 1)
                def _():
                    m_copy(1).wait_send()

                @pl.when(moved(seg + 1))
                def _():
                    m_copy(2).wait_send()

                for blk in range(8):
                    f_copy(blk).wait_send()

            for blk in range(8):
                @pl.when(blk != block)
                def _():
                    fb_copy(blk).wait_send()

        @pl.when(end & ((x == 0) | (x == 2)))
        def _():
            ex_copy(1).wait_send()

        @pl.when(end)
        def _():
            for k in range(3):
                e_copy(k).wait_send()

        @pl.when(jnp.logical_not(row) & (zi < 3))
        def _():
            lax.fori_loop(0, NP, p_done, 0)

        @pl.when(host)
        def _():
            const_copy().wait_send()
            for k in range(NP):
                map_copy(k).wait_send()

    z_sent()
    x_sent()
    rest_sent()


def per_device(transition, obs_gain, observed, init_mean, init_factor):
    vm = pl.BlockSpec(memory_space=pltpu.VMEM)
    f, b = (lambda *s: pltpu.VMEM(s, F32)), (lambda *s: pltpu.VMEM(s, BF16))
    dma = lambda *s: pltpu.SemaphoreType.DMA(s) if s else pltpu.SemaphoreType.DMA
    scratch = [
        f(D, D), f(2, D, D), b(D, D), b(D, D), f(2, PAD, D), f(PAD, D), f(2, PAD, D), f(PAD, D),
        b(2, D, D), b(2, D, D), f(D, D), b(D, D), b(D, D), f(HALF, D), f(2, D, D), b(2, D, D), b(2, D, D), b(D, D), b(D, D),
        f(4, PAD, D), f(PAD, D), f(PAD, D), f(PAD, D), f(PAD, D), f(PAD, D), f(8, 16, D), f(8, 16, D), b(D, D), b(D, D),
        f(PAD, D), f(PAD, D), f(PAD, D), f(PAD, D), f(D, D),
        dma(NP), dma(NP), dma(), dma(), dma(NP), dma(NC), dma(2, NC), dma(), dma(), dma(2), dma(2), dma(NX), dma(NX), dma(NX), dma(NX), dma(NX), dma(NX), dma(2, NX), dma(2, NX),
        dma(2), dma(4), dma(3), dma(), dma(), dma(8), dma(8), dma(8), dma(8), dma(), dma(3), dma(), dma(), dma(),
    ]
    outs = pl.pallas_call(
        kernel,
        out_shape=(jax.ShapeDtypeStruct((2, 4, D), F32), jax.ShapeDtypeStruct((1, 16, D), F32)),
        in_specs=[vm] * 5,
        out_specs=(vm, vm),
        scratch_shapes=scratch,
        compiler_params=pltpu.CompilerParams(
            collective_id=0, has_side_effects=True, vmem_limit_bytes=56 * 2**20
        ),
        name="filter_flow",
    )(transition, obs_gain, observed, init_mean, init_factor)

    def hand_on(a_ref, b_ref, a_out, b_out):
        a_out[...] = a_ref[...]
        b_out[...] = b_ref[...]

    return pl.pallas_call(
        hand_on, out_shape=tuple(jax.ShapeDtypeStruct(o.shape, o.dtype) for o in outs), in_specs=[vm] * 2, out_specs=(vm, vm),
        name="hand_on",
    )(*outs)


def solution(mesh):
    placed = P(("seg", "tm"), None, None)
    return jax.shard_map(
        per_device,
        mesh=mesh,
        in_specs=(placed, placed, placed, P(), P("tm", None)),
        out_specs=(placed, P("seg", "tm", None)),
        check_vma=False,
    )
```
